32 devices in a mesh: rep: 4 (over x, core), fsdp: 8 (over z, y).
Axes of the slice: x: 2, y: 2, z: 4, core: 2. Of those that a mesh axis runs over, the one named last changes fastest.
Arguments:
- tokens: bfloat16 [45312, 768], P(('rep', 'fsdp')), may hold values from -6 to 6
- lengths: int32 [124], replicated, may hold values from 196 to 1024, as said below
- assign: int32 [124], replicated, may hold values from 0 to 31, as said below
- w_in: bfloat16 [768, 5376], P('fsdp'), may hold values from -0.21875 to 0.21875
- w_out: bfloat16 [3840, 768], P('fsdp')
- ln_scale: bfloat16 [768], P('fsdp'), may hold values from 0.5 to 1.5
- q_scale: bfloat16 [64], P('fsdp'), may hold values from 1 to 2
- k_scale: bfloat16 [64], P('fsdp'), may hold values from 1 to 2
- mlp_bias: bfloat16 [3072], P('fsdp'), may hold values from -3 to 3
- out_bias: bfloat16 [768], P('fsdp'), may hold values from -3 to 3
- cotangent: bfloat16 [45312, 768], P(('rep', 'fsdp')), may hold values from -6 to 6
Outputs:
- output: bfloat16 [45312, 768], P(('rep', 'fsdp'))
- grad_tokens: bfloat16 [45312, 768], P(('rep', 'fsdp'))
- grad_w_in: float32 [768, 5376], P('fsdp')
- grad_w_out: float32 [3840, 768], P('fsdp')
- grad_ln_scale: float32 [768], P('fsdp')
- grad_q_scale: float32 [64], P('fsdp')
- grad_k_scale: float32 [64], P('fsdp')
- grad_mlp_bias: float32 [3072], P('fsdp')
- grad_out_bias: float32 [768], P('fsdp')
The draws below stay inside these ranges and needn't reach their ends.
Inputs may be any that keep to these rules, and one draw needn't show every extreme that they name: `lengths`: each image has 196 or 1024 tokens. `assign`: in each aligned group of eight devices one holds one image of 1024 tokens and two of 196 (1416 tokens), and the seven others hold 1, 2, 3, 4, 5, 6 and 7 images of 196 tokens; no device holds more than 1416 tokens.
All inputs are finite; a program needn't handle non-finite values.
Results may differ from the reference program's by a relative error of at most 0.012.
The reference program's roundings to bfloat16 on the way count: a program that leaves them out, or rounds other values in their place, can miss the bound.
Values may be sent and summed in bfloat16 or wider, within the bound.
No kernel may reach another device: no remote copies, remote signals or barrier semaphores. Data moves between devices by JAX's collectives and lax.ppermute only.
A program may use at most 320 MiB of HBM per device.

```python
import math
import jax
import jax.numpy as jnp
import numpy as np
from jax import lax

D = 768
HEADS = 12
HD = 64
FF = 3072
SMALL_LEN = 196
BIG_LEN = 1024
CAP = 1416
IMAGES = 124
TOKENS = 45312
N_REP = 4
N_FSDP = 8


def image_table(key):
    groups = IMAGES // 31
    roles = np.array([0, 0, 0] + [r for r in range(1, 8) for _ in range(r)], np.int32)
    large = np.array([1] + [0] * 30, np.int32)
    keys_all = jax.random.split(key, groups + 1)
    places = jax.vmap(lambda sub: jax.random.permutation(sub, 8))(keys_all[:groups]).astype(jnp.int32)
    device = jnp.arange(groups, dtype=jnp.int32)[:, None] * 8 + places[:, roles]
    length = jnp.broadcast_to(jnp.where(jnp.asarray(large) == 1, BIG_LEN, SMALL_LEN).astype(jnp.int32), (groups, 31))
    order = jax.random.permutation(keys_all[groups], IMAGES)
    return (device.reshape(-1)[order].astype(jnp.int32), length.reshape(-1)[order].astype(jnp.int32))


def draw_lengths(key, part):
    device, length = image_table(key)
    return length


def draw_assign(key, part):
    device, length = image_table(key)
    return device


def draw_w_out(key, part):
    key = jax.random.fold_in(key, 7)
    noise = jax.random.normal(key, (D + FF, D), jnp.float32)
    row_index = jnp.arange(D + FF)[:, None]
    scaled = jnp.where(row_index < D, noise * (4.0 / math.sqrt(D)), noise * (1.0 / math.sqrt(FF)))
    return scaled.astype(jnp.bfloat16)


def block_levels(own_key, shape, cuts, least, largest):
    def one(dim, shards_of):
        steps = jax.random.uniform(jax.random.fold_in(jax.random.fold_in(own_key, 6), dim), (shards_of,), jnp.float32, least / len(cuts), largest / len(cuts))
        return jnp.repeat(jnp.exp(steps), shape[dim] // shards_of).reshape((-1,) + (1,) * (len(shape) - dim - 1))

    level = one(*cuts[0])
    for cut in cuts[1:]:
        level = level * one(*cut)
    return level


def centred(key, dims, scale, limit, shards=(), held_as=jnp.bfloat16):
    drawn = jax.random.normal(key, dims, jnp.float32) * scale
    if len(shards) > 0:
        drawn = block_levels(key, dims, shards, -0.22, 0.18) * drawn
    return jnp.clip(drawn, min=-limit, max=limit).astype(held_as)


def setup_inputs(seed: int = 0) -> dict:
    keys = jax.random.split(jax.random.key(seed), 12)
    return {
        "tokens": centred(keys[0], (TOKENS, D), 1.0, 6.0, ((0, 32),)),
        "lengths": draw_lengths(jax.random.fold_in(keys[11], 71), 0),
        "assign": draw_assign(jax.random.fold_in(keys[11], 71), 0),
        "w_in": centred(keys[3], (D, 3 * D + FF), D ** -0.5, 0.21875, ((0, 8),)),
        "w_out": draw_w_out(jax.random.fold_in(keys[11], 71), 0),
        "ln_scale": jnp.clip(0.5 + 1.0 * jax.random.uniform(keys[5], (D,), jnp.float32) ** block_levels(keys[5], (D,), ((0, 8),), -0.2, 0.2), 0.5, 1.5).astype(jnp.bfloat16),
        "q_scale": jnp.clip(1.0 + 1.0 * jax.random.uniform(keys[6], (HD,), jnp.float32) ** block_levels(keys[6], (HD,), ((0, 8),), -0.2, 0.2), 1.0, 2.0).astype(jnp.bfloat16),
        "k_scale": jnp.clip(1.0 + 1.0 * jax.random.uniform(keys[7], (HD,), jnp.float32) ** block_levels(keys[7], (HD,), ((0, 8),), -0.2, 0.2), 1.0, 2.0).astype(jnp.bfloat16),
        "mlp_bias": centred(keys[8], (FF,), 0.5, 3.0, ((0, 8),)),
        "out_bias": centred(keys[9], (D,), 0.5, 3.0, ((0, 8),)),
        "cotangent": centred(keys[10], (TOKENS, D), 1.0, 6.0, ((0, 32),)),
    }


@jax.custom_vjp
def low(v):
    return lax.optimization_barrier(v.astype(jnp.bfloat16)).astype(jnp.float32)

@jax.custom_vjp
def low_back(v):
    return v

def low_keep(v):
    return (low(v), None)

def low_pass(kept, grad):
    return (grad,)

def back_keep(v):
    return (v, None)

def back_low(kept, grad):
    return (low(grad),)
low.defvjp(low_keep, low_pass)
low_back.defvjp(back_keep, back_low)
epsilon = 1e-06

def layer_norm(values, weight_gain):
    center = values - lax.optimization_barrier(jnp.mean(values, axis=-1, keepdims=True))
    spread = lax.optimization_barrier(jnp.mean(center * center, axis=-1, keepdims=True))
    return center * lax.rsqrt(spread + epsilon) * weight_gain

def product(left, right):
    return jnp.dot(left, right, precision=lax.Precision.HIGHEST, preferred_element_type=jnp.float32)

def layout(lengths, assign, device):
    own = assign == device
    own_sizes = jnp.where(own, lengths, 0).astype(jnp.int32)
    own_ends = jnp.cumsum(own_sizes).astype(jnp.int32)
    own_starts = own_ends - own_sizes
    position = jnp.arange(CAP, dtype=jnp.int32)[:, None]
    number = jnp.arange(IMAGES, dtype=jnp.int32)[None, :]
    inside = (position >= own_starts[None, :]) & (position < own_ends[None, :])
    filled = jnp.any(inside, axis=1)
    segment = lax.optimization_barrier(jnp.sum(jnp.where(inside, number, 0), axis=1)).astype(jnp.int32)
    return (jnp.where(filled, segment, -1).astype(jnp.int32), filled)

def layer_block(inputs, segment, filled, w_in, w_out, ln_scale, q_scale, k_scale, mlp_bias, out_bias):
    row_count = inputs.shape[0]
    normed = low(layer_norm(inputs, ln_scale))
    joined = low_back(product(normed, w_in))
    queries = joined[:, :D].reshape(row_count, HEADS, HD)
    keys_pre = joined[:, D:2 * D].reshape(row_count, HEADS, HD)
    values = low(joined[:, 2 * D:3 * D].reshape(row_count, HEADS, HD))
    hidden_pre = joined[:, 3 * D:]
    queries = low(layer_norm(queries, q_scale))
    keys_all = low(layer_norm(keys_pre, k_scale))
    scores = jnp.einsum('qhd,khd->hqk', queries, keys_all, precision=lax.Precision.HIGHEST) * HD ** (-0.5)
    scores = low_back(scores)
    allowed = segment[:, None] == segment[None, :]
    scores = jnp.where(allowed[None], scores, -1e+30)
    probs = low(jax.nn.softmax(scores, axis=-1))
    attended = jnp.einsum('hqk,khd->qhd', probs, values, precision=lax.Precision.HIGHEST)
    attended = low_back(attended.reshape(row_count, D))
    activated = jax.nn.gelu(hidden_pre + mlp_bias)
    merged = low(jnp.concatenate([attended, activated], axis=1))
    result = product(merged, w_out) + out_bias
    return jnp.where(filled[:, None], inputs + result, 0.0)

def reference(tokens, lengths, assign, w_in, w_out, ln_scale, q_scale, k_scale, mlp_bias, out_bias, cotangent):
    devices = N_REP * N_FSDP
    segments, fills = jax.vmap(lambda dev: layout(lengths, assign, dev))(jnp.arange(devices, dtype=jnp.int32))
    params = tuple((arr.astype(jnp.float32) for arr in (tokens, w_in, w_out, ln_scale, q_scale, k_scale, mlp_bias, out_bias)))

    def forward(inputs, w_in_f, w_out_f, ln_f, qs_f, ks_f, mb_f, ob_f):
        pieces = inputs.reshape(devices, CAP, D)

        def one_device(items):
            return layer_block(items[0], items[1], items[2], w_in_f, w_out_f, ln_f, qs_f, ks_f, mb_f, ob_f)
        outputs = lax.map(jax.checkpoint(one_device), (pieces, segments, fills))
        return outputs.reshape(TOKENS, D)
    output, pull = jax.vjp(forward, *params)
    grads = pull(cotangent.astype(jnp.float32))
    return (output.astype(jnp.bfloat16), grads[0].astype(jnp.bfloat16), grads[1], grads[2], grads[3], grads[4], grads[5], grads[6], grads[7])
```

```python
import functools

import jax
import jax.numpy as jnp
from jax import lax
from jax.experimental import pallas as pl
from jax.experimental.pallas import tpu as pltpu
from jax.sharding import PartitionSpec as P

D = 768
HD = 64
SMALL = 196
BIG = 1024
BLK = 208
CAN = 7 * BLK
ROWS = 3072
RB = 512
NRB = ROWS // RB
U = 512
EPS = 1e-06
BF = jnp.bfloat16
F32 = jnp.float32
VLIM = 60 * 1024 * 1024
ANYWHERE = pl.BlockSpec(memory_space=pltpu.VMEM)
SCALARS = pl.BlockSpec(memory_space=pltpu.SMEM)


def dot_nn(a, b):
    return lax.dot_general(a, b, (((1,), (0,)), ((), ())), preferred_element_type=F32)


def dot_nt(a, b):
    return lax.dot_general(a, b, (((1,), (1,)), ((), ())), preferred_element_type=F32)


def dot_tn(a, b):
    return lax.dot_general(a, b, (((0,), (0,)), ((), ())), preferred_element_type=F32)


def two_parts(x):
    hi = x.astype(BF)
    return hi, (x - hi.astype(F32)).astype(BF)


def call(body, out_shape, scratch, args, in_specs, out_specs=None, grid=None, prefetch=0, cost=None):
    params = pltpu.CompilerParams(vmem_limit_bytes=VLIM)
    if out_specs is None:
        out_specs = jax.tree.map(lambda _: ANYWHERE, out_shape)
    spec = pltpu.PrefetchScalarGridSpec(
        num_scalar_prefetch=prefetch,
        grid=grid or (),
        in_specs=in_specs,
        out_specs=out_specs,
        scratch_shapes=scratch,
    )
    estimate = None if cost is None else pl.CostEstimate(flops=cost[0], bytes_accessed=cost[1], transcendentals=0)
    return pl.pallas_call(body, grid_spec=spec, out_shape=out_shape, compiler_params=params, cost_estimate=estimate)(*args)


def head_mean_matrix(scale):
    row = lax.broadcasted_iota(jnp.int32, (256, 128), 0)
    col = lax.broadcasted_iota(jnp.int32, (256, 128), 1)
    same = (row // HD) % 2 == col // HD
    return jnp.where(same, scale, 0.0).astype(BF)


def per_head(x, matrix):
    hi, lo = two_parts(x)
    return dot_nn(jnp.concatenate([hi, lo], axis=1), matrix)


def attention_body(info, nrm, cot, wqkv, wo, gq, gk, att_o, dqkv_o, dw_o, dwo_o, dgq_o, dgk_o,
                   qa, kb, vv, qp, do, xq, xk, rq, rk, dq, dk, dv, dw, dwo, dg):
    nb = info[0]
    lane = lax.broadcasted_iota(jnp.int32, (1, 128), 1)
    first = lane < HD
    mean_m = head_mean_matrix(1.0 / HD)
    sum_m = head_mean_matrix(1.0)
    c_exp = 1.4426950408889634 / 8.0

    def norm(x, gain, xh_ref, r_ref, rows):
        center = x - per_head(x, mean_m)
        spread = per_head(center * center, mean_m)
        r = lax.rsqrt(spread + EPS)
        xh = center * r
        xh_ref[rows, :] = xh
        r_ref[rows, :] = r
        return (xh * gain).astype(BF)

    def project(i, carry):
        rows = pl.ds(pl.multiple_of(i * RB, RB), RB)
        y = dot_nn(nrm[rows, :], wqkv[...])
        q = norm(y[:, :128], gq[...], xq, rq, rows)
        k = norm(y[:, 128:256], gk[...], xk, rk, rows)
        v = y[:, 256:]
        qp[rows, :] = q
        hi, lo = two_parts(q.astype(F32) * c_exp)
        hi, lo = hi.astype(F32), lo.astype(F32)
        qa[0, rows, :] = jnp.where(first, hi, pltpu.roll(lo, HD, 1)).astype(BF)
        qa[1, rows, :] = jnp.where(first, pltpu.roll(hi, HD, 1), lo).astype(BF)
        kf = k.astype(F32)
        kr = pltpu.roll(kf, HD, 1)
        kb[0, rows, :] = jnp.where(first, kf, kr).astype(BF)
        kb[1, rows, :] = jnp.where(first, kr, kf).astype(BF)
        vv[0, rows, :] = jnp.where(first, v, 1.0).astype(BF)
        vv[1, rows, :] = jnp.where(first, 1.0, v).astype(BF)
        do[rows, :] = dot_nt(cot[rows, :], wo[...]).astype(BF)
        zero = jnp.zeros((RB, 128), F32)
        dq[rows, :] = zero
        dk[rows, :] = zero
        dv[rows, :] = zero
        att_o[rows, :] = zero.astype(BF)
        return carry

    lax.fori_loop(0, nb, project, 0)

    def block(q_rows, k_rows, n_q, n_k, masked, add):
        ps, pbs, xs = [], [], []
        for h in range(2):
            p = jnp.exp2(dot_nt(qa[h, q_rows, :], kb[h, k_rows, :]))
            if masked:
                keep = lax.broadcasted_iota(jnp.int32, (n_q, n_k), 1) < SMALL
                p = jnp.where(keep, p, 0.0)
            pb = p.astype(BF)
            ps.append(p)
            pbs.append(pb)
            xs.append(dot_nn(pb, vv[h, k_rows, :]))
        total = jnp.where(first, pltpu.roll(xs[0], HD, 1), pltpu.roll(xs[1], HD, 1))
        inverse = 1.0 / total
        out = jnp.where(first, xs[0], xs[1]) * inverse
        att_o[q_rows, :] = out.astype(BF)
        grad = do[q_rows, :].astype(F32)
        inner = per_head(grad * out, sum_m) * inverse
        scaled = (grad * inverse).astype(BF)
        scaled_f = scaled.astype(F32)
        i_hi, i_lo = two_parts(inner)
        i_hi, i_lo = i_hi.astype(F32), i_lo.astype(F32)
        dqs, dks, dvs = [], [], []
        for h in range(2):
            own = first if h == 0 else jnp.logical_not(first)
            base = HD * (1 - h)
            other = pltpu.roll(i_hi, HD, 1), pltpu.roll(i_lo, HD, 1)
            side = jnp.where(lane == base, -other[0], jnp.where(lane == base + 1, -other[1], 0.0))
            left = jnp.where(own, scaled_f, side).astype(BF)
            ds = (ps[h] * dot_nt(left, vv[h, k_rows, :])).astype(BF)
            dqs.append(dot_nn(ds, kb[h, k_rows, :]))
            dks.append(dot_tn(ds, qp[q_rows, :]))
            dvs.append(dot_tn(pbs[h], scaled))
        dq[q_rows, :] = jnp.where(first, dqs[0], dqs[1])
        new_k = jnp.where(first, dks[0], dks[1])
        new_v = jnp.where(first, dvs[0], dvs[1])
        if add:
            dk[k_rows, :] += new_k
            dv[k_rows, :] += new_v
        else:
            dk[k_rows, :] = new_k
            dv[k_rows, :] = new_v

    for s in range(2):
        base, big, count = info[1 + 3 * s], info[2 + 3 * s], info[3 + 3 * s]

        @pl.when(big == 1)
        def _():
            k_rows = pl.ds(pl.multiple_of(base, 16), BIG)

            def one(i, carry):
                block(pl.ds(pl.multiple_of(base + i * 256, 16), 256), k_rows, 256, BIG, False, True)
                return carry

            lax.fori_loop(0, BIG // 256, one, 0)

        def small(i, carry):
            rows = pl.ds(pl.multiple_of(base + big * BIG + i * BLK, 16), BLK)
            block(rows, rows, BLK, BLK, True, False)
            return carry

        lax.fori_loop(0, count, small, 0)

    dw[...] = jnp.zeros_like(dw)
    dwo[...] = jnp.zeros_like(dwo)
    dg[...] = jnp.zeros_like(dg)

    def pull(g_out, gain, xh, r, slot):
        dg[slot : slot + 1, :] += jnp.sum(g_out * xh, axis=0, keepdims=True)
        g = g_out * gain
        return r * (g - per_head(g, mean_m) - xh * per_head(g * xh, mean_m))

    def finish(i, carry):
        rows = pl.ds(pl.multiple_of(i * RB, RB), RB)
        gq_pre = pull(dq[rows, :] * 0.125, gq[...], xq[rows, :], rq[rows, :], 0)
        gk_pre = pull(dk[rows, :] * 0.125, gk[...], xk[rows, :], rk[rows, :], 1)
        g = jnp.concatenate([gq_pre, gk_pre, dv[rows, :]], axis=1).astype(BF)
        dqkv_o[rows, :] = g
        dw[...] += dot_tn(g, nrm[rows, :])
        dwo[...] += dot_tn(att_o[rows, :], cot[rows, :])
        return carry

    lax.fori_loop(0, nb, finish, 0)
    dw_o[...] = dw[...].astype(BF)
    dwo_o[...] = dwo[...].astype(BF)
    dgq_o[...] = dg[0:1, :]
    dgk_o[...] = dg[1:2, :]


def attention(info, nrm, cot, wqkv, wo, gq, gk):
    sds = jax.ShapeDtypeStruct
    outs = (sds((ROWS, 128), BF), sds((ROWS, 384), BF), sds((384, D), BF), sds((128, D), BF),
            sds((1, 128), F32), sds((1, 128), F32))
    v = pltpu.VMEM
    scratch = [v((2, ROWS, 128), BF)] * 3 + [v((ROWS, 128), BF)] * 2 + [v((ROWS, 128), F32)] * 7 + [
        v((384, D), F32), v((128, D), F32), v((8, 128), F32)]
    return call(attention_body, outs, scratch, (info, nrm, cot, wqkv, wo, gq, gk),
                [SCALARS] + [ANYWHERE] * 6, cost=(12 * 10**9, 14 * 10**6))


def mlp_body(info, nrm, cot, win, wout, bias, act_o, gm_o, dwin_o, dwout_o, db_o, dwin, dwout, db):
    i = pl.program_id(0)

    @pl.when(i == 0)
    def _():
        dwin[...] = jnp.zeros_like(dwin)
        dwout[...] = jnp.zeros_like(dwout)
        db[...] = jnp.zeros_like(db)

    @pl.when(i < info[0])
    def _():
        x = nrm[...]
        g = cot[...]
        pre = dot_nn(x, win[...]) + bias[...]
        ga = dot_nt(g, wout[...])
        c0 = 0.7978845608028654
        c1 = 0.044715 * c0
        sq = pre * pre
        t = jnp.tanh(pre * (c0 + c1 * sq))
        half = 0.5 * pre
        up = 1.0 + t
        act = (half * up).astype(BF)
        slope = 0.5 * up + half * (1.0 - t * t) * (c0 + 3.0 * c1 * sq)
        gmf = ga * slope
        gm = gmf.astype(BF)
        act_o[...] = act
        gm_o[...] = gm
        db[...] += jnp.sum(gmf, axis=0, keepdims=True)
        dwout[...] += dot_tn(act, g)
        dwin[...] += dot_tn(gm, x)

    @pl.when(i == pl.num_programs(0) - 1)
    def _():
        dwin_o[...] = dwin[...].astype(BF)
        dwout_o[...] = dwout[...].astype(BF)
        db_o[...] = db[...]


def clamp(i, info):
    return (jnp.minimum(i, info[0] - 1), 0)


def whole(i, info):
    return (0, 0)


def mlp(info, nrm, cot, win, wout, bias):
    sds = jax.ShapeDtypeStruct
    outs = (sds((ROWS, U), BF), sds((ROWS, U), BF), sds((U, D), BF), sds((U, D), BF), sds((1, U), F32))
    bs = pl.BlockSpec
    in_specs = [bs((RB, D), clamp), bs((RB, D), clamp), bs((D, U), whole), bs((U, D), whole), bs((1, U), whole)]
    out_specs = (bs((RB, U), clamp), bs((RB, U), clamp), bs((U, D), whole), bs((U, D), whole), bs((1, U), whole))
    v = pltpu.VMEM
    scratch = [v((U, D), F32), v((U, D), F32), v((1, U), F32)]
    return call(mlp_body, outs, scratch, (info, nrm, cot, win, wout, bias), in_specs, out_specs,
                grid=(NRB,), prefetch=1, cost=(10 * 10**9, 18 * 10**6))


def sums_body(info, *refs, n, transposed):
    i = pl.program_id(0)
    lefts, rights, out = refs[:n], refs[n : 2 * n], refs[2 * n]

    @pl.when(i < info[0])
    def _():
        total = None
        for a, b, t in zip(lefts, rights, transposed):
            part = dot_nt(a[...], b[...]) if t else dot_nn(a[...], b[...])
            total = part if total is None else total + part
        out[...] = total.astype(BF)

    @pl.when(i >= info[0])
    def _():
        out[...] = jnp.zeros_like(out)


def sums(info, lefts, rights, transposed):
    n = len(lefts)
    bs = pl.BlockSpec
    in_specs = [bs((RB, a.shape[1]), clamp) for a in lefts] + [bs(b.shape, whole) for b in rights]
    k = sum(a.shape[1] for a in lefts)
    return call(functools.partial(sums_body, n=n, transposed=transposed), jax.ShapeDtypeStruct((ROWS, D), BF), [],
                (info, *lefts, *rights), in_specs, bs((RB, D), lambda i, info: (i, 0)), grid=(NRB,), prefetch=1,
                cost=(2 * 2304 * k * D, 2 * 2304 * (k + D)))


def prepare_body(src, tokens, cot, gain, x_o, nrm_o, cot_o, gob_o):
    i = pl.program_id(0)
    pick = (src[...] == lax.broadcasted_iota(jnp.int32, (BLK, tokens.shape[0]), 1)).astype(BF)
    x = dot_nn(pick, tokens[...])
    g = dot_nn(pick, cot[...])
    x_o[...] = x.astype(BF)
    cot_o[...] = g.astype(BF)
    center = x - jnp.mean(x, axis=1, keepdims=True)
    spread = jnp.mean(center * center, axis=1, keepdims=True)
    nrm_o[...] = (center * lax.rsqrt(spread + EPS) * gain[...]).astype(BF)

    @pl.when(i == 0)
    def _():
        gob_o[...] = jnp.zeros_like(gob_o)

    gob_o[...] += jnp.sum(g, axis=0, keepdims=True)


def prepare(src, tokens, cot, gain):
    sds = jax.ShapeDtypeStruct
    bs = pl.BlockSpec
    cap = tokens.shape[0]
    row = bs((BLK, D), lambda i: (i, 0))
    fixed = lambda i: (0, 0)
    return call(prepare_body, (sds((CAN, D), BF),) * 3 + (sds((1, D), F32),), [], (src, tokens, cot, gain),
                [bs((BLK, 1), lambda i: (i, 0)), bs((cap, D), fixed), bs((cap, D), fixed), bs((1, D), fixed)],
                (row, row, row, bs((1, D), fixed)), grid=(CAN // BLK,), cost=(6 * 10**9, 13 * 10**6))


def back_rows(dst, held, out):
    cap = out.shape[0]
    for at in range(0, cap, 480):
        n = min(480, cap - at)
        pick = (dst[at : at + n, :] == lax.broadcasted_iota(jnp.int32, (n, CAN), 1)).astype(BF)
        out[at : at + n, :] = dot_nn(pick, held[...]).astype(BF)


def output_body(dst, x, a, b, bias, out, held):
    for i in range(CAN // BLK):
        rows = pl.ds(i * BLK, BLK)
        held[rows, :] = (x[rows, :].astype(F32) + (a[rows, :].astype(F32) + b[rows, :].astype(F32) + bias[...])).astype(BF)
    back_rows(dst, held, out)


def gradient_body(dst, x, a, b, cot, gain, out, held):
    for i in range(CAN // BLK):
        rows = pl.ds(i * BLK, BLK)
        v = x[rows, :].astype(F32)
        center = v - jnp.mean(v, axis=1, keepdims=True)
        r = lax.rsqrt(jnp.mean(center * center, axis=1, keepdims=True) + EPS)
        xh = center * r
        g = (a[rows, :].astype(F32) + b[rows, :].astype(F32)) * gain[...]
        gx = r * (g - jnp.mean(g, axis=1, keepdims=True) - xh * jnp.mean(g * xh, axis=1, keepdims=True))
        held[rows, :] = (cot[rows, :].astype(F32) + gx).astype(BF)
    back_rows(dst, held, out)


def last_rows(body, cap, args):
    return call(body, jax.ShapeDtypeStruct((cap, D), BF), [pltpu.VMEM((CAN, D), BF)], args, [ANYWHERE] * len(args),
                cost=(4 * 10**9, 12 * 10**6))


def unit_ranges(c, j):
    first = [(96 * c + 32 * j, 32)]
    return first + [(192 + 480 * s + 240 * c + 80 * j, 80) for s in range(6)]


def split_body(place, w_in, w_out, *outs):
    c, f = place[0], place[1]
    for cc in range(2):

        @pl.when(c == cc)
        def _():
            for p in range(3):
                for n in range(3):
                    at = D * n + 384 * cc + 128 * p
                    outs[p][96 * n : 96 * n + 96, :] = w_in[:, at : at + 128]
            for j in range(3):
                cols = [w_in[:, 3 * D + u : 3 * D + u + n] for u, n in unit_ranges(cc, j)]
                m = jnp.concatenate(cols, axis=1)
                outs[3 + j][0:96, :] = m[:, :256]
                outs[3 + j][96:192, :] = m[:, 256:]
            outs[6][...] = w_out[:, 384 * cc : 384 * cc + 384]
            for j in range(3):
                for t in range(3):
                    lanes = slice(256 * t, 256 * t + 256)
                    at = 192 + 80 * t

                    @pl.when(f != 1)
                    def _():
                        outs[3 + j][at : at + 80, :] = w_out[240 * cc + 80 * j : 240 * cc + 80 * j + 80, lanes]

                    @pl.when(f == 1)
                    def _():
                        a, b = 144 * cc + 48 * j, 288 + 96 * cc + 32 * j
                        outs[3 + j][at : at + 48, :] = w_out[a : a + 48, lanes]
                        outs[3 + j][at + 48 : at + 80, :] = w_out[b : b + 32, lanes]


def split(place, w_in, w_out):
    sds = jax.ShapeDtypeStruct
    outs = (sds((288, 128), BF),) * 3 + (sds((432, 256), BF),) * 3 + (sds((480, 384), BF),)
    return call(split_body, outs, [], (place, w_in, w_out), [SCALARS, ANYWHERE, ANYWHERE], cost=(0, 4 * 10**6))


def slot_of(place, f):
    dz = place[3] ^ (f >> 1)
    return place[2] ^ (f & 1), ((dz & 1) << 1) | (dz >> 1)


def taken(place, near, far, f):
    side, at = slot_of(place, f)
    return jnp.where(side == 0, near[at], far[at])


def join_pair_body(place, near, far, w):
    for f in range(8):
        piece = taken(place, near, far, f)
        for n in range(3):
            w[96 * f : 96 * f + 96, 128 * n : 128 * n + 128] = piece[96 * n : 96 * n + 96]


def join_pair(place, near, far):
    return call(join_pair_body, jax.ShapeDtypeStruct((D, 384), BF), [], (place, near, far), [SCALARS, ANYWHERE, ANYWHERE],
                cost=(0, 2 * 10**6))


def join_chunk_body(place, near, far, win, wout):
    for f in range(8):
        piece = taken(place, near, far, f)
        for n in range(2):
            win[96 * f : 96 * f + 96, 256 * n : 256 * n + 256] = piece[96 * n : 96 * n + 96]
        for t in range(3):
            part = piece[192 + 80 * t : 272 + 80 * t]
            lanes = slice(256 * t, 256 * t + 256)
            if f == 1:
                wout[0:32, lanes] = part[48:]
            elif f > 1:
                wout[80 * f - 128 : 80 * f - 48, lanes] = part


def join_chunk(place, near, far):
    sds = jax.ShapeDtypeStruct
    return call(join_chunk_body, (sds((D, U), BF), sds((U, D), BF)), [], (place, near, far), [SCALARS, ANYWHERE, ANYWHERE],
                cost=(0, 4 * 10**6))


def put(place, near, far, f, fill):
    side, at = slot_of(place, f)

    @pl.when(side == 0)
    def _():
        fill(near.at[at])

    @pl.when(side != 0)
    def _():
        fill(far.at[at])


def cut_pair_body(place, dw, near, far):
    full = jnp.transpose(dw[...].astype(F32)).astype(BF)
    for f in range(8):

        def fill(ref, f=f):
            for n in range(3):
                ref[96 * n : 96 * n + 96, :] = full[96 * f : 96 * f + 96, 128 * n : 128 * n + 128]

        put(place, near, far, f, fill)


def cut_pair(place, dw):
    sds = jax.ShapeDtypeStruct
    return call(cut_pair_body, (sds((4, 288, 128), BF),) * 2, [], (place, dw), [SCALARS, ANYWHERE], cost=(0, 2 * 10**6))


def cut_chunk_body(place, dwin, dwout, slots, near, far):
    full = jnp.transpose(dwin[...].astype(F32)).astype(BF)
    for f in range(8):

        def fill(ref, f=f):
            for n in range(2):
                ref[96 * n : 96 * n + 96, :] = full[96 * f : 96 * f + 96, 256 * n : 256 * n + 256]
            for t in range(3):
                lanes = slice(256 * t, 256 * t + 256)
                at = 192 + 80 * t
                if f == 0:
                    ref[at : at + 80, :] = slots[0:80, lanes]
                elif f == 1:
                    ref[at : at + 48, :] = slots[80:128, lanes]
                    ref[at + 48 : at + 80, :] = dwout[0:32, lanes]
                else:
                    ref[at : at + 80, :] = dwout[80 * f - 128 : 80 * f - 48, lanes]

        put(place, near, far, f, fill)


def cut_chunk(place, dwin, dwout, slots):
    sds = jax.ShapeDtypeStruct
    return call(cut_chunk_body, (sds((4, 432, 256), BF),) * 2, [], (place, dwin, dwout, slots),
                [SCALARS] + [ANYWHERE] * 3, cost=(0, 4 * 10**6))


def final_body(place, w_in, ln, *refs):
    own, other = refs[:6], refs[6:12]
    gin, gout, gln = refs[12:]
    c, f = place[0], place[1]
    for cc in range(2):
        sources = [jnp.where(c == cc, a[...], b[...]) for a, b in zip(own, other)]
        for p in range(3):
            for n in range(3):
                at = D * n + 384 * cc + 128 * p
                gin[:, at : at + 128] = sources[p][96 * n : 96 * n + 96, :]
        for j in range(3):
            s = sources[3 + j]
            m = jnp.concatenate([s[0:96], s[96:192]], axis=1)
            done = 0
            for u, n in unit_ranges(cc, j):
                gin[:, 3 * D + u : 3 * D + u + n] = m[:, done : done + n]
                done += n
            for t in range(3):
                lanes = slice(256 * t, 256 * t + 256)
                part = s[192 + 80 * t : 272 + 80 * t]

                @pl.when(f != 1)
                def _():
                    gout[240 * cc + 80 * j : 240 * cc + 80 * j + 80, lanes] = part

                @pl.when(f == 1)
                def _():
                    a, b = 144 * cc + 48 * j, 288 + 96 * cc + 32 * j
                    gout[a : a + 48, lanes] = part[:48]
                    gout[b : b + 32, lanes] = part[48:]
    total = jnp.sum(w_in[...].astype(F32) * gin[...], axis=1, keepdims=True)
    gln[...] = total / ln[...]


def final(place, w_in, ln, own, other):
    sds = jax.ShapeDtypeStruct
    outs = (sds((96, 7 * D), F32), sds((480, D), F32), sds((96, 1), F32))
    return call(final_body, outs, [], (place, w_in, ln, *own, *other), [SCALARS] + [ANYWHERE] * 14, cost=(0, 10**7))


def routes():
    places = [(x, c, z, y) for x in range(2) for c in range(2) for z in range(4) for y in range(2)]
    number = lambda x, c, z, y: (x * 2 + c) * 8 + z * 2 + y
    pairs = lambda move: [(number(*p), number(*move(*p))) for p in places]
    out = {
        "core": pairs(lambda x, c, z, y: (x, 1 - c, z, y)),
        "x": pairs(lambda x, c, z, y: (1 - x, c, z, y)),
        "y": pairs(lambda x, c, z, y: (x, c, z, 1 - y)),
        "z1": pairs(lambda x, c, z, y: (x, c, z ^ 1, y)),
        "z2": pairs(lambda x, c, z, y: (x, c, z ^ 2, y)),
    }
    at = lambda n: (n % 8) // 2
    out["z2_up"] = [(a, b) for a, b in out["z2"] if at(a) == 0]
    out["z1_up"] = [(a, b) for a, b in out["z1"] if at(a) % 2 == 0]
    return out


def images(lengths, assign, device):
    own = assign == device
    small = own & (lengths == SMALL)
    large = own & (lengths == BIG)
    number = lax.iota(jnp.int32, lengths.shape[0])
    count = jnp.sum(small.astype(jnp.int32))
    has = jnp.sum(large.astype(jnp.int32))
    at = jnp.sum(jnp.where(large, number, 0))
    before = jnp.where(has > 0, jnp.sum((small & (number < at)).astype(jnp.int32)), count)
    return count, has, before


def row_tables(count, has, before, cap):
    row = lax.broadcasted_iota(jnp.int32, (CAN, 1), 0)
    rest = row - BIG * has
    slot, offset = rest // BLK, rest % BLK
    small_src = slot * SMALL + offset + jnp.where(slot >= before, BIG * has, 0)
    src = jnp.where(rest < 0, SMALL * before + row, jnp.where((offset < SMALL) & (slot < count), small_src, -1))
    row = lax.broadcasted_iota(jnp.int32, (cap, 1), 0)
    rest = row - SMALL * before
    inside = (rest >= 0) & (rest < BIG * has)
    rest = row - jnp.where(rest >= BIG * has, BIG * has, 0)
    slot, offset = rest // SMALL, rest % SMALL
    dst = jnp.where(inside, row - SMALL * before, jnp.where(slot < count, BIG * has + slot * BLK + offset, -1))
    return src, dst


def per_device_paired(
    tokens, lengths, assign, w_in, w_out, ln_scale, q_scale, k_scale, mlp_bias, out_bias, cotangent
):
    way = routes()
    go = lambda v, name: lax.ppermute(v, ("rep", "fsdp"), way[name])
    rep, f = lax.axis_index("rep"), lax.axis_index("fsdp")
    c, y, z = rep % 2, f % 2, f // 2
    cap = tokens.shape[0]
    place = jnp.stack([c, f, y, z]).astype(jnp.int32)

    device = rep * 8 + f
    count, has, before = images(lengths, assign, device)
    count_b, has_b, _ = images(lengths, assign, device + 8 - 16 * c)
    src, dst = row_tables(count, has, before, cap)
    blocks, blocks_b = jnp.where(has > 0, 7, count), jnp.where(has_b > 0, 7, count_b)
    base = BLK * blocks
    active = (BLK * (blocks + blocks_b) + RB - 1) // RB
    info = jnp.stack([active, 0 * base, has, count, base, has_b, count_b, 0 * base]).astype(jnp.int32)

    def gather(piece):
        two = jnp.stack([piece, go(piece, "z2")])
        four = jnp.concatenate([two, go(two, "z1")])
        return four, go(four, "y")

    packed = jnp.concatenate([ln_scale, q_scale, k_scale, mlp_bias, out_bias, jnp.zeros((48,), BF)]).reshape(5, 128)
    small = jnp.concatenate(gather(packed)).reshape(8, 640)
    shard = lax.iota(jnp.int32, 8)
    dz = z ^ (shard >> 1)
    position = 4 * (y ^ (shard & 1)) + (((dz & 1) << 1) | (dz >> 1))
    order = (position[:, None] == shard[None, :]).astype(BF)
    small = dot_nn(order, small)
    ln = small[:, :96].reshape(1, D)
    gq = jnp.tile(small[:, 96:104].reshape(1, HD), (1, 2))
    gk = jnp.tile(small[:, 104:112].reshape(1, HD), (1, 2))
    mb = small[:, 112:496].reshape(4 * D)
    ob = small[:, 496:592].reshape(1, D)
    mb = jnp.concatenate([mb[:192].reshape(2, 3, 32), mb[192:].reshape(6, 2, 3, 80).transpose(1, 2, 0, 3).reshape(2, 3, 480)], axis=2)
    mb = lax.dynamic_index_in_dim(mb, c, 0, False)

    pieces = split(place, w_in, w_out)
    wqkv = [join_pair(place, *gather(piece)) for piece in pieces[:3]]
    wo = pieces[6]
    wo = jnp.where(z == 0, wo, go(wo, "z2_up"))
    wo = jnp.where(z % 2 == 0, wo, go(wo, "z1_up"))
    wo_b = go(wo, "y")
    wo = jnp.concatenate([jnp.where(y == 0, wo, wo_b), jnp.where(y == 0, wo_b, wo)[:288]])
    mine = lax.dynamic_slice_in_dim(wo, 384 * c, 384, 0)
    theirs = go(lax.dynamic_slice_in_dim(wo, 384 - 384 * c, 384, 0), "core")
    wo = jnp.where(c == 0, jnp.concatenate([mine, theirs], axis=1), jnp.concatenate([theirs, mine], axis=1))
    chunks = [join_chunk(place, *gather(piece)) for piece in pieces[3:6]]

    x, nrm, cot, gob = prepare(src, tokens, cotangent, ln)

    def both(own):
        full = jnp.pad(own, ((0, ROWS - CAN), (0, 0)))
        return lax.dynamic_update_slice(full, go(own, "core"), (base, jnp.int32(0)))

    nrm2, cot2 = both(nrm), both(cot)

    def scatter(near, far):
        add = lambda a, b: (a.astype(F32) + b.astype(F32)).astype(BF)
        four = go(far, "y")
        s_near, s_far = add(near[:2], four[:2]), add(near[2:], four[2:])
        two = go(s_far, "z1")
        one = add(s_near[0], two[0])
        one = add(one, go(add(s_near[1], two[1]), "z2"))
        total = one.astype(F32) + go(one, "x").astype(F32)
        return total, go(total, "core")

    att, dqkv, dwo, dgq, dgk, reduced = [], [], [], 0.0, 0.0, []
    for p in range(3):
        a, dj, dw, dwo_p, dgq_p, dgk_p = attention(info, nrm2, cot2, wqkv[p], wo[128 * p : 128 * p + 128], gq, gk)
        att.append(a)
        dqkv.append(dj)
        dwo.append(dwo_p)
        dgq, dgk = dgq + dgq_p, dgk + dgk_p
        reduced.append(scatter(*cut_pair(place, dw)))
    dwo = jnp.concatenate(dwo)
    recv = go(lax.dynamic_slice_in_dim(dwo, 240 - 144 * c, 144, 0), "core")
    slots = jnp.where(c == 0, jnp.concatenate([dwo[:240], recv]), jnp.concatenate([recv, dwo[:96], dwo[240:]]))

    act, gm, dbs = [], [], []
    for j in range(3):
        a, g, dwin, dwout, db = mlp(info, nrm2, cot2, *chunks[j], mb[j : j + 1])
        act.append(a)
        gm.append(g)
        dbs.append(db)
        slot = jnp.concatenate([slots[80 * j : 80 * j + 80], slots[240 + 48 * j : 288 + 48 * j]])
        reduced.append(scatter(*cut_chunk(place, dwin, dwout, slot)))

    db = jnp.concatenate(dbs, axis=0).reshape(12, 128)
    none = jnp.zeros_like(db)
    vec = jnp.concatenate([gob.reshape(6, 128), dgq, dgk, jnp.where(c == 0, db, none), jnp.where(c == 0, none, db)])
    for name in ("core", "x", "y", "z1", "z2"):
        vec = vec + go(vec, name)
    g_ob = lax.dynamic_slice_in_dim(vec[:6].reshape(D), 96 * f, 96, 0)
    g_qs = lax.dynamic_slice_in_dim(vec[6, :HD] + vec[6, HD:], 8 * f, 8, 0)
    g_ks = lax.dynamic_slice_in_dim(vec[7, :HD] + vec[7, HD:], 8 * f, 8, 0)
    g_mb = vec[8:].reshape(2, 3, U)
    g_mb = jnp.concatenate([g_mb[:, :, :32].reshape(192), g_mb[:, :, 32:].reshape(2, 3, 6, 80).transpose(2, 0, 1, 3).reshape(2880)])
    g_mb = lax.dynamic_slice_in_dim(g_mb, 384 * f, 384, 0)

    def exchanged(part):
        return part[:CAN], go(lax.dynamic_slice_in_dim(part, base, CAN, 0), "core")

    part = sums(info, att + act, [wo[128 * p : 128 * p + 128] for p in range(3)] + [w for _, w in chunks], [False] * 6)
    output = last_rows(output_body, cap, (dst, x, *exchanged(part), ob))
    part = sums(info, dqkv + gm, wqkv + [w for w, _ in chunks], [True] * 6)
    grad_tokens = last_rows(gradient_body, cap, (dst, x, *exchanged(part), cot, ln))

    own_ln = ln_scale.astype(F32).reshape(96, 1)
    g_win, g_wout, g_ln = final(place, w_in, own_ln, [r[0] for r in reduced], [r[1] for r in reduced])
    return output, grad_tokens, g_win, g_wout, g_ln.reshape(96), g_qs, g_ks, g_mb, g_ob


HEADS = 12
epsilon = 1e-06


def layer_norm(values, weight_gain):
    center = values - jnp.mean(values, axis=-1, keepdims=True)
    spread = jnp.mean(center * center, axis=-1, keepdims=True)
    return center * lax.rsqrt(spread + epsilon) * weight_gain


def layout(lengths, assign, device, row_count):
    own = assign == device
    own_sizes = jnp.where(own, lengths, 0)
    own_ends = jnp.cumsum(own_sizes)
    own_starts = own_ends - own_sizes
    position = lax.broadcasted_iota(jnp.int32, (row_count, lengths.shape[0]), 0)
    number = lax.broadcasted_iota(jnp.int32, (row_count, lengths.shape[0]), 1)
    inside = (position >= own_starts[None, :]) & (position < own_ends[None, :])
    filled = jnp.any(inside, axis=1)
    segment = jnp.sum(jnp.where(inside, number, 0), axis=1)
    return (jnp.where(filled, segment, -1), filled)


def contract_rows(left, right):
    return lax.dot_general(
        left, right, (((0,), (0,)), ((), ())), preferred_element_type=jnp.float32
    )


def contract_cols(left, right):
    return lax.dot_general(
        left, right, (((1,), (1,)), ((), ())), preferred_element_type=jnp.float32
    )


def per_device(
    tokens, lengths, assign, w_in, w_out, ln_scale, q_scale, k_scale, mlp_bias, out_bias, cotangent
):
    row_count = tokens.shape[0]
    head_dim = HD
    head_count = HEADS
    width = head_dim * head_count
    factor = head_dim ** (-0.5)
    device = lax.axis_index("rep") * lax.axis_size("fsdp") + lax.axis_index("fsdp")
    segment, filled = layout(lengths, assign, device, row_count)
    allowed = segment[:, None] == segment[None, :]
    params = (w_in, w_out, ln_scale, q_scale, k_scale, mlp_bias, out_bias)
    full = (
        lax.all_gather(params[0], "fsdp", axis=0, tiled=True),
        lax.all_gather(params[1], "fsdp", axis=0, tiled=True),
        lax.all_gather(params[2], "fsdp", axis=0, tiled=True),
        lax.all_gather(params[3], "fsdp", axis=0, tiled=True),
        lax.all_gather(params[4], "fsdp", axis=0, tiled=True),
        lax.all_gather(params[5], "fsdp", axis=0, tiled=True),
        lax.all_gather(params[6], "fsdp", axis=0, tiled=True),
    )
    win_full, wout_full = (full[0], full[1])
    small = [arr.astype(jnp.float32) for arr in full[2:]]
    ln_full, qs_full, ks_full, mb_full, ob_full = small
    inputs = tokens.astype(jnp.float32)
    normed_f, ln_pull = jax.vjp(layer_norm, inputs, ln_full)
    normed = normed_f.astype(jnp.bfloat16)
    joined = jnp.dot(normed, win_full, preferred_element_type=jnp.float32)
    q_pre = joined[:, :width].reshape(row_count, head_count, head_dim)
    k_pre = joined[:, width : 2 * width].reshape(row_count, head_count, head_dim)
    values = joined[:, 2 * width : 3 * width].astype(jnp.bfloat16)
    hidden_pre = joined[:, 3 * width :]
    q_norm, q_pull = jax.vjp(layer_norm, q_pre, qs_full)
    k_norm, k_pull = jax.vjp(layer_norm, k_pre, ks_full)
    queries = q_norm.reshape(row_count, width).astype(jnp.bfloat16)
    keys_all = k_norm.reshape(row_count, width).astype(jnp.bfloat16)

    def head_slice(array, head_index):
        return lax.dynamic_slice_in_dim(array, head_index * head_dim, head_dim, 1)

    def head_scores(head_index):
        raw = (
            contract_cols(head_slice(queries, head_index), head_slice(keys_all, head_index))
            * factor
        )
        return jnp.where(allowed, raw, -1e30)

    def head_forward(head_index):
        scores = head_scores(head_index)
        top = jnp.max(scores, axis=1, keepdims=True)
        expon = jnp.exp(scores - top)
        total = jnp.sum(expon, axis=1, keepdims=True)
        probs = (expon / total).astype(jnp.bfloat16)
        head_out = jnp.dot(
            probs, head_slice(values, head_index), preferred_element_type=jnp.float32
        )
        return (head_out, (top + jnp.log(total))[:, 0])

    head_outs, log_totals = lax.map(head_forward, jnp.arange(head_count))
    attended = jnp.transpose(head_outs, (1, 0, 2)).reshape(row_count, width)
    activated, gelu_pull = jax.vjp(lambda pre, bias: jax.nn.gelu(pre + bias), hidden_pre, mb_full)
    merged = jnp.concatenate([attended, activated], axis=1).astype(jnp.bfloat16)
    result = jnp.dot(merged, wout_full, preferred_element_type=jnp.float32) + ob_full
    output = jnp.where(filled[:, None], inputs + result, 0.0).astype(jnp.bfloat16)
    back = (
        lax.all_gather(params[0], "fsdp", axis=0, tiled=True),
        lax.all_gather(params[1], "fsdp", axis=0, tiled=True),
        lax.all_gather(params[2], "fsdp", axis=0, tiled=True),
        lax.all_gather(params[3], "fsdp", axis=0, tiled=True),
        lax.all_gather(params[4], "fsdp", axis=0, tiled=True),
        lax.all_gather(params[5], "fsdp", axis=0, tiled=True),
        lax.all_gather(params[6], "fsdp", axis=0, tiled=True),
    )
    win_back, wout_back = (back[0], back[1])
    grad_rows = jnp.where(filled[:, None], cotangent.astype(jnp.float32), 0.0)
    grad_low = grad_rows.astype(jnp.bfloat16)
    grad_ob = jnp.sum(grad_rows, axis=0)
    grad_wout = contract_rows(merged, grad_low)
    grad_merged = contract_cols(grad_low, wout_back)
    grad_attended = grad_merged[:, :width].astype(jnp.bfloat16)
    grad_m, grad_mb = gelu_pull(grad_merged[:, width:])

    def head_backward(head_index):
        scores = head_scores(head_index)
        probs_full = jnp.exp(scores - log_totals[head_index][:, None])
        probs = probs_full.astype(jnp.bfloat16)
        grad_head = head_slice(grad_attended, head_index)
        grad_probs = contract_cols(grad_head, head_slice(values, head_index))
        inner = jnp.sum(probs_full * grad_probs, axis=1, keepdims=True)
        grad_scores = (probs_full * (grad_probs - inner)).astype(jnp.bfloat16)
        grad_q = (
            jnp.dot(
                grad_scores, head_slice(keys_all, head_index), preferred_element_type=jnp.float32
            )
            * factor
        )
        grad_k = contract_rows(grad_scores, head_slice(queries, head_index)) * factor
        grad_v = contract_rows(probs, grad_head)
        return (grad_q, grad_k, grad_v)

    grad_qh, grad_kh, grad_vh = lax.map(head_backward, jnp.arange(head_count))
    grad_qn = jnp.transpose(grad_qh, (1, 0, 2))
    grad_kn = jnp.transpose(grad_kh, (1, 0, 2))
    grad_values = jnp.transpose(grad_vh, (1, 0, 2)).reshape(row_count, width)
    grad_q_pre, grad_qs = q_pull(grad_qn)
    grad_k_pre, grad_ks = k_pull(grad_kn)
    grad_joined = jnp.concatenate(
        [
            grad_q_pre.reshape(row_count, width),
            grad_k_pre.reshape(row_count, width),
            grad_values,
            grad_m,
        ],
        axis=1,
    ).astype(jnp.bfloat16)
    grad_win = contract_rows(normed, grad_joined)
    grad_normed = contract_cols(grad_joined, win_back)
    grad_x_norm, grad_ln = ln_pull(grad_normed)
    grad_tokens = (grad_rows + grad_x_norm).astype(jnp.bfloat16)
    grads = (grad_win, grad_wout, grad_ln, grad_qs, grad_ks, grad_mb, grad_ob)
    shares = (
        lax.psum_scatter(grads[0], "fsdp", scatter_dimension=0, tiled=True),
        lax.psum_scatter(grads[1], "fsdp", scatter_dimension=0, tiled=True),
        lax.psum_scatter(grads[2], "fsdp", scatter_dimension=0, tiled=True),
        lax.psum_scatter(grads[3], "fsdp", scatter_dimension=0, tiled=True),
        lax.psum_scatter(grads[4], "fsdp", scatter_dimension=0, tiled=True),
        lax.psum_scatter(grads[5], "fsdp", scatter_dimension=0, tiled=True),
        lax.psum_scatter(grads[6], "fsdp", scatter_dimension=0, tiled=True),
    )
    shares = lax.psum(
        (shares[0], shares[1], shares[2], shares[3], shares[4], shares[5], shares[6]), "rep"
    )
    return (
        output,
        grad_tokens,
        shares[0],
        shares[1],
        shares[2],
        shares[3],
        shares[4],
        shares[5],
        shares[6],
    )


def solution(mesh):
    in_specs = (
        P(("rep", "fsdp"), None),
        P(),
        P(),
        P("fsdp", None),
        P("fsdp", None),
        P("fsdp"),
        P("fsdp"),
        P("fsdp"),
        P("fsdp"),
        P("fsdp"),
        P(("rep", "fsdp"), None),
    )
    out_specs = (
        P(("rep", "fsdp"), None),
        P(("rep", "fsdp"), None),
        P("fsdp", None),
        P("fsdp", None),
        P("fsdp"),
        P("fsdp"),
        P("fsdp"),
        P("fsdp"),
        P("fsdp"),
    )
    paired = dict(mesh.shape) == {"rep": 4, "fsdp": 8}
    return jax.shard_map(
        per_device_paired if paired else per_device, mesh=mesh, in_specs=in_specs, out_specs=out_specs, check_vma=False
    )
```

```python
import functools

import jax
import jax.numpy as jnp
from jax import lax
from jax.experimental import pallas as pl
from jax.experimental.pallas import tpu as pltpu
from jax.sharding import PartitionSpec as P

D = 768
HD = 64
SMALL = 196
BIG = 1024
BLK = 208
CAN = 7 * BLK
ROWS = 3072
ROOM = 3584
RB = 512
NRB = ROWS // RB
U = 512
EPS = 1e-06
BF = jnp.bfloat16
F32 = jnp.float32
VLIM = 60 * 1024 * 1024
ANYWHERE = pl.BlockSpec(memory_space=pltpu.VMEM)
TICK = jax.ShapeDtypeStruct((1,), F32)
SCALARS = pl.BlockSpec(memory_space=pltpu.SMEM)


def dot_nn(a, b):
    return lax.dot_general(a, b, (((1,), (0,)), ((), ())), preferred_element_type=F32)


def dot_nt(a, b):
    return lax.dot_general(a, b, (((1,), (1,)), ((), ())), preferred_element_type=F32)


def dot_tn(a, b):
    return lax.dot_general(a, b, (((0,), (0,)), ((), ())), preferred_element_type=F32)


def two_parts(x):
    hi = x.astype(BF)
    return hi, (x - hi.astype(F32)).astype(BF)


def call(body, out_shape, scratch, args, in_specs, out_specs=None, grid=None, prefetch=0, cost=None, after=(), tick=False):
    if after:
        inner, n, skip = body, len(args), len(after)

        def body(*refs):
            inner(*refs[:n], *refs[n + skip :])

        args = (*args, *after)
        in_specs = [*in_specs] + [pl.BlockSpec(memory_space=pl.ANY)] * skip
    params = pltpu.CompilerParams(vmem_limit_bytes=VLIM)
    if out_specs is None:
        out_specs = jax.tree.map(lambda _: ANYWHERE, out_shape)
    if tick:
        many = isinstance(out_shape, tuple)
        out_shape = (*out_shape, TICK) if many else (out_shape, TICK)
        out_specs = (*out_specs, SCALARS) if many else (out_specs, SCALARS)
        untold, place = body, len(args) + len(out_shape) - 1

        def body(*refs):
            refs[place][0] = jnp.float32(0)
            untold(*refs[:place], *refs[place + 1 :])

    spec = pltpu.PrefetchScalarGridSpec(
        num_scalar_prefetch=prefetch,
        grid=grid or (),
        in_specs=in_specs,
        out_specs=out_specs,
        scratch_shapes=scratch,
    )
    estimate = None if cost is None else pl.CostEstimate(flops=cost[0], bytes_accessed=cost[1], transcendentals=0)
    return pl.pallas_call(body, grid_spec=spec, out_shape=out_shape, compiler_params=params, cost_estimate=estimate)(*args)


NB, BLOCKS_A, LARGE_A, SMALL_A, BASE, BLOCKS_B, LARGE_B, SMALL_B, BEFORE = range(9)
CORE, FSDP, Y, Z, SELF, MATE = range(6)


def unit_ranges(c, j):
    first = [(96 * c + 32 * j, 32)]
    return first + [(192 + 480 * s + 240 * c + 80 * j, 80) for s in range(6)]


def split_body(place, lengths, assign, w_in, w_out, ln, qs, ks, mb, ob, info, g, m0, m1, m2, wo):
    def count(i, carry):
        before, small_a, large_a, small_b, large_b = carry
        large = (lengths[i] == BIG).astype(jnp.int32)
        a = (assign[i] == place[SELF]).astype(jnp.int32)
        b = (assign[i] == place[MATE]).astype(jnp.int32)
        before = jnp.where(a * large == 1, small_a, before)
        return before, small_a + a * (1 - large), large_a + a * large, small_b + b * (1 - large), large_b + b * large

    zero = jnp.int32(0)
    before, small_a, large_a, small_b, large_b = lax.fori_loop(0, lengths.shape[0], count, (zero,) * 5)
    blocks_a = jnp.where(large_a > 0, 7, small_a)
    blocks_b = jnp.where(large_b > 0, 7, small_b)
    info[NB] = (BLK * (blocks_a + blocks_b) + RB - 1) // RB
    info[BLOCKS_A], info[LARGE_A], info[SMALL_A] = blocks_a, large_a, small_a
    info[BASE] = BLK * blocks_a
    info[BLOCKS_B], info[LARGE_B], info[SMALL_B] = blocks_b, large_b, small_b
    info[BEFORE] = jnp.where(large_a > 0, before, small_a)

    c, f = place[CORE], place[FSDP]
    g[864:880, :] = jnp.zeros((16, 128), BF)
    g[864:865, :96] = ln[...]
    g[865:866, :8] = qs[...]
    g[866:867, :8] = ks[...]
    g[867:868, :96] = ob[...]
    for n in range(3):
        g[868 + n : 869 + n, :] = mb[:, 128 * n : 128 * n + 128]
    for cc in range(2):

        @pl.when(c == cc)
        def _():
            for p in range(3):
                for n in range(3):
                    at = D * n + 384 * cc + 128 * p
                    row = 288 * p + 96 * n
                    g[row : row + 96, :] = w_in[:, at : at + 128]
            wo[...] = w_out[:, 384 * cc : 384 * cc + 384]
            for j, piece in enumerate((m0, m1, m2)):
                cols = [w_in[:, 3 * D + u : 3 * D + u + n] for u, n in unit_ranges(cc, j)]
                m = jnp.concatenate(cols, axis=1)
                piece[0:96, :] = m[:, :256]
                piece[96:192, :] = m[:, 256:]
                for t in range(3):
                    lanes = slice(256 * t, 256 * t + 256)
                    at = 192 + 80 * t

                    @pl.when(f != 1)
                    def _():
                        piece[at : at + 80, :] = w_out[240 * cc + 80 * j : 240 * cc + 80 * j + 80, lanes]

                    @pl.when(f == 1)
                    def _():
                        a, b = 144 * cc + 48 * j, 288 + 96 * cc + 32 * j
                        piece[at : at + 48, :] = w_out[a : a + 48, lanes]
                        piece[at + 48 : at + 80, :] = w_out[b : b + 32, lanes]


def split(place, lengths, assign, w_in, w_out, *small):
    sds = jax.ShapeDtypeStruct
    outs = (sds((16,), jnp.int32), sds((880, 128), BF)) + (sds((432, 256), BF),) * 3 + (sds((480, 384), BF),)
    return call(split_body, outs, [], (place, lengths, assign, w_in, w_out, *small), [SCALARS] * 3 + [ANYWHERE] * 7,
                (SCALARS,) + (ANYWHERE,) * 5, cost=(0, 4 * 10**6))


def slot_of(place, f):
    dz = place[Z] ^ (f >> 1)
    return place[Y] ^ (f & 1), ((dz & 1) << 1) | (dz >> 1)


def taken(place, near, far, f, rows):
    side, at = slot_of(place, f)
    return jnp.where(side == 0, near[at, rows, :], far[at, rows, :])


def put(place, near, far, f, fill):
    side, at = slot_of(place, f)

    @pl.when(side == 0)
    def _():
        fill(near.at[at])

    @pl.when(side != 0)
    def _():
        fill(far.at[at])


def pick_rows(info, first, n, cap):
    row = first + lax.broadcasted_iota(jnp.int32, (n, 1), 0)
    large = BIG * info[LARGE_A]
    rest = row - large
    slot = sum((rest >= BLK * i).astype(jnp.int32) for i in range(1, 8))
    offset = rest - BLK * slot
    small = slot * SMALL + offset + jnp.where(slot >= info[BEFORE], large, 0)
    small = jnp.where((offset < SMALL) & (slot < info[SMALL_A]), small, -1)
    at = jnp.where(rest < 0, SMALL * info[BEFORE] + row, small)
    return (at == lax.broadcasted_iota(jnp.int32, (n, cap), 1)).astype(BF)


def pick_slots(info, first, n):
    row = first + lax.broadcasted_iota(jnp.int32, (n, 1), 0)
    large = BIG * info[LARGE_A]
    start = SMALL * info[BEFORE]
    inside = (row >= start) & (row < start + large)
    rest = row - jnp.where(row >= start + large, large, 0)
    slot = sum((rest >= SMALL * i).astype(jnp.int32) for i in range(1, 8))
    small = jnp.where(slot < info[SMALL_A], large + slot * BLK + rest - SMALL * slot, -1)
    at = jnp.where(inside, row - start, small)
    return (at == lax.broadcasted_iota(jnp.int32, (n, CAN), 1)).astype(BF)


def prepare_body(info, tokens, cot, out, gob_o):
    i = pl.program_id(0)
    pick = pick_rows(info, i * BLK, BLK, tokens.shape[0])
    g = dot_nn(pick, cot[...])
    out[0] = dot_nn(pick, tokens[...]).astype(BF)
    out[1] = g.astype(BF)

    @pl.when(i == 0)
    def _():
        gob_o[...] = jnp.zeros_like(gob_o)

    gob_o[...] += jnp.sum(g, axis=0, keepdims=True)


def prepare(info, tokens, cot):
    sds = jax.ShapeDtypeStruct
    bs = pl.BlockSpec
    cap = tokens.shape[0]
    fixed = lambda i, info: (0, 0)
    return call(prepare_body, (sds((2, CAN, D), BF), sds((1, D), F32)), [], (info, tokens, cot),
                [bs((cap, D), fixed), bs((cap, D), fixed)], (bs((2, BLK, D), lambda i, info: (0, i, 0)), bs((1, D), fixed)),
                grid=(CAN // BLK,), prefetch=1, cost=(6 * 10**9, 13 * 10**6))


def combine_body(info, place, own, other, near, far, nrm, cot, ln_o, ob_o, gain_o, mb_o):
    base = pl.multiple_of(info[BASE], 16)
    small = [taken(place, near, far, f, slice(864, 880)).astype(F32) for f in range(8)]
    ln = jnp.concatenate([s[0:1, :96] for s in small], axis=1)
    ln_o[...] = ln
    ob_o[...] = jnp.concatenate([s[3:4, :96] for s in small], axis=1)
    gain_o[...] = jnp.concatenate(([s[1:2, :8] for s in small] * 2) + ([s[2:3, :8] for s in small] * 2), axis=1)
    mb = jnp.concatenate([s[4 + n : 5 + n, :] for s in small for n in range(3)], axis=1)
    for j in range(3):
        rows = [jnp.concatenate([mb[:, u : u + n] for u, n in unit_ranges(cc, j)], axis=1) for cc in range(2)]
        mb_o[j : j + 1, :] = jnp.where(place[CORE] == 0, rows[0], rows[1])

    def copy(source, i, to):
        rows = pl.ds(pl.multiple_of(i * BLK, 16), BLK)
        to = pl.ds(pl.multiple_of(to, 16), BLK)
        v = source[0, rows, :].astype(F32)
        center = v - jnp.mean(v, axis=1, keepdims=True)
        spread = jnp.mean(center * center, axis=1, keepdims=True)
        nrm[to, :] = (center * lax.rsqrt(spread + EPS) * ln).astype(BF)
        cot[to, :] = source[1, rows, :]

    def from_own(i, carry):
        copy(own, i, i * BLK)
        return carry

    def from_other(i, carry):
        copy(other, i, base + i * BLK)
        return carry

    lax.fori_loop(0, info[BLOCKS_A], from_own, 0)
    lax.fori_loop(0, info[BLOCKS_B], from_other, 0)
    end = pl.ds(pl.multiple_of(base + info[BLOCKS_B] * BLK, 16), RB)
    nrm[end, :] = jnp.zeros((RB, D), BF)
    cot[end, :] = jnp.zeros((RB, D), BF)


def combine(info, place, own, other, near, far, after=()):
    sds = jax.ShapeDtypeStruct
    outs = (sds((ROOM, D), BF),) * 2 + (sds((1, D), F32),) * 2 + (sds((1, 256), F32), sds((3, U), F32))
    return call(combine_body, outs, [], (info, place, own, other, near, far), [SCALARS] * 2 + [ANYWHERE] * 4,
                cost=(0, 18 * 10**6), after=after)


def back_rows(info, held, out):
    cap = out.shape[0]
    for at in range(0, cap, 480):
        n = min(480, cap - at)
        out[at : at + n, :] = dot_nn(pick_slots(info, at, n), held[...]).astype(BF)


def output_body(info, x, a, b, bias, out, held):
    for i in range(CAN // BLK):
        rows = pl.ds(i * BLK, BLK)
        held[rows, :] = (x[0, rows, :].astype(F32) + (a[rows, :].astype(F32) + b[rows, :].astype(F32) + bias[...])).astype(BF)
    back_rows(info, held, out)


def gradient_body(info, x, a, b, gain, out, held):
    for i in range(CAN // BLK):
        rows = pl.ds(i * BLK, BLK)
        v = x[0, rows, :].astype(F32)
        center = v - jnp.mean(v, axis=1, keepdims=True)
        r = lax.rsqrt(jnp.mean(center * center, axis=1, keepdims=True) + EPS)
        xh = center * r
        g = (a[rows, :].astype(F32) + b[rows, :].astype(F32)) * gain[...]
        gx = r * (g - jnp.mean(g, axis=1, keepdims=True) - xh * jnp.mean(g * xh, axis=1, keepdims=True))
        held[rows, :] = (x[1, rows, :].astype(F32) + gx).astype(BF)
    back_rows(info, held, out)


def last_rows(body, cap, args, after=()):
    return call(body, jax.ShapeDtypeStruct((cap, D), BF), [pltpu.VMEM((CAN, D), BF)], args, [SCALARS] + [ANYWHERE] * (len(args) - 1),
                cost=(4 * 10**9, 12 * 10**6), after=after, tick=True)


def head_rows_body(place, a, b, mine, theirs):
    for yy in range(2):

        @pl.when(place[Y] == yy)
        def _():
            lo, hi = (a, b) if yy == 0 else (b, a)
            for cc in range(2):

                @pl.when(place[CORE] == cc)
                def _():
                    first, second = (mine, theirs) if cc == 0 else (theirs, mine)
                    first[...] = lo[0:384, :]
                    second[0:96, :] = lo[384:480, :]
                    second[96:384, :] = hi[0:288, :]


def head_rows(place, a, b):
    sds = jax.ShapeDtypeStruct
    return call(head_rows_body, (sds((384, 384), BF),) * 2, [], (place, a, b), [SCALARS, ANYWHERE, ANYWHERE], cost=(0, 10**6))


def attention_body(info, place, nrm_h, cot_h, near, far, wo_a, wo_b, gain, *refs, pair, cut):
    refs = list(refs)
    dws = [refs.pop(0) for _ in range(2)] if cut else []
    att_o, dqkv_o, w_o, wo_o, dwo_o, dg_o = refs[:6]
    refs = refs[6:]
    if cut:
        near_o, far_o = refs[:2]
        refs = refs[2:]
    else:
        dw_o = refs.pop(0)
    nrm, cot, sems, qa, kb, vv, qp, do, xh, rr, dqk, dv, dw, dwo = refs
    nb = info[NB]
    moves = []
    for i in range(NRB):
        rows = pl.ds(i * RB, RB)
        moves.append((pltpu.make_async_copy(nrm_h.at[rows, :], nrm.at[rows, :], sems.at[0, i]),
                      pltpu.make_async_copy(cot_h.at[rows, :], cot.at[rows, :], sems.at[1, i])))
        for move in moves[-1]:
            move.start()

    lane = lax.broadcasted_iota(jnp.int32, (1, 128), 1)
    first = lane < HD
    same = lax.broadcasted_iota(jnp.int32, (256, 256), 0) // HD == lax.broadcasted_iota(jnp.int32, (256, 256), 1) // HD
    mean_m = jnp.where(same, 1.0 / HD, 0.0).astype(BF)
    sum_m = jnp.where(same[:, :128] | same[:, 128:], 1.0, 0.0).astype(BF)
    c_exp = 1.4426950408889634 / 8.0

    row0 = 288 * pair
    for f in range(8):
        piece = taken(place, near, far, f, slice(row0, row0 + 288))
        for n in range(3):
            w_o[96 * f : 96 * f + 96, 128 * n : 128 * n + 128] = piece[96 * n : 96 * n + 96]
    mine, theirs = wo_a[128 * pair : 128 * pair + 128, :], wo_b[128 * pair : 128 * pair + 128, :]
    wo_o[:, :384] = jnp.where(place[CORE] == 0, mine, theirs)
    wo_o[:, 384:] = jnp.where(place[CORE] == 0, theirs, mine)

    def mean(x):
        return dot_nn(x.astype(BF), mean_m)

    def project(i):
        for move in moves[i]:
            move.wait()

        @pl.when(i < nb)
        def _():
            rows = pl.ds(i * RB, RB)
            y = dot_nn(nrm[rows, :], w_o[...])
            qk, v = y[:, :256], y[:, 256:]
            center = qk - mean(qk)
            r = lax.rsqrt(mean(center * center) + EPS)
            x = center * r
            xh[rows, :] = x
            rr[rows, :] = r
            qk = (x * gain[...]).astype(BF)
            q = qk[:, :128]
            qp[rows, :] = q
            hi, lo = two_parts(q.astype(F32) * c_exp)
            hi, lo = hi.astype(F32), lo.astype(F32)
            qa[0, rows, :] = jnp.where(first, hi, pltpu.roll(lo, HD, 1)).astype(BF)
            qa[1, rows, :] = jnp.where(first, pltpu.roll(hi, HD, 1), lo).astype(BF)
            kf = qk[:, 128:].astype(F32)
            kr = pltpu.roll(kf, HD, 1)
            kb[0, rows, :] = jnp.where(first, kf, kr).astype(BF)
            kb[1, rows, :] = jnp.where(first, kr, kf).astype(BF)
            vv[0, rows, :] = jnp.where(first, v, 1.0).astype(BF)
            vv[1, rows, :] = jnp.where(first, 1.0, v).astype(BF)
            do[rows, :] = dot_nt(cot[rows, :], wo_o[...]).astype(BF)
            dqk[rows, :] = jnp.zeros((RB, 256), F32)
            dv[rows, :] = jnp.zeros((RB, 128), F32)
            att_o[rows, :] = jnp.zeros((RB, 128), BF)

    for i in range(NRB):
        project(i)

    def blocks(items, masked, add):
        both = [(i, h) for i in range(len(items)) for h in range(2)]
        ql = [[qa[h, it[0], :] for h in range(2)] for it in items]
        kl = [[kb[h, it[1], :] for h in range(2)] for it in items]
        vl = [[vv[h, it[1], :] for h in range(2)] for it in items]
        grads = [do[it[0], :].astype(F32) for it in items]
        plain = [qp[it[0], :] for it in items]
        p, pb, xs = {}, {}, {}
        for i, h in both:
            e = jnp.exp2(dot_nt(ql[i][h], kl[i][h]))
            if masked:
                e = jnp.where(lax.broadcasted_iota(jnp.int32, e.shape, 1) < SMALL, e, 0.0)
            p[i, h] = e
            pb[i, h] = e.astype(BF)
        for i, h in both:
            xs[i, h] = dot_nn(pb[i, h], vl[i][h])
        outs, scaled, lefts = [], [], {}
        for i in range(len(items)):
            total = jnp.where(first, pltpu.roll(xs[i, 0], HD, 1), pltpu.roll(xs[i, 1], HD, 1))
            inverse = 1.0 / total
            out = jnp.where(first, xs[i, 0], xs[i, 1]) * inverse
            outs.append(out.astype(BF))
            hi, lo = two_parts(grads[i] * out)
            inner = dot_nn(jnp.concatenate([hi, lo], axis=1), sum_m) * inverse
            s = (grads[i] * inverse).astype(BF)
            scaled.append(s)
            sf = s.astype(F32)
            hi, lo = two_parts(inner)
            hi, lo = pltpu.roll(hi.astype(F32), HD, 1), pltpu.roll(lo.astype(F32), HD, 1)
            for h in range(2):
                own = first if h == 0 else jnp.logical_not(first)
                at = HD * (1 - h)
                side = jnp.where(lane == at, -hi, jnp.where(lane == at + 1, -lo, 0.0))
                lefts[i, h] = jnp.where(own, sf, side).astype(BF)
        ds = {}
        for i, h in both:
            ds[i, h] = (p[i, h] * dot_nt(lefts[i, h], vl[i][h])).astype(BF)
        dq = {t: dot_nn(ds[t], kl[t[0]][t[1]]) for t in both}
        dk = {t: dot_tn(ds[t], plain[t[0]]) for t in both}
        dvs = {t: dot_tn(pb[t], scaled[t[0]]) for t in both}
        for i, (q_rows, k_rows) in enumerate(items):
            att_o[q_rows, :] = outs[i]
            dqk[q_rows, :128] = jnp.where(first, dq[i, 0], dq[i, 1])
            new_k = jnp.where(first, dk[i, 0], dk[i, 1])
            new_v = jnp.where(first, dvs[i, 0], dvs[i, 1])
            if add:
                dqk[k_rows, 128:] += new_k
                dv[k_rows, :] += new_v
            else:
                dqk[k_rows, 128:] = new_k
                dv[k_rows, :] = new_v

    count_a, count_b = info[SMALL_A], info[SMALL_B]

    def small_rows(i):
        row_a = BIG * info[LARGE_A] + BLK * i
        row_b = info[BASE] + BIG * info[LARGE_B] + BLK * (i - count_a)
        row = jnp.where(i < count_a, row_a, jnp.where(i < count_a + count_b, row_b, ROWS))
        return pl.ds(pl.multiple_of(row, 16), BLK)

    def smalls(i, carry):
        a, b = small_rows(2 * i), small_rows(2 * i + 1)
        blocks([(a, a), (b, b)], True, False)
        return carry

    lax.fori_loop(0, (count_a + count_b + 1) // 2, smalls, 0)

    for base, large in ((0, info[LARGE_A]), (info[BASE], info[LARGE_B])):

        @pl.when(large == 1)
        def _():
            k_rows = pl.ds(pl.multiple_of(base, 16), BIG)

            def one(i, carry):
                blocks([(pl.ds(pl.multiple_of(base + i * 256, 16), 256), k_rows)], False, True)
                return carry

            lax.fori_loop(0, BIG // 256, one, 0)

    dw[...] = jnp.zeros_like(dw)
    dwo[...] = jnp.zeros_like(dwo)
    dg_o[...] = jnp.zeros_like(dg_o)

    def finish(i, carry):
        rows = pl.ds(pl.multiple_of(i * RB, RB), RB)
        g_out = dqk[rows, :] * 0.125
        x = xh[rows, :]
        dg_o[...] += jnp.sum(g_out * x, axis=0, keepdims=True)
        g = g_out * gain[...]
        g = rr[rows, :] * (g - mean(g) - x * mean(g * x))
        g = jnp.concatenate([g.astype(BF), dv[rows, :].astype(BF)], axis=1)
        dqkv_o[rows, :] = g
        dw[...] += dot_tn(g, nrm[rows, :])
        dwo[...] += dot_tn(att_o[rows, :], cot[rows, :])
        return carry

    lax.fori_loop(0, nb, finish, 0)
    dwo_o[...] = dwo[...].astype(BF)
    if not cut:
        dw_o[...] = dw[...].astype(BF)
        return
    full = [jnp.transpose(d[...].astype(F32)).astype(BF) for d in (*dws, dw)]
    for f in range(8):

        def fill(ref, f=f):
            for q in range(3):
                for n in range(3):
                    at = 288 * q + 96 * n
                    ref[at : at + 96, :] = full[q][96 * f : 96 * f + 96, 128 * n : 128 * n + 128]

        put(place, near_o, far_o, f, fill)


def attention(info, place, nrm, cot, near, far, wo_a, wo_b, gain, pair, dws=(), after=()):
    sds = jax.ShapeDtypeStruct
    cut = len(dws) > 0
    more = ROWS + 256
    outs = (sds((more, 128), BF), sds((ROWS, 384), BF), sds((D, 384), BF), sds((128, D), BF), sds((128, D), BF), sds((1, 256), F32))
    outs += ((sds((4, 864, 128), BF),) * 2) if cut else (sds((384, D), BF),)
    v = pltpu.VMEM
    scratch = [v((ROWS, D), BF)] * 2 + [pltpu.SemaphoreType.DMA((2, NRB))] + [v((2, more, 128), BF)] * 3 + [
        v((more, 128), BF)] * 2 + [v((ROWS, 256), F32)] * 2 + [v((more, 256), F32), v((more, 128), F32), v((384, D), F32), v((128, D), F32)]
    hbm = pl.BlockSpec(memory_space=pl.ANY)
    return call(functools.partial(attention_body, pair=pair, cut=cut), outs, scratch,
                (info, place, nrm, cot, near, far, wo_a, wo_b, gain, *dws),
                [SCALARS] * 2 + [hbm] * 2 + [ANYWHERE] * (5 + len(dws)), cost=(12 * 10**9, 14 * 10**6), after=after, tick=True)


def mlp_body(info, place, nrm, cot, near, far, mb, slots, act_o, gm_o, win, wout, near_o, far_o, db, dwin, dwout, *, chunk):
    i = pl.program_id(0)

    @pl.when(i == 0)
    def _():
        dwin[...] = jnp.zeros_like(dwin)
        dwout[...] = jnp.zeros_like(dwout)
        db[...] = jnp.zeros_like(db)
        for f in range(8):
            piece = taken(place, near, far, f, slice(0, 432))
            for n in range(2):
                win[96 * f : 96 * f + 96, 256 * n : 256 * n + 256] = piece[96 * n : 96 * n + 96]
            for t in range(3):
                part = piece[192 + 80 * t : 272 + 80 * t]
                lanes = slice(256 * t, 256 * t + 256)
                if f == 1:
                    wout[0:32, lanes] = part[48:]
                elif f > 1:
                    wout[80 * f - 128 : 80 * f - 48, lanes] = part

    @pl.when(i < info[NB])
    def _():
        c0 = 0.7978845608028654
        c1 = 0.044715 * c0
        x = nrm[...]
        g = cot[...]
        for n in range(0, U, SUB):
            lanes = slice(n, n + SUB)
            pre = dot_nn(x, win[:, lanes]) + mb[chunk : chunk + 1, lanes]
            ga = dot_nt(g, wout[lanes, :])
            sq = pre * pre
            t = jnp.tanh(pre * (c0 + c1 * sq))
            half = 0.5 * pre
            up = 1.0 + t
            act = (half * up).astype(BF)
            slope = 0.5 * up + half * (1.0 - t * t) * (c0 + 3.0 * c1 * sq)
            gmf = ga * slope
            gm = gmf.astype(BF)
            act_o[:, lanes] = act
            gm_o[:, lanes] = gm
            db[:, lanes] += jnp.sum(gmf, axis=0, keepdims=True)
            dwout[lanes, :] += dot_tn(act, g)
            dwin[lanes, :] += dot_tn(gm, x)

    @pl.when(i == pl.num_programs(0) - 1)
    def _():
        full = jnp.transpose(dwin[...]).astype(BF)
        for f in range(8):

            def fill(ref, f=f):
                for n in range(2):
                    ref[96 * n : 96 * n + 96, :] = full[96 * f : 96 * f + 96, 256 * n : 256 * n + 256]
                for t in range(3):
                    lanes = slice(256 * t, 256 * t + 256)
                    at = 192 + 80 * t
                    if f == 0:
                        ref[at : at + 80, :] = slots[80 * chunk : 80 * chunk + 80, lanes]
                    elif f == 1:
                        ref[at : at + 48, :] = slots[240 + 48 * chunk : 288 + 48 * chunk, lanes]
                        ref[at + 48 : at + 80, :] = dwout[0:32, lanes].astype(BF)
                    else:
                        ref[at : at + 80, :] = dwout[80 * f - 128 : 80 * f - 48, lanes].astype(BF)

            put(place, near_o, far_o, f, fill)


SUB = 256


def clamp(i, info, *_):
    return (jnp.minimum(i, info[NB] - 1), 0)


def whole(i, *_):
    return (0, 0)


def whole3(i, *_):
    return (0, 0, 0)


def mlp(info, place, nrm, cot, near, far, mb, slots, chunk, after=()):
    sds = jax.ShapeDtypeStruct
    outs = (sds((ROWS, U), BF), sds((ROWS, U), BF), sds((D, U), BF), sds((U, D), BF), sds((4, 432, 256), BF),
            sds((4, 432, 256), BF), sds((1, U), F32))
    bs = pl.BlockSpec
    piece = bs((4, 432, 256), whole3)
    in_specs = [bs((RB, D), clamp), bs((RB, D), clamp), piece, piece, bs((3, U), whole), bs((384, D), whole)]
    out_specs = (bs((RB, U), clamp), bs((RB, U), clamp), bs((D, U), whole), bs((U, D), whole), piece, piece, bs((1, U), whole))
    v = pltpu.VMEM
    scratch = [v((U, D), F32), v((U, D), F32)]
    return call(functools.partial(mlp_body, chunk=chunk), outs, scratch, (info, place, nrm, cot, near, far, mb, slots),
                in_specs, out_specs, grid=(NRB,), prefetch=2, cost=(10 * 10**9, 18 * 10**6), after=after, tick=True)


def sums_body(info, *refs, n, transposed):
    i = pl.program_id(0)
    lefts, rights, own, other, left, right, held = refs[:n], refs[n : 2 * n], *refs[2 * n :]

    @pl.when(i == 0)
    def _():
        at = 0
        for b in rights:
            k = b.shape[1] if transposed else b.shape[0]
            if transposed:
                right[:, at : at + k] = b[...]
            else:
                right[at : at + k, :] = b[...]
            at += k

    @pl.when(i < info[NB])
    def _():
        at = 0
        for a in lefts:
            left[:, at : at + a.shape[1]] = a[...]
            at += a.shape[1]
        total = dot_nt(left[...], right[...]) if transposed else dot_nn(left[...], right[...])
        held[pl.ds(pl.multiple_of(i * RB, RB), RB), :] = total.astype(BF)

    @pl.when(i >= info[NB])
    def _():
        held[pl.ds(pl.multiple_of(i * RB, RB), RB), :] = jnp.zeros((RB, D), BF)

    @pl.when(i == pl.num_programs(0) - 1)
    def _():
        own[...] = held[:CAN, :]
        other[...] = held[pl.ds(pl.multiple_of(info[BASE], 16), CAN), :]


def sums(info, lefts, rights, transposed, after=()):
    n = len(lefts)
    bs = pl.BlockSpec
    sds = jax.ShapeDtypeStruct
    in_specs = [bs((RB, a.shape[1]), clamp) for a in lefts] + [bs(b.shape, whole) for b in rights]
    k = sum(a.shape[1] for a in lefts)
    v = pltpu.VMEM
    scratch = [v((RB, k), BF), v((D, k) if transposed else (k, D), BF), v((ROWS, D), BF)]
    return call(functools.partial(sums_body, n=n, transposed=transposed), (sds((CAN, D), BF),) * 2, scratch,
                (info, *lefts, *rights), in_specs, (bs((CAN, D), whole),) * 2, grid=(NRB,), prefetch=1,
                cost=(2 * 2304 * k * D, 2 * 2304 * (k + D)), after=after, tick=True)


def final_body(place, w_in, ln, vec, *refs):
    own, other = refs[:4], refs[4:8]
    gin, gout, gln, gqs, gks, gmb, gob = refs[8:]
    c, f = place[CORE], place[FSDP]
    for cc in range(2):
        sources = [jnp.where(c == cc, a[...], b[...]) for a, b in zip(own, other)]
        for p in range(3):
            for n in range(3):
                at = D * n + 384 * cc + 128 * p
                gin[:, at : at + 128] = sources[0][288 * p + 96 * n : 288 * p + 96 * n + 96, :]
        for j in range(3):
            s = sources[1 + j]
            m = jnp.concatenate([s[0:96], s[96:192]], axis=1)
            done = 0
            for u, n in unit_ranges(cc, j):
                gin[:, 3 * D + u : 3 * D + u + n] = m[:, done : done + n]
                done += n
            for t in range(3):
                lanes = slice(256 * t, 256 * t + 256)
                part = s[192 + 80 * t : 272 + 80 * t]

                @pl.when(f != 1)
                def _():
                    gout[240 * cc + 80 * j : 240 * cc + 80 * j + 80, lanes] = part

                @pl.when(f == 1)
                def _():
                    a, b = 144 * cc + 48 * j, 288 + 96 * cc + 32 * j
                    gout[a : a + 48, lanes] = part[:48]
                    gout[b : b + 32, lanes] = part[48:]
    total = jnp.sum(w_in[...].astype(F32) * gin[...], axis=1, keepdims=True)
    gln[...] = total / ln[...]
    rows = [vec[r : r + 1, :] for r in range(32)]
    ob = jnp.concatenate(rows[:6], axis=1)
    qs = rows[6][:, :HD] + rows[6][:, HD:]
    ks = rows[7][:, :HD] + rows[7][:, HD:]
    parts = {}
    for cc in range(2):
        for j in range(3):
            m = jnp.concatenate(rows[8 + 12 * cc + 4 * j : 12 + 12 * cc + 4 * j], axis=1)
            done = 0
            for u, n in unit_ranges(cc, j):
                parts[u] = m[:, done : done + n]
                done += n
    mb = jnp.concatenate([parts[u] for u in sorted(parts)], axis=1)
    for ff in range(8):

        @pl.when(f == ff)
        def _():
            gob[...] = ob[:, 96 * ff : 96 * ff + 96]
            gqs[...] = qs[:, 8 * ff : 8 * ff + 8]
            gks[...] = ks[:, 8 * ff : 8 * ff + 8]
            gmb[...] = mb[:, 384 * ff : 384 * ff + 384]


def final(place, w_in, ln, vec, own, other, after=()):
    sds = jax.ShapeDtypeStruct
    outs = (sds((96, 7 * D), F32), sds((480, D), F32), sds((96, 1), F32), sds((1, 8), F32), sds((1, 8), F32),
            sds((1, 384), F32), sds((1, 96), F32))
    return call(final_body, outs, [], (place, w_in, ln, vec, *own, *other), [SCALARS] + [ANYWHERE] * 11, cost=(0, 10**7), after=after)


def routes():
    places = [(x, c, z, y) for x in range(2) for c in range(2) for z in range(4) for y in range(2)]
    number = lambda x, c, z, y: (x * 2 + c) * 8 + z * 2 + y
    pairs = lambda move: [(number(*p), number(*move(*p))) for p in places]
    out = {
        "core": pairs(lambda x, c, z, y: (x, 1 - c, z, y)),
        "x": pairs(lambda x, c, z, y: (1 - x, c, z, y)),
        "y": pairs(lambda x, c, z, y: (x, c, z, 1 - y)),
        "z1": pairs(lambda x, c, z, y: (x, c, z ^ 1, y)),
        "z2": pairs(lambda x, c, z, y: (x, c, z ^ 2, y)),
    }
    at = lambda n: (n % 8) // 2
    out["z2_up"] = [(a, b) for a, b in out["z2"] if at(a) == 0]
    out["z1_up"] = [(a, b) for a, b in out["z1"] if at(a) % 2 == 0]
    return out


def per_device_paired(
    tokens, lengths, assign, w_in, w_out, ln_scale, q_scale, k_scale, mlp_bias, out_bias, cotangent
):
    way = routes()
    go = lambda v, name: lax.ppermute(v, ("rep", "fsdp"), way[name])
    rep, f = lax.axis_index("rep"), lax.axis_index("fsdp")
    c, y, z = rep % 2, f % 2, f // 2
    cap = tokens.shape[0]
    device = rep * 8 + f
    place = jnp.stack([c, f, y, z, device, device + 8 - 16 * c]).astype(jnp.int32)

    late = lambda v, tick: v if tick is None else v + tick[0].astype(v.dtype)
    first = lambda piece, tick=None: jnp.stack([piece, late(go(piece, "z2"), tick)])
    second = lambda two, tick=None: jnp.concatenate([two, late(go(two, "z1"), tick)])
    third = lambda four: (four, go(four, "y"))
    vectors = (v.reshape(1, -1) for v in (ln_scale, q_scale, k_scale, mlp_bias, out_bias))
    info, g, m0, m1, m2, wo = split(place, lengths, assign, w_in, w_out, *vectors)
    own, gob = prepare(info, tokens, cotangent)
    other = go(own, "core")
    g = third(second(first(g)))
    nrm, cot, ln, ob, gain, mb = combine(info, place, own, other, *g)
    wo = jnp.where(z == 0, wo, go(wo, "z2_up"))
    wo = jnp.where(z % 2 == 0, wo, go(wo, "z1_up"))
    wo_a, wo_b = head_rows(place, wo, go(wo, "y"))
    wo_b = go(wo_b, "core")
    m0, m1, m2 = first(m0), first(m1), first(m2)

    def add(a, b, tick):
        return (a.astype(F32) + b.astype(F32) + tick[0]).astype(BF)

    def sum_y(near, far, tick):
        four = go(far, "y")
        return add(near[:2], four[:2], tick), add(near[2:], four[2:], tick)

    def sum_z1(near, far, tick):
        two = go(far, "z1")
        return add(near[0], two[0], tick), add(near[1], two[1], tick)

    def sum_z2(near, far, tick):
        return add(near, go(far, "z2"), tick)

    def sum_x(one, tick):
        return one.astype(F32) + go(one, "x").astype(F32) + tick[0]

    def heads(p, dws, after):
        return attention(info, place, nrm, cot, *g, wo_a, wo_b, gain, p, dws, after)

    *a0, tick = heads(0, (), (m0, m1, m2))
    m0, m1, m2 = second(m0, tick), second(m1, tick), second(m2, tick)
    *a1, tick = heads(1, (), (m0, m1, m2))
    m0, m1, m2 = third(m0), third(m1), third(m2)
    *a2, tick = heads(2, (a0[6], a1[6]), (m0[1], m1[1], a1[0]))
    att, dqkv, ws, wos, dwos, dgs = zip(a0[:6], a1[:6], a2[:6])
    g_h = a2[6:]
    dwo = jnp.concatenate(dwos)
    recv = go(lax.dynamic_slice_in_dim(dwo, 240 - 144 * c, 144, 0), "core")
    slots = jnp.where(c == 0, jnp.concatenate([dwo[:240], recv]), jnp.concatenate([recv, dwo[:96], dwo[240:]]))

    def hidden(j, m, after):
        return mlp(info, place, nrm, cot, *m, mb, slots, j, after)

    *h0, tick = hidden(0, m0, (m2[1],))
    g_h = sum_y(*g_h, tick)
    *h1, tick = hidden(1, m1, (*g_h, h0[0]))
    g_h, g_0 = sum_z1(*g_h, tick), sum_y(*h0[4:6], tick)
    *h2, tick = hidden(2, m2, (*g_h, *g_0, h1[0]))
    act, gm, wins, wouts, _, _, dbs = zip(h0, h1, h2)

    db = jnp.concatenate(dbs, axis=0).reshape(12, 128)
    none = jnp.zeros_like(db)
    vec = jnp.concatenate([gob.reshape(6, 128), sum(dgs).reshape(2, 128), jnp.where(c == 0, db, none), jnp.where(c == 0, none, db)])
    vec = vec + go(vec, "core")

    g_h, g_0, g_1 = sum_z2(*g_h, tick), sum_z1(*g_0, tick), sum_y(*h1[4:6], tick)
    part, away, tick = sums(info, (*att, *act), (*wos, *wouts), False, (g_h, *g_0, *g_1, vec))
    away = go(away, "core")
    g_h, g_0, g_1, g_2 = sum_x(g_h, tick), sum_z2(*g_0, tick), sum_z1(*g_1, tick), sum_y(*h2[4:6], tick)
    vec = vec + go(vec, "x") + tick[0]
    part_b, away_b, tick = sums(info, (*dqkv, *gm), (*ws, *wins), True, (g_h, g_0, *g_1, *g_2, vec))
    away_b = go(away_b, "core")
    g_0, g_1, g_2 = sum_x(g_0, tick), sum_z2(*g_1, tick), sum_z1(*g_2, tick)
    vec = vec + go(vec, "y") + tick[0]
    output, tick = last_rows(output_body, cap, (info, own, part, away, ob), (g_0, g_1, *g_2, vec))
    g_1, g_2 = sum_x(g_1, tick), sum_z2(*g_2, tick)
    vec = vec + go(vec, "z1") + tick[0]
    grad_tokens, tick = last_rows(gradient_body, cap, (info, own, part_b, away_b, ln), (g_1, g_2, vec))
    g_2 = sum_x(g_2, tick)
    vec = vec + go(vec, "z2") + tick[0]

    grads = (g_h, g_0, g_1, g_2)
    g_win, g_wout, *small = final(place, w_in, ln_scale.astype(F32).reshape(96, 1), vec, grads, [go(g, "core") for g in grads], (output, grad_tokens))
    return (output, grad_tokens, g_win, g_wout, *(g.reshape(-1) for g in small))


HEADS = 12
epsilon = 1e-06


def layer_norm(values, weight_gain):
    center = values - jnp.mean(values, axis=-1, keepdims=True)
    spread = jnp.mean(center * center, axis=-1, keepdims=True)
    return center * lax.rsqrt(spread + epsilon) * weight_gain


def layout(lengths, assign, device, row_count):
    own = assign == device
    own_sizes = jnp.where(own, lengths, 0)
    own_ends = jnp.cumsum(own_sizes)
    own_starts = own_ends - own_sizes
    position = lax.broadcasted_iota(jnp.int32, (row_count, lengths.shape[0]), 0)
    number = lax.broadcasted_iota(jnp.int32, (row_count, lengths.shape[0]), 1)
    inside = (position >= own_starts[None, :]) & (position < own_ends[None, :])
    filled = jnp.any(inside, axis=1)
    segment = jnp.sum(jnp.where(inside, number, 0), axis=1)
    return (jnp.where(filled, segment, -1), filled)


def contract_rows(left, right):
    return lax.dot_general(
        left, right, (((0,), (0,)), ((), ())), preferred_element_type=jnp.float32
    )


def contract_cols(left, right):
    return lax.dot_general(
        left, right, (((1,), (1,)), ((), ())), preferred_element_type=jnp.float32
    )


def per_device(
    tokens, lengths, assign, w_in, w_out, ln_scale, q_scale, k_scale, mlp_bias, out_bias, cotangent
):
    row_count = tokens.shape[0]
    head_dim = HD
    head_count = HEADS
    width = head_dim * head_count
    factor = head_dim ** (-0.5)
    device = lax.axis_index("rep") * lax.axis_size("fsdp") + lax.axis_index("fsdp")
    segment, filled = layout(lengths, assign, device, row_count)
    allowed = segment[:, None] == segment[None, :]
    params = (w_in, w_out, ln_scale, q_scale, k_scale, mlp_bias, out_bias)
    full = (
        lax.all_gather(params[0], "fsdp", axis=0, tiled=True),
        lax.all_gather(params[1], "fsdp", axis=0, tiled=True),
        lax.all_gather(params[2], "fsdp", axis=0, tiled=True),
        lax.all_gather(params[3], "fsdp", axis=0, tiled=True),
        lax.all_gather(params[4], "fsdp", axis=0, tiled=True),
        lax.all_gather(params[5], "fsdp", axis=0, tiled=True),
        lax.all_gather(params[6], "fsdp", axis=0, tiled=True),
    )
    win_full, wout_full = (full[0], full[1])
    small = [arr.astype(jnp.float32) for arr in full[2:]]
    ln_full, qs_full, ks_full, mb_full, ob_full = small
    inputs = tokens.astype(jnp.float32)
    normed_f, ln_pull = jax.vjp(layer_norm, inputs, ln_full)
    normed = normed_f.astype(jnp.bfloat16)
    joined = jnp.dot(normed, win_full, preferred_element_type=jnp.float32)
    q_pre = joined[:, :width].reshape(row_count, head_count, head_dim)
    k_pre = joined[:, width : 2 * width].reshape(row_count, head_count, head_dim)
    values = joined[:, 2 * width : 3 * width].astype(jnp.bfloat16)
    hidden_pre = joined[:, 3 * width :]
    q_norm, q_pull = jax.vjp(layer_norm, q_pre, qs_full)
    k_norm, k_pull = jax.vjp(layer_norm, k_pre, ks_full)
    queries = q_norm.reshape(row_count, width).astype(jnp.bfloat16)
    keys_all = k_norm.reshape(row_count, width).astype(jnp.bfloat16)

    def head_slice(array, head_index):
        return lax.dynamic_slice_in_dim(array, head_index * head_dim, head_dim, 1)

    def head_scores(head_index):
        raw = (
            contract_cols(head_slice(queries, head_index), head_slice(keys_all, head_index))
            * factor
        )
        return jnp.where(allowed, raw, -1e30)

    def head_forward(head_index):
        scores = head_scores(head_index)
        top = jnp.max(scores, axis=1, keepdims=True)
        expon = jnp.exp(scores - top)
        total = jnp.sum(expon, axis=1, keepdims=True)
        probs = (expon / total).astype(jnp.bfloat16)
        head_out = jnp.dot(
            probs, head_slice(values, head_index), preferred_element_type=jnp.float32
        )
        return (head_out, (top + jnp.log(total))[:, 0])

    head_outs, log_totals = lax.map(head_forward, jnp.arange(head_count))
    attended = jnp.transpose(head_outs, (1, 0, 2)).reshape(row_count, width)
    activated, gelu_pull = jax.vjp(lambda pre, bias: jax.nn.gelu(pre + bias), hidden_pre, mb_full)
    merged = jnp.concatenate([attended, activated], axis=1).astype(jnp.bfloat16)
    result = jnp.dot(merged, wout_full, preferred_element_type=jnp.float32) + ob_full
    output = jnp.where(filled[:, None], inputs + result, 0.0).astype(jnp.bfloat16)
    back = (
        lax.all_gather(params[0], "fsdp", axis=0, tiled=True),
        lax.all_gather(params[1], "fsdp", axis=0, tiled=True),
        lax.all_gather(params[2], "fsdp", axis=0, tiled=True),
        lax.all_gather(params[3], "fsdp", axis=0, tiled=True),
        lax.all_gather(params[4], "fsdp", axis=0, tiled=True),
        lax.all_gather(params[5], "fsdp", axis=0, tiled=True),
        lax.all_gather(params[6], "fsdp", axis=0, tiled=True),
    )
    win_back, wout_back = (back[0], back[1])
    grad_rows = jnp.where(filled[:, None], cotangent.astype(jnp.float32), 0.0)
    grad_low = grad_rows.astype(jnp.bfloat16)
    grad_ob = jnp.sum(grad_rows, axis=0)
    grad_wout = contract_rows(merged, grad_low)
    grad_merged = contract_cols(grad_low, wout_back)
    grad_attended = grad_merged[:, :width].astype(jnp.bfloat16)
    grad_m, grad_mb = gelu_pull(grad_merged[:, width:])

    def head_backward(head_index):
        scores = head_scores(head_index)
        probs_full = jnp.exp(scores - log_totals[head_index][:, None])
        probs = probs_full.astype(jnp.bfloat16)
        grad_head = head_slice(grad_attended, head_index)
        grad_probs = contract_cols(grad_head, head_slice(values, head_index))
        inner = jnp.sum(probs_full * grad_probs, axis=1, keepdims=True)
        grad_scores = (probs_full * (grad_probs - inner)).astype(jnp.bfloat16)
        grad_q = (
            jnp.dot(
                grad_scores, head_slice(keys_all, head_index), preferred_element_type=jnp.float32
            )
            * factor
        )
        grad_k = contract_rows(grad_scores, head_slice(queries, head_index)) * factor
        grad_v = contract_rows(probs, grad_head)
        return (grad_q, grad_k, grad_v)

    grad_qh, grad_kh, grad_vh = lax.map(head_backward, jnp.arange(head_count))
    grad_qn = jnp.transpose(grad_qh, (1, 0, 2))
    grad_kn = jnp.transpose(grad_kh, (1, 0, 2))
    grad_values = jnp.transpose(grad_vh, (1, 0, 2)).reshape(row_count, width)
    grad_q_pre, grad_qs = q_pull(grad_qn)
    grad_k_pre, grad_ks = k_pull(grad_kn)
    grad_joined = jnp.concatenate(
        [
            grad_q_pre.reshape(row_count, width),
            grad_k_pre.reshape(row_count, width),
            grad_values,
            grad_m,
        ],
        axis=1,
    ).astype(jnp.bfloat16)
    grad_win = contract_rows(normed, grad_joined)
    grad_normed = contract_cols(grad_joined, win_back)
    grad_x_norm, grad_ln = ln_pull(grad_normed)
    grad_tokens = (grad_rows + grad_x_norm).astype(jnp.bfloat16)
    grads = (grad_win, grad_wout, grad_ln, grad_qs, grad_ks, grad_mb, grad_ob)
    shares = (
        lax.psum_scatter(grads[0], "fsdp", scatter_dimension=0, tiled=True),
        lax.psum_scatter(grads[1], "fsdp", scatter_dimension=0, tiled=True),
        lax.psum_scatter(grads[2], "fsdp", scatter_dimension=0, tiled=True),
        lax.psum_scatter(grads[3], "fsdp", scatter_dimension=0, tiled=True),
        lax.psum_scatter(grads[4], "fsdp", scatter_dimension=0, tiled=True),
        lax.psum_scatter(grads[5], "fsdp", scatter_dimension=0, tiled=True),
        lax.psum_scatter(grads[6], "fsdp", scatter_dimension=0, tiled=True),
    )
    shares = lax.psum(
        (shares[0], shares[1], shares[2], shares[3], shares[4], shares[5], shares[6]), "rep"
    )
    return (
        output,
        grad_tokens,
        shares[0],
        shares[1],
        shares[2],
        shares[3],
        shares[4],
        shares[5],
        shares[6],
    )


def solution(mesh):
    in_specs = (
        P(("rep", "fsdp"), None),
        P(),
        P(),
        P("fsdp", None),
        P("fsdp", None),
        P("fsdp"),
        P("fsdp"),
        P("fsdp"),
        P("fsdp"),
        P("fsdp"),
        P(("rep", "fsdp"), None),
    )
    out_specs = (
        P(("rep", "fsdp"), None),
        P(("rep", "fsdp"), None),
        P("fsdp", None),
        P("fsdp", None),
        P("fsdp"),
        P("fsdp"),
        P("fsdp"),
        P("fsdp"),
        P("fsdp"),
    )
    paired = dict(mesh.shape) == {"rep": 4, "fsdp": 8}
    return jax.shard_map(
        per_device_paired if paired else per_device, mesh=mesh, in_specs=in_specs, out_specs=out_specs, check_vma=False
    )
```

```python
import functools

import jax
import jax.numpy as jnp
from jax import lax
from jax.experimental import pallas as pl
from jax.experimental.pallas import tpu as pltpu
from jax.sharding import PartitionSpec as P

D = 768
HD = 64
SMALL = 196
BIG = 1024
BLK = 208
CAN = 7 * BLK
ROWS = 3072
ROOM = 3584
RB = 512
NRB = ROWS // RB
U = 512
EPS = 1e-06
BF = jnp.bfloat16
F32 = jnp.float32
VLIM = 60 * 1024 * 1024
ANYWHERE = pl.BlockSpec(memory_space=pltpu.VMEM)
TICK = jax.ShapeDtypeStruct((1,), F32)
SCALARS = pl.BlockSpec(memory_space=pltpu.SMEM)


def dot_nn(a, b):
    return lax.dot_general(a, b, (((1,), (0,)), ((), ())), preferred_element_type=F32)


def dot_nt(a, b):
    return lax.dot_general(a, b, (((1,), (1,)), ((), ())), preferred_element_type=F32)


def dot_tn(a, b):
    return lax.dot_general(a, b, (((0,), (0,)), ((), ())), preferred_element_type=F32)


def two_parts(x):
    hi = x.astype(BF)
    return hi, (x - hi.astype(F32)).astype(BF)


def call(body, out_shape, scratch, args, in_specs, out_specs=None, grid=None, prefetch=0, cost=None, after=(), tick=False, alias=None):
    if after:
        inner, n, skip = body, len(args), len(after)

        def body(*refs):
            inner(*refs[:n], *refs[n + skip :])

        args = (*args, *after)
        in_specs = [*in_specs] + [pl.BlockSpec(memory_space=pl.ANY)] * skip
    params = pltpu.CompilerParams(vmem_limit_bytes=VLIM)
    if out_specs is None:
        out_specs = jax.tree.map(lambda _: ANYWHERE, out_shape)
    if tick:
        many = isinstance(out_shape, tuple)
        out_shape = (*out_shape, TICK) if many else (out_shape, TICK)
        out_specs = (*out_specs, SCALARS) if many else (out_specs, SCALARS)
        untold, place = body, len(args) + len(out_shape) - 1

        def body(*refs):
            refs[place][0] = jnp.float32(0)
            untold(*refs[:place], *refs[place + 1 :])

    spec = pltpu.PrefetchScalarGridSpec(
        num_scalar_prefetch=prefetch,
        grid=grid or (),
        in_specs=in_specs,
        out_specs=out_specs,
        scratch_shapes=scratch,
    )
    estimate = None if cost is None else pl.CostEstimate(flops=20 * cost[0], bytes_accessed=20 * cost[1], transcendentals=0)
    return pl.pallas_call(body, grid_spec=spec, out_shape=out_shape, compiler_params=params, cost_estimate=estimate, input_output_aliases=alias or {})(*args)


NB, BLOCKS_A, LARGE_A, SMALL_A, BASE, BLOCKS_B, LARGE_B, SMALL_B, BEFORE = range(9)
CORE, FSDP, Y, Z, SELF, MATE, X = range(7)


def unit_ranges(c, j):
    first = [(96 * c + 32 * j, 32)]
    return first + [(192 + 480 * s + 240 * c + 80 * j, 80) for s in range(6)]


def plan_body(place, lengths, assign, w_in, w_out, ln, qs, ks, mb, ob, info, a, wo):
    def count(i, carry):
        before, small_a, large_a, small_b, large_b = carry
        large = (lengths[i] == BIG).astype(jnp.int32)
        a = (assign[i] == place[SELF]).astype(jnp.int32)
        b = (assign[i] == place[MATE]).astype(jnp.int32)
        before = jnp.where(a * large == 1, small_a, before)
        return before, small_a + a * (1 - large), large_a + a * large, small_b + b * (1 - large), large_b + b * large

    zero = jnp.int32(0)
    before, small_a, large_a, small_b, large_b = lax.fori_loop(0, lengths.shape[0], count, (zero,) * 5)
    blocks_a = jnp.where(large_a > 0, 7, small_a)
    blocks_b = jnp.where(large_b > 0, 7, small_b)
    info[NB] = (BLK * (blocks_a + blocks_b) + RB - 1) // RB
    info[BLOCKS_A], info[LARGE_A], info[SMALL_A] = blocks_a, large_a, small_a
    info[BASE] = BLK * blocks_a
    info[BLOCKS_B], info[LARGE_B], info[SMALL_B] = blocks_b, large_b, small_b
    info[BEFORE] = jnp.where(large_a > 0, before, small_a)

    a[288:304, :] = jnp.zeros((16, 128), BF)
    a[288:289, :96] = ln[...]
    a[289:290, :8] = qs[...]
    a[290:291, :8] = ks[...]
    a[291:292, :96] = ob[...]
    for n in range(3):
        a[292 + n : 293 + n, :] = mb[:, 128 * n : 128 * n + 128]
    for cc in range(2):

        @pl.when(place[CORE] == cc)
        def _():
            for n in range(3):
                at = D * n + 384 * cc
                a[96 * n : 96 * n + 96, :] = w_in[:, at : at + 128]
                wo[480 * n : 480 * n + 480, :] = w_out[:, 384 * cc + 128 * n : 384 * cc + 128 * n + 128]


def plan(place, lengths, assign, w_in, w_out, *small):
    sds = jax.ShapeDtypeStruct
    outs = (sds((16,), jnp.int32), sds((304, 128), BF), sds((1440, 128), BF))
    return call(plan_body, outs, [], (place, lengths, assign, w_in, w_out, *small), [SCALARS] * 3 + [ANYWHERE] * 7,
                (SCALARS,) + (ANYWHERE,) * 2, cost=(0, 2 * 10**6))


def split_body(place, w_in, w_out, own, b, m, own_o, full):
    c, f = place[CORE], place[FSDP]
    for cc in range(2):

        @pl.when(c == cc)
        def _():
            for p in range(2):
                for n in range(3):
                    at = D * n + 384 * cc + 128 * p + 128
                    row = 288 * p + 96 * n
                    b[row : row + 96, :] = w_in[:, at : at + 128]
            for j in range(3):
                cols = [w_in[:, 3 * D + u : 3 * D + u + n] for u, n in unit_ranges(cc, j)]
                half = jnp.concatenate(cols, axis=1)
                full[j, 0:96, :] = half[:, :256]
                full[j, 96:192, :] = half[:, 256:]
                for t in range(3):
                    lanes = slice(256 * t, 256 * t + 256)
                    at = 192 + 80 * t

                    @pl.when(f != 1)
                    def _():
                        full[j, at : at + 80, :] = w_out[240 * cc + 80 * j : 240 * cc + 80 * j + 80, lanes]

                    @pl.when(f == 1)
                    def _():
                        a, b = 144 * cc + 48 * j, 288 + 96 * cc + 32 * j
                        full[j, at : at + 48, :] = w_out[a : a + 48, lanes]
                        full[j, at + 48 : at + 80, :] = w_out[b : b + 32, lanes]

    m[:, 0:THIRD, :] = full[:, 0:THIRD, :]
    m[:, THIRD:, :] = jnp.where(place[X] == 0, full[:, THIRD : 2 * THIRD, :], full[:, 2 * THIRD :, :])


THIRD = 144


def split(place, w_in, w_out, own, after):
    sds = jax.ShapeDtypeStruct
    outs = (sds((576, 128), BF), sds((3, 2 * THIRD, 256), BF), sds(own.shape, BF))
    hbm = pl.BlockSpec(memory_space=pl.ANY)
    return call(split_body, outs, [pltpu.VMEM((3, 3 * THIRD, 256), BF)], (place, w_in, w_out, own),
                [SCALARS] + [ANYWHERE] * 2 + [hbm], (ANYWHERE,) * 2 + (hbm,), cost=(0, 4 * 10**6), after=after, alias={3: 2})


def slot_of(place, f):
    dz = place[Z] ^ (f >> 1)
    return place[Y] ^ (f & 1), ((dz & 1) << 1) | (dz >> 1)


def taken(place, near, far, f, rows):
    side, at = slot_of(place, f)
    return jnp.where(side == 0, near[at, rows, :], far[at, rows, :])


def put(place, near, far, f, fill):
    side, at = slot_of(place, f)

    @pl.when(side == 0)
    def _():
        fill(near.at[at])

    @pl.when(side != 0)
    def _():
        fill(far.at[at])


def pick_rows(info, first, n, cap):
    row = first + lax.broadcasted_iota(jnp.int32, (n, 1), 0)
    large = BIG * info[LARGE_A]
    rest = row - large
    slot = sum((rest >= BLK * i).astype(jnp.int32) for i in range(1, 8))
    offset = rest - BLK * slot
    small = slot * SMALL + offset + jnp.where(slot >= info[BEFORE], large, 0)
    small = jnp.where((offset < SMALL) & (slot < info[SMALL_A]), small, -1)
    at = jnp.where(rest < 0, SMALL * info[BEFORE] + row, small)
    return (at == lax.broadcasted_iota(jnp.int32, (n, cap), 1)).astype(BF)


def pick_slots(info, first, n):
    row = first + lax.broadcasted_iota(jnp.int32, (n, 1), 0)
    large = BIG * info[LARGE_A]
    start = SMALL * info[BEFORE]
    inside = (row >= start) & (row < start + large)
    rest = row - jnp.where(row >= start + large, large, 0)
    slot = sum((rest >= SMALL * i).astype(jnp.int32) for i in range(1, 8))
    small = jnp.where(slot < info[SMALL_A], large + slot * BLK + rest - SMALL * slot, -1)
    at = jnp.where(inside, row - start, small)
    return (at == lax.broadcasted_iota(jnp.int32, (n, CAN), 1)).astype(BF)


def prepare_body(info, tokens, cot, out, gob_o):
    i = pl.program_id(0)
    pick = pick_rows(info, i * BLK, BLK, tokens.shape[0])
    g = dot_nn(pick, cot[...])
    out[0] = dot_nn(pick, tokens[...]).astype(BF)
    out[1] = g.astype(BF)

    @pl.when(i == 0)
    def _():
        gob_o[...] = jnp.zeros_like(gob_o)

    gob_o[...] += jnp.sum(g, axis=0, keepdims=True)


def prepare(info, tokens, cot, after):
    sds = jax.ShapeDtypeStruct
    bs = pl.BlockSpec
    cap = tokens.shape[0]
    fixed = lambda i, info: (0, 0)
    return call(prepare_body, (sds((2, CAN, D), BF), sds((1, D), F32)), [], (info, tokens, cot),
                [bs((cap, D), fixed), bs((cap, D), fixed)], (bs((2, BLK, D), lambda i, info: (0, i, 0)), bs((1, D), fixed)),
                grid=(CAN // BLK,), prefetch=1, cost=(6 * 10**9, 13 * 10**6), after=after, tick=True)


def combine_body(info, place, own, other, near, far, nrm, cot, ln_o, ob_o, gain_o, mb_o):
    base = pl.multiple_of(info[BASE], 16)
    small = [taken(place, near, far, f, slice(0, 16)).astype(F32) for f in range(8)]
    ln = jnp.concatenate([s[0:1, :96] for s in small], axis=1)
    ln_o[...] = ln
    ob_o[...] = jnp.concatenate([s[3:4, :96] for s in small], axis=1)
    gain_o[...] = jnp.concatenate(([s[1:2, :8] for s in small] * 2) + ([s[2:3, :8] for s in small] * 2), axis=1)
    mb = jnp.concatenate([s[4 + n : 5 + n, :] for s in small for n in range(3)], axis=1)
    for j in range(3):
        rows = [jnp.concatenate([mb[:, u : u + n] for u, n in unit_ranges(cc, j)], axis=1) for cc in range(2)]
        mb_o[j : j + 1, :] = jnp.where(place[CORE] == 0, rows[0], rows[1])

    def copy(source, i, to):
        rows = pl.ds(pl.multiple_of(i * BLK, 16), BLK)
        to = pl.ds(pl.multiple_of(to, 16), BLK)
        v = source[0, rows, :].astype(F32)
        center = v - jnp.mean(v, axis=1, keepdims=True)
        spread = jnp.mean(center * center, axis=1, keepdims=True)
        nrm[to, :] = (center * lax.rsqrt(spread + EPS) * ln).astype(BF)
        cot[to, :] = source[1, rows, :]

    def from_own(i, carry):
        copy(own, i, i * BLK)
        return carry

    def from_other(i, carry):
        copy(other, i, base + i * BLK)
        return carry

    lax.fori_loop(0, info[BLOCKS_A], from_own, 0)
    lax.fori_loop(0, info[BLOCKS_B], from_other, 0)
    end = pl.ds(pl.multiple_of(base + info[BLOCKS_B] * BLK, 16), RB)
    nrm[end, :] = jnp.zeros((RB, D), BF)
    cot[end, :] = jnp.zeros((RB, D), BF)


def combine(info, place, own, other, near, far, after=()):
    sds = jax.ShapeDtypeStruct
    outs = (sds((ROOM, D), BF),) * 2 + (sds((1, D), F32),) * 2 + (sds((1, 256), F32), sds((3, U), F32))
    return call(combine_body, outs, [], (info, place, own, other, near, far), [SCALARS] * 2 + [ANYWHERE] * 4,
                cost=(0, 18 * 10**6), after=after, tick=True)


def back_rows(info, held, out):
    cap = out.shape[0]
    for at in range(0, cap, 480):
        n = min(480, cap - at)
        out[at : at + n, :] = dot_nn(pick_slots(info, at, n), held[...]).astype(BF)


def output_body(info, x, a, b, bias, out, held):
    for i in range(CAN // BLK):
        rows = pl.ds(i * BLK, BLK)
        held[rows, :] = (x[0, rows, :].astype(F32) + (a[rows, :].astype(F32) + b[rows, :].astype(F32) + bias[...])).astype(BF)
    back_rows(info, held, out)


def gradient_body(info, x, a, b, gain, out, held):
    for i in range(CAN // BLK):
        rows = pl.ds(i * BLK, BLK)
        v = x[0, rows, :].astype(F32)
        center = v - jnp.mean(v, axis=1, keepdims=True)
        r = lax.rsqrt(jnp.mean(center * center, axis=1, keepdims=True) + EPS)
        xh = center * r
        g = (a[rows, :].astype(F32) + b[rows, :].astype(F32)) * gain[...]
        gx = r * (g - jnp.mean(g, axis=1, keepdims=True) - xh * jnp.mean(g * xh, axis=1, keepdims=True))
        held[rows, :] = (x[1, rows, :].astype(F32) + gx).astype(BF)
    back_rows(info, held, out)


def last_rows(body, cap, args, after=()):
    return call(body, jax.ShapeDtypeStruct((cap, D), BF), [pltpu.VMEM((CAN, D), BF)], args, [SCALARS] + [ANYWHERE] * (len(args) - 1),
                cost=(4 * 10**9, 12 * 10**6), after=after, tick=True)


def head_rows_body(place, a, b, mine, theirs):
    for yy in range(2):

        @pl.when(place[Y] == yy)
        def _():
            lo, hi = (a, b) if yy == 0 else (b, a)
            for cc in range(2):

                @pl.when(place[CORE] == cc)
                def _():
                    first, second = (mine, theirs) if cc == 0 else (theirs, mine)
                    for n in range(3):
                        lanes = slice(128 * n, 128 * n + 128)
                        at = PARTS + 480 * n
                        first[:, lanes] = lo[at : at + 384, :]
                        second[0:96, lanes] = lo[at + 384 : at + 480, :]
                        second[96:384, lanes] = hi[at : at + 288, :]


def head_rows(place, a, b):
    sds = jax.ShapeDtypeStruct
    return call(head_rows_body, (sds((384, 384), BF),) * 2, [], (place, a, b), [SCALARS, ANYWHERE, ANYWHERE], cost=(0, 10**6))


PARTS = 4 * 304


def attention_body(info, place, nrm_h, cot_h, near, far, wo_a, wo_b, gain, *refs, pair, cut):
    refs = list(refs)
    dws = [refs.pop(0) for _ in range(2)] if cut else []
    att_o, dqkv_o, w_o, wo_o, dwo_o, dg_o = refs[:6]
    refs = refs[6:]
    if cut:
        near_o, far_o = refs[:2]
        refs = refs[2:]
    else:
        dw_o = refs.pop(0)
    nrm, cot, sems, qa, kb, vv, qp, do, xh, rr, dqk, dv, dw, dwo = refs
    nb = info[NB]
    moves = []
    for i in range(NRB):
        rows = pl.ds(i * RB, RB)
        moves.append((pltpu.make_async_copy(nrm_h.at[rows, :], nrm.at[rows, :], sems.at[0, i]),
                      pltpu.make_async_copy(cot_h.at[rows, :], cot.at[rows, :], sems.at[1, i])))
        for move in moves[-1]:
            move.start()

    lane = lax.broadcasted_iota(jnp.int32, (1, 128), 1)
    first = lane < HD
    same = lax.broadcasted_iota(jnp.int32, (256, 256), 0) // HD == lax.broadcasted_iota(jnp.int32, (256, 256), 1) // HD
    mean_m = jnp.where(same, 1.0 / HD, 0.0).astype(BF)
    sum_m = jnp.where(same[:, :128] | same[:, 128:], 1.0, 0.0).astype(BF)
    c_exp = 1.4426950408889634 / 8.0

    for f in range(8):
        if pair == 0:
            side, at = slot_of(place, f)
            rows = pl.ds(pl.multiple_of(304 * at, 16), 288)
            piece = jnp.where(side == 0, near[rows, :], far[rows, :])
        else:
            piece = taken(place, near, far, f, slice(288 * (pair - 1), 288 * pair))
        for n in range(3):
            w_o[96 * f : 96 * f + 96, 128 * n : 128 * n + 128] = piece[96 * n : 96 * n + 96]
    mine, theirs = wo_a[128 * pair : 128 * pair + 128, :], wo_b[128 * pair : 128 * pair + 128, :]
    wo_o[:, :384] = jnp.where(place[CORE] == 0, mine, theirs)
    wo_o[:, 384:] = jnp.where(place[CORE] == 0, theirs, mine)

    def mean(x):
        return dot_nn(x.astype(BF), mean_m)

    def project(i):
        for move in moves[i]:
            move.wait()

        @pl.when(i < nb)
        def _():
            rows = pl.ds(i * RB, RB)
            y = dot_nn(nrm[rows, :], w_o[...])
            qk, v = y[:, :256], y[:, 256:]
            center = qk - mean(qk)
            r = lax.rsqrt(mean(center * center) + EPS)
            x = center * r
            xh[rows, :] = x
            rr[rows, :] = r
            qk = (x * gain[...]).astype(BF)
            q = qk[:, :128]
            qp[rows, :] = q
            hi, lo = two_parts(q.astype(F32) * c_exp)
            hi, lo = hi.astype(F32), lo.astype(F32)
            qa[0, rows, :] = jnp.where(first, hi, pltpu.roll(lo, HD, 1)).astype(BF)
            qa[1, rows, :] = jnp.where(first, pltpu.roll(hi, HD, 1), lo).astype(BF)
            kf = qk[:, 128:].astype(F32)
            kr = pltpu.roll(kf, HD, 1)
            kb[0, rows, :] = jnp.where(first, kf, kr).astype(BF)
            kb[1, rows, :] = jnp.where(first, kr, kf).astype(BF)
            vv[0, rows, :] = jnp.where(first, v, 1.0).astype(BF)
            vv[1, rows, :] = jnp.where(first, 1.0, v).astype(BF)
            do[rows, :] = dot_nt(cot[rows, :], wo_o[...]).astype(BF)
            dqk[rows, :] = jnp.zeros((RB, 256), F32)
            dv[rows, :] = jnp.zeros((RB, 128), F32)
            att_o[rows, :] = jnp.zeros((RB, 128), BF)

    for i in range(NRB):
        project(i)

    def blocks(items, masked, add):
        both = [(i, h) for i in range(len(items)) for h in range(2)]
        ql = [[qa[h, it[0], :] for h in range(2)] for it in items]
        kl = [[kb[h, it[1], :] for h in range(2)] for it in items]
        vl = [[vv[h, it[1], :] for h in range(2)] for it in items]
        grads = [do[it[0], :].astype(F32) for it in items]
        plain = [qp[it[0], :] for it in items]
        p, pb, xs = {}, {}, {}
        for i, h in both:
            e = jnp.exp2(dot_nt(ql[i][h], kl[i][h]))
            if masked:
                e = jnp.where(lax.broadcasted_iota(jnp.int32, e.shape, 1) < SMALL, e, 0.0)
            p[i, h] = e
            pb[i, h] = e.astype(BF)
        for i, h in both:
            xs[i, h] = dot_nn(pb[i, h], vl[i][h])
        outs, scaled, lefts = [], [], {}
        for i in range(len(items)):
            total = jnp.where(first, pltpu.roll(xs[i, 0], HD, 1), pltpu.roll(xs[i, 1], HD, 1))
            inverse = 1.0 / total
            out = jnp.where(first, xs[i, 0], xs[i, 1]) * inverse
            outs.append(out.astype(BF))
            hi, lo = two_parts(grads[i] * out)
            inner = dot_nn(jnp.concatenate([hi, lo], axis=1), sum_m) * inverse
            s = (grads[i] * inverse).astype(BF)
            scaled.append(s)
            sf = s.astype(F32)
            hi, lo = two_parts(inner)
            hi, lo = pltpu.roll(hi.astype(F32), HD, 1), pltpu.roll(lo.astype(F32), HD, 1)
            for h in range(2):
                own = first if h == 0 else jnp.logical_not(first)
                at = HD * (1 - h)
                side = jnp.where(lane == at, -hi, jnp.where(lane == at + 1, -lo, 0.0))
                lefts[i, h] = jnp.where(own, sf, side).astype(BF)
        ds = {}
        for i, h in both:
            ds[i, h] = (p[i, h] * dot_nt(lefts[i, h], vl[i][h])).astype(BF)
        dq = {t: dot_nn(ds[t], kl[t[0]][t[1]]) for t in both}
        dk = {t: dot_tn(ds[t], plain[t[0]]) for t in both}
        dvs = {t: dot_tn(pb[t], scaled[t[0]]) for t in both}
        for i, (q_rows, k_rows) in enumerate(items):
            att_o[q_rows, :] = outs[i]
            dqk[q_rows, :128] = jnp.where(first, dq[i, 0], dq[i, 1])
            new_k = jnp.where(first, dk[i, 0], dk[i, 1])
            new_v = jnp.where(first, dvs[i, 0], dvs[i, 1])
            if add:
                dqk[k_rows, 128:] += new_k
                dv[k_rows, :] += new_v
            else:
                dqk[k_rows, 128:] = new_k
                dv[k_rows, :] = new_v

    count_a, count_b = info[SMALL_A], info[SMALL_B]

    def small_rows(i):
        row_a = BIG * info[LARGE_A] + BLK * i
        row_b = info[BASE] + BIG * info[LARGE_B] + BLK * (i - count_a)
        row = jnp.where(i < count_a, row_a, jnp.where(i < count_a + count_b, row_b, ROWS))
        return pl.ds(pl.multiple_of(row, 16), BLK)

    def smalls(i, carry):
        a, b = small_rows(2 * i), small_rows(2 * i + 1)
        blocks([(a, a), (b, b)], True, False)
        return carry

    lax.fori_loop(0, (count_a + count_b + 1) // 2, smalls, 0)

    for base, large in ((0, info[LARGE_A]), (info[BASE], info[LARGE_B])):

        @pl.when(large == 1)
        def _():
            k_rows = pl.ds(pl.multiple_of(base, 16), BIG)

            def one(i, carry):
                blocks([(pl.ds(pl.multiple_of(base + i * 256, 16), 256), k_rows)], False, True)
                return carry

            lax.fori_loop(0, BIG // 256, one, 0)

    dw[...] = jnp.zeros_like(dw)
    dwo[...] = jnp.zeros_like(dwo)
    dg_o[...] = jnp.zeros_like(dg_o)

    def finish(i, carry):
        rows = pl.ds(pl.multiple_of(i * RB, RB), RB)
        g_out = dqk[rows, :] * 0.125
        x = xh[rows, :]
        dg_o[...] += jnp.sum(g_out * x, axis=0, keepdims=True)
        g = g_out * gain[...]
        g = rr[rows, :] * (g - mean(g) - x * mean(g * x))
        g = jnp.concatenate([g.astype(BF), dv[rows, :].astype(BF)], axis=1)
        dqkv_o[rows, :] = g
        dw[...] += dot_tn(g, nrm[rows, :])
        dwo[...] += dot_tn(att_o[rows, :], cot[rows, :])
        return carry

    lax.fori_loop(0, nb, finish, 0)
    dwo_o[...] = dwo[...].astype(BF)
    if not cut:
        dw_o[...] = dw[...].astype(BF)
        return
    full = [jnp.transpose(d[...].astype(F32)).astype(BF) for d in (*dws, dw)]
    for f in range(8):

        def fill(ref, f=f):
            for q in range(3):
                for n in range(3):
                    at = 288 * q + 96 * n
                    ref[at : at + 96, :] = full[q][96 * f : 96 * f + 96, 128 * n : 128 * n + 128]

        put(place, near_o, far_o, f, fill)


def attention(info, place, nrm, cot, near, far, wo_a, wo_b, gain, pair, dws=(), after=()):
    sds = jax.ShapeDtypeStruct
    cut = len(dws) > 0
    more = ROWS + 256
    outs = (sds((more, 128), BF), sds((ROWS, 384), BF), sds((D, 384), BF), sds((128, D), BF), sds((128, D), BF), sds((1, 256), F32))
    outs += ((sds((4, 864, 128), BF),) * 2) if cut else (sds((384, D), BF),)
    v = pltpu.VMEM
    scratch = [v((ROWS, D), BF)] * 2 + [pltpu.SemaphoreType.DMA((2, NRB))] + [v((2, more, 128), BF)] * 3 + [
        v((more, 128), BF)] * 2 + [v((ROWS, 256), F32)] * 2 + [v((more, 256), F32), v((more, 128), F32), v((384, D), F32), v((128, D), F32)]
    hbm = pl.BlockSpec(memory_space=pl.ANY)
    return call(functools.partial(attention_body, pair=pair, cut=cut), outs, scratch,
                (info, place, nrm, cot, near, far, wo_a, wo_b, gain, *dws),
                [SCALARS] * 2 + [hbm] * 2 + [ANYWHERE] * (5 + len(dws)), cost=(12 * 10**9, 14 * 10**6), after=after, tick=True)


def mlp_body(info, place, nrm_h, cot_h, near, far, cross, mb, slots, act_h, gm_h, win, wout, near_o, far_o, db,
             nrm, cot, act, gm, dwin, dwout, sems, out_sems, *, chunk):
    nb = info[NB]

    def incoming(i):
        rows = pl.ds(pl.multiple_of(i * RB, RB), RB)
        return (pltpu.make_async_copy(nrm_h.at[rows, :], nrm.at[rows, :], sems.at[0, i]),
                pltpu.make_async_copy(cot_h.at[rows, :], cot.at[rows, :], sems.at[1, i]))

    def outgoing(i):
        rows = pl.ds(pl.multiple_of(i * RB, RB), RB)
        return (pltpu.make_async_copy(act.at[rows, :], act_h.at[rows, :], out_sems.at[0, i]),
                pltpu.make_async_copy(gm.at[rows, :], gm_h.at[rows, :], out_sems.at[1, i]))

    def over(body):
        def step(i, carry):
            body(i)
            return carry

        lax.fori_loop(0, nb, step, 0)

    over(lambda i: [move.start() for move in incoming(i)])
    dwin[...] = jnp.zeros_like(dwin)
    dwout[...] = jnp.zeros_like(dwout)
    db[...] = jnp.zeros_like(db)
    for f in range(8):
        side, at = slot_of(place, f)
        piece = jnp.where(side == 0, near[at, 0], far[at, 0])
        third = cross[4 * side + at, 0]
        swap = place[X] != 0
        piece = jnp.concatenate([piece[:THIRD], jnp.where(swap, third, piece[THIRD:]), jnp.where(swap, piece[THIRD:], third)])
        for n in range(2):
            win[96 * f : 96 * f + 96, 256 * n : 256 * n + 256] = piece[96 * n : 96 * n + 96]
        for t in range(3):
            part = piece[192 + 80 * t : 272 + 80 * t]
            lanes = slice(256 * t, 256 * t + 256)
            if f == 1:
                wout[0:32, lanes] = part[48:]
            elif f > 1:
                wout[80 * f - 128 : 80 * f - 48, lanes] = part

    c0 = 0.7978845608028654
    c1 = 0.044715 * c0

    def start(i):
        rows = pl.ds(pl.multiple_of(i * RB, RB), RB)
        for move in incoming(i):
            move.wait()
        return dot_nn(nrm[rows, :], win[...]) + mb[chunk : chunk + 1, :], dot_nt(cot[rows, :], wout[...])

    def middle(i, pre, ga):
        rows = pl.ds(pl.multiple_of(i * RB, RB), RB)
        sq = pre * pre
        t = jnp.tanh(pre * (c0 + c1 * sq))
        half = 0.5 * pre
        up = 1.0 + t
        act[rows, :] = (half * up).astype(BF)
        slope = 0.5 * up + half * (1.0 - t * t) * (c0 + 3.0 * c1 * sq)
        gmf = ga * slope
        gm[rows, :] = gmf.astype(BF)
        db[...] += jnp.sum(gmf, axis=0, keepdims=True)

    def end(i):
        rows = pl.ds(pl.multiple_of(i * RB, RB), RB)
        dwout[...] += dot_tn(act[rows, :], cot[rows, :])
        dwin[...] += dot_tn(gm[rows, :], nrm[rows, :])

    middle(0, *start(0))

    def step(i, carry):
        pre, ga = start(i)
        middle(i, pre, ga)
        end(i - 1)
        for move in outgoing(i - 1):
            move.start()
        return carry

    lax.fori_loop(1, nb, step, 0)
    end(nb - 1)
    for move in outgoing(nb - 1):
        move.start()
    full = jnp.transpose(dwin[...]).astype(BF)
    for f in range(8):

        def fill(ref, f=f):
            for n in range(2):
                ref[96 * n : 96 * n + 96, :] = full[96 * f : 96 * f + 96, 256 * n : 256 * n + 256]
            for t in range(3):
                lanes = slice(256 * t, 256 * t + 256)
                at = 192 + 80 * t
                if f == 0:
                    ref[at : at + 80, :] = slots[80 * chunk : 80 * chunk + 80, lanes]
                elif f == 1:
                    ref[at : at + 48, :] = slots[240 + 48 * chunk : 288 + 48 * chunk, lanes]
                    ref[at + 48 : at + 80, :] = dwout[0:32, lanes].astype(BF)
                else:
                    ref[at : at + 80, :] = dwout[80 * f - 128 : 80 * f - 48, lanes].astype(BF)

        put(place, near_o, far_o, f, fill)
    over(lambda i: [move.wait() for move in outgoing(i)])


def clamp(i, info, *_):
    return (jnp.minimum(i, info[NB] - 1), 0)


def whole(i, *_):
    return (0, 0)


def whole3(i, *_):
    return (0, 0, 0)


def mlp(info, place, nrm, cot, near, far, cross, mb, slots, chunk, after=()):
    sds = jax.ShapeDtypeStruct
    outs = (sds((ROWS, U), BF), sds((ROWS, U), BF), sds((D, U), BF), sds((U, D), BF), sds((4, 432, 256), BF),
            sds((4, 432, 256), BF), sds((1, U), F32))
    hbm = pl.BlockSpec(memory_space=pl.ANY)
    bs = pl.BlockSpec
    own = lambda i: (0, chunk, 0, 0)
    pieces = [bs((4, 1, 2 * THIRD, 256), own), bs((4, 1, 2 * THIRD, 256), own), bs((8, 1, THIRD, 256), own)]
    fixed = [bs(v.shape, lambda i: (0, 0)) for v in (mb, slots)]
    done = [bs(o.shape, (lambda i: (0, 0)) if len(o.shape) == 2 else (lambda i: (0, 0, 0))) for o in outs[2:]]
    v = pltpu.VMEM
    scratch = [v((ROWS, D), BF)] * 2 + [v((ROWS, U), BF)] * 2 + [v((U, D), F32)] * 2 + [pltpu.SemaphoreType.DMA((2, NRB))] * 2
    return call(functools.partial(mlp_body, chunk=chunk), outs, scratch, (info, place, nrm, cot, near, far, cross, mb, slots),
                [SCALARS] * 2 + [hbm] * 2 + pieces + fixed, (hbm,) * 2 + tuple(done), grid=(1,), cost=(10 * 10**9, 18 * 10**6),
                after=after, tick=True)


def sums_body(info, *refs, n, transposed):
    i = pl.program_id(0)
    lefts, rights, own, other, left, right, held, sems = refs[:n], refs[n : 2 * n], *refs[2 * n :]

    @pl.when(i == 0)
    def _():
        at = 0
        for b in rights:
            k = b.shape[1] if transposed else b.shape[0]
            if transposed:
                right[:, at : at + k] = b[...]
            else:
                right[at : at + k, :] = b[...]
            at += k

    @pl.when(i < info[NB])
    def _():
        at = 0
        for a in lefts:
            left[:, at : at + a.shape[1]] = a[...]
            at += a.shape[1]
        total = dot_nt(left[...], right[...]) if transposed else dot_nn(left[...], right[...])
        held[pl.ds(pl.multiple_of(i * RB, RB), RB), :] = total.astype(BF)

    @pl.when(i >= info[NB])
    def _():
        held[pl.ds(pl.multiple_of(i * RB, RB), RB), :] = jnp.zeros((RB, D), BF)

    move_own = pltpu.make_async_copy(held.at[pl.ds(0, CAN), :], own, sems.at[0])

    @pl.when(i == (CAN - 1) // RB)
    def _():
        move_own.start()

    @pl.when(i == pl.num_programs(0) - 1)
    def _():
        move_other = pltpu.make_async_copy(held.at[pl.ds(pl.multiple_of(info[BASE], 16), CAN), :], other, sems.at[1])
        move_other.start()
        move_own.wait()
        move_other.wait()


def sums(info, lefts, rights, transposed, after=()):
    n = len(lefts)
    bs = pl.BlockSpec
    sds = jax.ShapeDtypeStruct
    in_specs = [bs((RB, a.shape[1]), clamp) for a in lefts] + [bs(b.shape, whole) for b in rights]
    k = sum(a.shape[1] for a in lefts)
    v = pltpu.VMEM
    scratch = [v((RB, k), BF), v((D, k) if transposed else (k, D), BF), v((ROWS, D), BF), pltpu.SemaphoreType.DMA((2,))]
    hbm = bs(memory_space=pl.ANY)
    return call(functools.partial(sums_body, n=n, transposed=transposed), (sds((CAN, D), BF),) * 2, scratch,
                (info, *lefts, *rights), in_specs, (hbm,) * 2, grid=(NRB,), prefetch=1,
                cost=(2 * 2304 * k * D, 2 * 2304 * (k + D)), after=after, tick=True)


def adds_body(*refs, kinds):
    n = len(kinds)
    outs = list(refs[2 * n :])
    for (a, b), kind in zip(zip(refs[:n], refs[n : 2 * n]), kinds):
        total = a[...].astype(F32) + b[...].astype(F32)
        if kind == "halves":
            half = a.shape[0] // 2
            outs.pop(0)[...] = total[:half].astype(BF)
            outs.pop(0)[...] = total[half:].astype(BF)
        else:
            out = outs.pop(0)
            out[...] = total.astype(out.dtype)


def adds(items, after):
    sds = jax.ShapeDtypeStruct
    outs, shapes = [], []
    for a, _, kind in items:
        shape = (a.shape[0] // 2, *a.shape[1:]) if kind == "halves" else a.shape
        outs += [sds(shape, F32 if kind == "float" else BF)] * (2 if kind == "halves" else 1)
    args = [a for a, _, _ in items] + [b for _, b, _ in items]
    done = call(functools.partial(adds_body, kinds=[k for _, _, k in items]), tuple(outs), [], args, [ANYWHERE] * len(args),
                cost=(0, 3 * 10**6), after=after)
    done, results = list(done), []
    for _, _, kind in items:
        results.append((done.pop(0), done.pop(0)) if kind == "halves" else done.pop(0))
    return results


def final_body(place, w_in, ln, *refs):
    own, other = refs[:5], refs[5:10]
    gin, gout, gln, gqs, gks, gmb, gob = refs[10:]
    vec_a, vec_b = own[4], other[4]
    c, f = place[CORE], place[FSDP]
    for cc in range(2):
        sources = [jnp.where(c == cc, a[0], b[0]) for a, b in zip(own[:4], other[:4])]
        for p in range(3):
            for n in range(3):
                at = D * n + 384 * cc + 128 * p
                gin[:, at : at + 128] = sources[0][288 * p + 96 * n : 288 * p + 96 * n + 96, :]
        for j in range(3):
            s = sources[1 + j]
            m = jnp.concatenate([s[0:96], s[96:192]], axis=1)
            done = 0
            for u, n in unit_ranges(cc, j):
                gin[:, 3 * D + u : 3 * D + u + n] = m[:, done : done + n]
                done += n
            for t in range(3):
                lanes = slice(256 * t, 256 * t + 256)
                part = s[192 + 80 * t : 272 + 80 * t]

                @pl.when(f != 1)
                def _():
                    gout[240 * cc + 80 * j : 240 * cc + 80 * j + 80, lanes] = part

                @pl.when(f == 1)
                def _():
                    a, b = 144 * cc + 48 * j, 288 + 96 * cc + 32 * j
                    gout[a : a + 48, lanes] = part[:48]
                    gout[b : b + 32, lanes] = part[48:]
    total = jnp.sum(w_in[...].astype(F32) * gin[...], axis=1, keepdims=True)
    gln[...] = jnp.transpose(jnp.broadcast_to(total, (96, 128)))[0:1, :] / ln[...]
    both = [vec_a[r : r + 1, :] + vec_b[r : r + 1, :] for r in range(8)]
    ob = jnp.concatenate(both[:6], axis=1)
    qs = both[6][:, :HD] + both[6][:, HD:]
    ks = both[7][:, :HD] + both[7][:, HD:]
    parts = {}
    for cc in range(2):
        vec = jnp.where(c == cc, vec_a[...], vec_b[...])
        for j in range(3):
            m = jnp.concatenate([vec[r : r + 1] for r in range(8 + 4 * j, 12 + 4 * j)], axis=1)
            done = 0
            for u, n in unit_ranges(cc, j):
                parts[u] = m[:, done : done + n]
                done += n
    mb = jnp.concatenate([parts[u] for u in sorted(parts)], axis=1)
    for ff in range(8):

        @pl.when(f == ff)
        def _():
            gob[...] = ob[:, 96 * ff : 96 * ff + 96]
            gqs[...] = qs[:, 8 * ff : 8 * ff + 8]
            gks[...] = ks[:, 8 * ff : 8 * ff + 8]
            gmb[...] = mb[:, 384 * ff : 384 * ff + 384]


def final(place, w_in, ln, own, other, after=()):
    sds = jax.ShapeDtypeStruct
    outs = (sds((96, 7 * D), F32), sds((480, D), F32), sds((1, 96), F32), sds((1, 8), F32), sds((1, 8), F32),
            sds((1, 384), F32), sds((1, 96), F32))
    return call(final_body, outs, [], (place, w_in, ln, *own, *other), [SCALARS] + [ANYWHERE] * 12, cost=(0, 10**7), after=after)


def routes():
    places = [(x, c, z, y) for x in range(2) for c in range(2) for z in range(4) for y in range(2)]
    number = lambda x, c, z, y: (x * 2 + c) * 8 + z * 2 + y
    pairs = lambda move: [(number(*p), number(*move(*p))) for p in places]
    out = {
        "core": pairs(lambda x, c, z, y: (x, 1 - c, z, y)),
        "x": pairs(lambda x, c, z, y: (1 - x, c, z, y)),
        "y": pairs(lambda x, c, z, y: (x, c, z, 1 - y)),
        "z1": pairs(lambda x, c, z, y: (x, c, z ^ 1, y)),
        "z2": pairs(lambda x, c, z, y: (x, c, z ^ 2, y)),
    }
    at = lambda n: (n % 8) // 2
    out["z2_up"] = [(a, b) for a, b in out["z2"] if at(a) == 0]
    out["z1_up"] = [(a, b) for a, b in out["z1"] if at(a) % 2 == 0]
    return out


def per_device_paired(
    tokens, lengths, assign, w_in, w_out, ln_scale, q_scale, k_scale, mlp_bias, out_bias, cotangent
):
    way = routes()
    go = lambda v, name: lax.ppermute(v, ("rep", "fsdp"), way[name])
    rep, f = lax.axis_index("rep"), lax.axis_index("fsdp")
    c, y, z = rep % 2, f % 2, f // 2
    cap = tokens.shape[0]
    device = rep * 8 + f
    place = jnp.stack([c, f, y, z, device, device + 8 - 16 * c, rep // 2]).astype(jnp.int32)

    late = lambda v, tick: v if tick is None else v + tick[0].astype(v.dtype)
    first = lambda piece, tick=None: jnp.stack([piece, late(go(piece, "z2"), tick)])
    second = lambda two, tick=None: jnp.concatenate([two, late(go(two, "z1"), tick)])
    third = lambda four: (four, go(four, "y"))
    vectors = (v.reshape(1, -1) for v in (ln_scale, q_scale, k_scale, mlp_bias, out_bias))
    info, a, wo = plan(place, lengths, assign, w_in, w_out, *vectors)
    a_b, wo_b = go(a, "z2"), go(wo, "z2_up")
    wo = jnp.where(z == 0, wo, wo_b)
    near = jnp.concatenate([a, a_b, wo])
    own, gob, tick = prepare(info, tokens, cotangent, (near,))
    far = late(go(near, "z1"), tick)
    b, m, own = split(place, w_in, w_out, own, (far,))
    b = first(b)
    wo = jnp.where(z % 2 == 0, wo, far[608:])
    near = jnp.concatenate([near[:608], far[:608], wo])
    vectors = third(near[:PARTS].reshape(4, 304, 128)[:, 288:])
    other = go(own, "core")
    far = go(near, "y")
    b = second(b)
    m = first(m)
    nrm, cot, ln, ob, gain, mb, tick = combine(info, place, own, other, *vectors)
    far = late(far, tick)
    wo_a, wo_b = head_rows(place, near, far)
    wo_b = go(wo_b, "core")

    def heads(p, g, dws, after):
        return attention(info, place, nrm, cot, *g, wo_a, wo_b, gain, p, dws, after)

    *a0, tick = heads(0, (near, far), (), (b, m))
    b = third(b)
    b = b[0], late(b[1], tick)
    m = second(m, tick)
    *a1, tick = heads(1, b, (), (m,))
    near, far = third(m)
    cross = jnp.concatenate([near[:, :, THIRD:], late(far[:, :, THIRD:], tick)])
    *a2, tick = heads(2, b, (a0[6], a1[6]), (cross,))
    cross = go(cross, "x")
    att, dqkv, ws, wos, dwos, dgs = zip(a0[:6], a1[:6], a2[:6])
    g_h = a2[6:]
    dwo = jnp.concatenate(dwos)
    recv = go(lax.dynamic_slice_in_dim(dwo, 240 - 144 * c, 144, 0), "core")
    slots = jnp.where(c == 0, jnp.concatenate([dwo[:240], recv]), jnp.concatenate([recv, dwo[:96], dwo[240:]]))

    def hidden(j, after):
        return mlp(info, place, nrm, cot, near, far, cross, mb, slots, j, after)

    step_y = lambda g: (g[0], go(g[1], "y"), "halves")
    step_z1 = lambda g: (g[0], go(g[1], "z1"), "halves")
    step_z2 = lambda g: (g[0], go(g[1], "z2"), "whole")
    step_x = lambda g: (g, go(g, "x"), "float")
    step_v = lambda v, name: (v, go(v, name), "float")

    *h0, tick = hidden(0, ())
    (g_h,) = adds([step_y(g_h)], (tick,))
    *h1, tick = hidden(1, (*g_h, h0[0]))
    g_h, g_0 = adds([step_z1(g_h), step_y(h0[4:6])], (tick,))
    *h2, tick = hidden(2, (*g_h, *g_0, h1[0]))
    act, gm, wins, wouts, _, _, dbs = zip(h0, h1, h2)

    vec = jnp.concatenate([gob.reshape(6, 128), sum(dgs).reshape(2, 128), *(db.reshape(4, 128) for db in dbs), jnp.zeros((4, 128), F32)])

    g_h, g_0, g_1 = adds([step_z2(g_h), step_z1(g_0), step_y(h1[4:6])], (tick,))
    part, away, tick = sums(info, (*att, *act), (*wos, *wouts), False, (g_h, *g_0, *g_1))
    away = go(away, "core")
    g_h, g_0, g_1, g_2, vec = adds([step_x(g_h), step_z2(g_0), step_z1(g_1), step_y(h2[4:6]), step_v(vec, "x")], (tick,))
    part_b, away_b, tick = sums(info, (*dqkv, *gm), (*ws, *wins), True, (g_h, g_0, *g_1, *g_2, vec))
    away_b = go(away_b, "core")
    g_0, g_1, g_2, vec = adds([step_x(g_0), step_z2(g_1), step_z1(g_2), step_v(vec, "y")], (tick,))
    output, tick = last_rows(output_body, cap, (info, own, part, away, ob), (g_0, g_1, *g_2, vec))
    g_1, g_2, vec = adds([step_x(g_1), step_z2(g_2), step_v(vec, "z1")], (tick,))
    grad_tokens, tick = last_rows(gradient_body, cap, (info, own, part_b, away_b, ln), (g_1, g_2, vec))
    g_2, vec = adds([step_x(g_2), step_v(vec, "z2")], (tick,))

    grads = (g_h, g_0, g_1, g_2)
    grads = (*grads, vec)
    g_win, g_wout, *small = final(place, w_in, ln_scale.astype(F32).reshape(1, 96), grads, [go(g, "core") for g in grads], (output, grad_tokens))
    return (output, grad_tokens, g_win, g_wout, *(g.reshape(-1) for g in small))


HEADS = 12
epsilon = 1e-06


def layer_norm(values, weight_gain):
    center = values - jnp.mean(values, axis=-1, keepdims=True)
    spread = jnp.mean(center * center, axis=-1, keepdims=True)
    return center * lax.rsqrt(spread + epsilon) * weight_gain


def layout(lengths, assign, device, row_count):
    own = assign == device
    own_sizes = jnp.where(own, lengths, 0)
    own_ends = jnp.cumsum(own_sizes)
    own_starts = own_ends - own_sizes
    position = lax.broadcasted_iota(jnp.int32, (row_count, lengths.shape[0]), 0)
    number = lax.broadcasted_iota(jnp.int32, (row_count, lengths.shape[0]), 1)
    inside = (position >= own_starts[None, :]) & (position < own_ends[None, :])
    filled = jnp.any(inside, axis=1)
    segment = jnp.sum(jnp.where(inside, number, 0), axis=1)
    return (jnp.where(filled, segment, -1), filled)


def contract_rows(left, right):
    return lax.dot_general(
        left, right, (((0,), (0,)), ((), ())), preferred_element_type=jnp.float32
    )


def contract_cols(left, right):
    return lax.dot_general(
        left, right, (((1,), (1,)), ((), ())), preferred_element_type=jnp.float32
    )


def per_device(
    tokens, lengths, assign, w_in, w_out, ln_scale, q_scale, k_scale, mlp_bias, out_bias, cotangent
):
    row_count = tokens.shape[0]
    head_dim = HD
    head_count = HEADS
    width = head_dim * head_count
    factor = head_dim ** (-0.5)
    device = lax.axis_index("rep") * lax.axis_size("fsdp") + lax.axis_index("fsdp")
    segment, filled = layout(lengths, assign, device, row_count)
    allowed = segment[:, None] == segment[None, :]
    params = (w_in, w_out, ln_scale, q_scale, k_scale, mlp_bias, out_bias)
    full = (
        lax.all_gather(params[0], "fsdp", axis=0, tiled=True),
        lax.all_gather(params[1], "fsdp", axis=0, tiled=True),
        lax.all_gather(params[2], "fsdp", axis=0, tiled=True),
        lax.all_gather(params[3], "fsdp", axis=0, tiled=True),
        lax.all_gather(params[4], "fsdp", axis=0, tiled=True),
        lax.all_gather(params[5], "fsdp", axis=0, tiled=True),
        lax.all_gather(params[6], "fsdp", axis=0, tiled=True),
    )
    win_full, wout_full = (full[0], full[1])
    small = [arr.astype(jnp.float32) for arr in full[2:]]
    ln_full, qs_full, ks_full, mb_full, ob_full = small
    inputs = tokens.astype(jnp.float32)
    normed_f, ln_pull = jax.vjp(layer_norm, inputs, ln_full)
    normed = normed_f.astype(jnp.bfloat16)
    joined = jnp.dot(normed, win_full, preferred_element_type=jnp.float32)
    q_pre = joined[:, :width].reshape(row_count, head_count, head_dim)
    k_pre = joined[:, width : 2 * width].reshape(row_count, head_count, head_dim)
    values = joined[:, 2 * width : 3 * width].astype(jnp.bfloat16)
    hidden_pre = joined[:, 3 * width :]
    q_norm, q_pull = jax.vjp(layer_norm, q_pre, qs_full)
    k_norm, k_pull = jax.vjp(layer_norm, k_pre, ks_full)
    queries = q_norm.reshape(row_count, width).astype(jnp.bfloat16)
    keys_all = k_norm.reshape(row_count, width).astype(jnp.bfloat16)

    def head_slice(array, head_index):
        return lax.dynamic_slice_in_dim(array, head_index * head_dim, head_dim, 1)

    def head_scores(head_index):
        raw = (
            contract_cols(head_slice(queries, head_index), head_slice(keys_all, head_index))
            * factor
        )
        return jnp.where(allowed, raw, -1e30)

    def head_forward(head_index):
        scores = head_scores(head_index)
        top = jnp.max(scores, axis=1, keepdims=True)
        expon = jnp.exp(scores - top)
        total = jnp.sum(expon, axis=1, keepdims=True)
        probs = (expon / total).astype(jnp.bfloat16)
        head_out = jnp.dot(
            probs, head_slice(values, head_index), preferred_element_type=jnp.float32
        )
        return (head_out, (top + jnp.log(total))[:, 0])

    head_outs, log_totals = lax.map(head_forward, jnp.arange(head_count))
    attended = jnp.transpose(head_outs, (1, 0, 2)).reshape(row_count, width)
    activated, gelu_pull = jax.vjp(lambda pre, bias: jax.nn.gelu(pre + bias), hidden_pre, mb_full)
    merged = jnp.concatenate([attended, activated], axis=1).astype(jnp.bfloat16)
    result = jnp.dot(merged, wout_full, preferred_element_type=jnp.float32) + ob_full
    output = jnp.where(filled[:, None], inputs + result, 0.0).astype(jnp.bfloat16)
    back = (
        lax.all_gather(params[0], "fsdp", axis=0, tiled=True),
        lax.all_gather(params[1], "fsdp", axis=0, tiled=True),
        lax.all_gather(params[2], "fsdp", axis=0, tiled=True),
        lax.all_gather(params[3], "fsdp", axis=0, tiled=True),
        lax.all_gather(params[4], "fsdp", axis=0, tiled=True),
        lax.all_gather(params[5], "fsdp", axis=0, tiled=True),
        lax.all_gather(params[6], "fsdp", axis=0, tiled=True),
    )
    win_back, wout_back = (back[0], back[1])
    grad_rows = jnp.where(filled[:, None], cotangent.astype(jnp.float32), 0.0)
    grad_low = grad_rows.astype(jnp.bfloat16)
    grad_ob = jnp.sum(grad_rows, axis=0)
    grad_wout = contract_rows(merged, grad_low)
    grad_merged = contract_cols(grad_low, wout_back)
    grad_attended = grad_merged[:, :width].astype(jnp.bfloat16)
    grad_m, grad_mb = gelu_pull(grad_merged[:, width:])

    def head_backward(head_index):
        scores = head_scores(head_index)
        probs_full = jnp.exp(scores - log_totals[head_index][:, None])
        probs = probs_full.astype(jnp.bfloat16)
        grad_head = head_slice(grad_attended, head_index)
        grad_probs = contract_cols(grad_head, head_slice(values, head_index))
        inner = jnp.sum(probs_full * grad_probs, axis=1, keepdims=True)
        grad_scores = (probs_full * (grad_probs - inner)).astype(jnp.bfloat16)
        grad_q = (
            jnp.dot(
                grad_scores, head_slice(keys_all, head_index), preferred_element_type=jnp.float32
            )
            * factor
        )
        grad_k = contract_rows(grad_scores, head_slice(queries, head_index)) * factor
        grad_v = contract_rows(probs, grad_head)
        return (grad_q, grad_k, grad_v)

    grad_qh, grad_kh, grad_vh = lax.map(head_backward, jnp.arange(head_count))
    grad_qn = jnp.transpose(grad_qh, (1, 0, 2))
    grad_kn = jnp.transpose(grad_kh, (1, 0, 2))
    grad_values = jnp.transpose(grad_vh, (1, 0, 2)).reshape(row_count, width)
    grad_q_pre, grad_qs = q_pull(grad_qn)
    grad_k_pre, grad_ks = k_pull(grad_kn)
    grad_joined = jnp.concatenate(
        [
            grad_q_pre.reshape(row_count, width),
            grad_k_pre.reshape(row_count, width),
            grad_values,
            grad_m,
        ],
        axis=1,
    ).astype(jnp.bfloat16)
    grad_win = contract_rows(normed, grad_joined)
    grad_normed = contract_cols(grad_joined, win_back)
    grad_x_norm, grad_ln = ln_pull(grad_normed)
    grad_tokens = (grad_rows + grad_x_norm).astype(jnp.bfloat16)
    grads = (grad_win, grad_wout, grad_ln, grad_qs, grad_ks, grad_mb, grad_ob)
    shares = (
        lax.psum_scatter(grads[0], "fsdp", scatter_dimension=0, tiled=True),
        lax.psum_scatter(grads[1], "fsdp", scatter_dimension=0, tiled=True),
        lax.psum_scatter(grads[2], "fsdp", scatter_dimension=0, tiled=True),
        lax.psum_scatter(grads[3], "fsdp", scatter_dimension=0, tiled=True),
        lax.psum_scatter(grads[4], "fsdp", scatter_dimension=0, tiled=True),
        lax.psum_scatter(grads[5], "fsdp", scatter_dimension=0, tiled=True),
        lax.psum_scatter(grads[6], "fsdp", scatter_dimension=0, tiled=True),
    )
    shares = lax.psum(
        (shares[0], shares[1], shares[2], shares[3], shares[4], shares[5], shares[6]), "rep"
    )
    return (
        output,
        grad_tokens,
        shares[0],
        shares[1],
        shares[2],
        shares[3],
        shares[4],
        shares[5],
        shares[6],
    )


def solution(mesh):
    in_specs = (
        P(("rep", "fsdp"), None),
        P(),
        P(),
        P("fsdp", None),
        P("fsdp", None),
        P("fsdp"),
        P("fsdp"),
        P("fsdp"),
        P("fsdp"),
        P("fsdp"),
        P(("rep", "fsdp"), None),
    )
    out_specs = (
        P(("rep", "fsdp"), None),
        P(("rep", "fsdp"), None),
        P("fsdp", None),
        P("fsdp", None),
        P("fsdp"),
        P("fsdp"),
        P("fsdp"),
        P("fsdp"),
        P("fsdp"),
    )
    paired = dict(mesh.shape) == {"rep": 4, "fsdp": 8}
    return jax.shard_map(
        per_device_paired if paired else per_device, mesh=mesh, in_specs=in_specs, out_specs=out_specs, check_vma=False
    )
```

```python
import functools

import jax
import jax.numpy as jnp
from jax import lax
from jax.experimental import pallas as pl
from jax.experimental.pallas import tpu as pltpu
from jax.sharding import PartitionSpec as P

D = 768
HD = 64
SMALL = 196
BIG = 1024
BLK = 208
CAN = 7 * BLK
ROWS = 3072
ROOM = 3584
RB = 512
NRB = ROWS // RB
U = 512
EPS = 1e-06
BF = jnp.bfloat16
F32 = jnp.float32
VMEM_MIB = 34
ANYWHERE = pl.BlockSpec(memory_space=pltpu.VMEM)
TICK = jax.ShapeDtypeStruct((1,), F32)
SCALARS = pl.BlockSpec(memory_space=pltpu.SMEM)


def dot_nn(a, b):
    return lax.dot_general(a, b, (((1,), (0,)), ((), ())), preferred_element_type=F32)


def dot_nt(a, b):
    return lax.dot_general(a, b, (((1,), (1,)), ((), ())), preferred_element_type=F32)


def dot_tn(a, b):
    return lax.dot_general(a, b, (((0,), (0,)), ((), ())), preferred_element_type=F32)


def two_parts(x):
    hi = x.astype(BF)
    return hi, (x - hi.astype(F32)).astype(BF)


def call(body, out_shape, scratch, args, in_specs, out_specs=None, grid=None, prefetch=0, cost=None, after=(), tick=False, alias=None, vmem=VMEM_MIB):
    if after:
        inner, n, skip = body, len(args), len(after)

        def body(*refs):
            inner(*refs[:n], *refs[n + skip :])

        args = (*args, *after)
        in_specs = [*in_specs] + [pl.BlockSpec(memory_space=pl.ANY)] * skip
    params = pltpu.CompilerParams(vmem_limit_bytes=vmem * 2**20)
    if out_specs is None:
        out_specs = jax.tree.map(lambda _: ANYWHERE, out_shape)
    if tick:
        many = isinstance(out_shape, tuple)
        out_shape = (*out_shape, TICK) if many else (out_shape, TICK)
        out_specs = (*out_specs, SCALARS) if many else (out_specs, SCALARS)
        untold, place = body, len(args) + len(out_shape) - 1

        def body(*refs):
            refs[place][0] = jnp.float32(0)
            untold(*refs[:place], *refs[place + 1 :])

    spec = pltpu.PrefetchScalarGridSpec(
        num_scalar_prefetch=prefetch,
        grid=grid or (),
        in_specs=in_specs,
        out_specs=out_specs,
        scratch_shapes=scratch,
    )
    estimate = None if cost is None else pl.CostEstimate(flops=20 * cost[0], bytes_accessed=20 * cost[1], transcendentals=0)
    return pl.pallas_call(body, grid_spec=spec, out_shape=out_shape, compiler_params=params, cost_estimate=estimate, input_output_aliases=alias or {})(*args)


NB, BLOCKS_A, LARGE_A, SMALL_A, BASE, BLOCKS_B, LARGE_B, SMALL_B, BEFORE = range(9)
CORE, FSDP, Y, Z, SELF, MATE, X = range(7)


def unit_ranges(c, j):
    first = [(96 * c + 32 * j, 32)]
    return first + [(192 + 480 * s + 240 * c + 80 * j, 80) for s in range(6)]


def plan_body(place, lengths, assign, w_in, w_out, ln, qs, ks, mb, ob, info, a, b, wo):
    def count(i, carry):
        before, small_a, large_a, small_b, large_b = carry
        large = (lengths[i] == BIG).astype(jnp.int32)
        me = (assign[i] == place[SELF]).astype(jnp.int32)
        mate = (assign[i] == place[MATE]).astype(jnp.int32)
        before = jnp.where(me * large == 1, small_a, before)
        return before, small_a + me * (1 - large), large_a + me * large, small_b + mate * (1 - large), large_b + mate * large

    zero = jnp.int32(0)
    before, small_a, large_a, small_b, large_b = lax.fori_loop(0, lengths.shape[0], count, (zero,) * 5)
    blocks_a = jnp.where(large_a > 0, 7, small_a)
    blocks_b = jnp.where(large_b > 0, 7, small_b)
    info[NB] = (BLK * (blocks_a + blocks_b) + RB - 1) // RB
    info[BLOCKS_A], info[LARGE_A], info[SMALL_A] = blocks_a, large_a, small_a
    info[BASE] = BLK * blocks_a
    info[BLOCKS_B], info[LARGE_B], info[SMALL_B] = blocks_b, large_b, small_b
    info[BEFORE] = jnp.where(large_a > 0, before, small_a)

    a[288:304, :] = jnp.zeros((16, 128), BF)
    a[288:289, :96] = ln[...]
    a[289:290, :8] = qs[...]
    a[290:291, :8] = ks[...]
    a[291:292, :96] = ob[...]
    for n in range(3):
        a[292 + n : 293 + n, :] = mb[:, 128 * n : 128 * n + 128]
    for cc in range(2):

        @pl.when(place[CORE] == cc)
        def _():
            for n in range(3):
                at = D * n + 384 * cc
                a[96 * n : 96 * n + 96, :] = w_in[:, at : at + 128]
                for p in range(2):
                    row = 288 * p + 96 * n
                    b[row : row + 96, :] = w_in[:, at + 128 * p + 128 : at + 128 * p + 256]
                wo[480 * n : 480 * n + 480, :] = w_out[:, 384 * cc + 128 * n : 384 * cc + 128 * n + 128]


def plan(place, lengths, assign, w_in, w_out, *small):
    sds = jax.ShapeDtypeStruct
    outs = (sds((16,), jnp.int32), sds((304, 128), BF), sds((576, 128), BF), sds((1440, 128), BF))
    return call(plan_body, outs, [], (place, lengths, assign, w_in, w_out, *small), [SCALARS] * 3 + [ANYWHERE] * 7,
                (SCALARS,) + (ANYWHERE,) * 3, vmem=60, cost=(0, 2 * 10**6))


def split_body(place, w_in, w_out, own, m, own_o):
    c, f = place[CORE], place[FSDP]
    for cc in range(2):

        @pl.when(c == cc)
        def _():
            for j in range(3):
                cols = [w_in[:, 3 * D + u : 3 * D + u + n] for u, n in unit_ranges(cc, j)]
                half = jnp.concatenate(cols, axis=1)
                m[j, 0:96, :] = half[:, :256]
                m[j, 96:192, :] = half[:, 256:]
                for t in range(3):
                    lanes = slice(256 * t, 256 * t + 256)
                    at = 192 + 80 * t

                    @pl.when(f != 1)
                    def _():
                        m[j, at : at + 80, :] = w_out[240 * cc + 80 * j : 240 * cc + 80 * j + 80, lanes]

                    @pl.when(f == 1)
                    def _():
                        a, b = 144 * cc + 48 * j, 288 + 96 * cc + 32 * j
                        m[j, at : at + 48, :] = w_out[a : a + 48, lanes]
                        m[j, at + 48 : at + 80, :] = w_out[b : b + 32, lanes]


def split(place, w_in, w_out, own, after):
    sds = jax.ShapeDtypeStruct
    outs = (sds((3, 432, 256), BF), sds(own.shape, BF))
    hbm = pl.BlockSpec(memory_space=pl.ANY)
    return call(split_body, outs, [], (place, w_in, w_out, own), [SCALARS] + [ANYWHERE] * 2 + [hbm], (ANYWHERE, hbm),
                cost=(0, 4 * 10**6), after=after, alias={3: 1})


def slot_of(place, f):
    dz = place[Z] ^ (f >> 1)
    return place[Y] ^ (f & 1), ((dz & 1) << 1) | (dz >> 1)


def taken(place, near, far, f, rows):
    side, at = slot_of(place, f)
    return jnp.where(side == 0, near[at, rows, :], far[at, rows, :])


def put(place, near, far, f, fill):
    side, at = slot_of(place, f)

    @pl.when(side == 0)
    def _():
        fill(near.at[at])

    @pl.when(side != 0)
    def _():
        fill(far.at[at])


def each_image(info, move):
    start = SMALL * info[BEFORE]

    @pl.when(info[LARGE_A] == 1)
    def _():
        for t in range(5):
            move(BLK * t, start + BLK * t, min(BLK, BIG - BLK * t))

    def small(i, carry):
        large = BIG * info[LARGE_A]
        move(pl.multiple_of(large + BLK * i, 16), SMALL * i + jnp.where(i >= info[BEFORE], large, 0), SMALL)
        return carry

    lax.fori_loop(0, info[SMALL_A], small, 0)


WINDOW = BLK + 16


def window_of(slot):
    first = (slot // 16) * 16
    return pl.ds(pl.multiple_of(first, 16), WINDOW), slot - first


def prepare_body(info, tokens, cot, out, gob_o, pad_x, pad_g):
    cap = tokens.shape[0]
    for pad, held in ((pad_x, tokens), (pad_g, cot)):
        pad[0:cap, :] = held[...]
        pad[cap:, :] = jnp.zeros((pad.shape[0] - cap, D), BF)
    out[...] = jnp.zeros_like(out)
    gob_o[...] = jnp.zeros_like(gob_o)
    apart = lax.broadcasted_iota(jnp.int32, (BLK, WINDOW), 1) - lax.broadcasted_iota(jnp.int32, (BLK, WINDOW), 0)
    row = lax.broadcasted_iota(jnp.int32, (BLK, WINDOW), 0)

    def move(to, slot, n):
        window, shift = window_of(slot)
        pick = ((apart == shift) & (row < n)).astype(BF)
        rows = pl.ds(to, BLK)
        g = dot_nn(pick, pad_g[window, :])
        out[0, rows, :] = dot_nn(pick, pad_x[window, :]).astype(BF)
        out[1, rows, :] = g.astype(BF)
        gob_o[...] += jnp.sum(g, axis=0, keepdims=True)

    each_image(info, move)


def prepare(info, tokens, cot, after):
    sds = jax.ShapeDtypeStruct
    pad = pltpu.VMEM((CAN + 16, D), BF)
    return call(prepare_body, (sds((2, CAN, D), BF), sds((1, D), F32)), [pad, pad], (info, tokens, cot),
                [SCALARS] + [ANYWHERE] * 2, vmem=60, cost=(10**9, 9 * 10**6), after=after, tick=True)


def combine_body(info, place, own, other, near, far, nrm, cot, ln_o, ob_o, gain_o, mb_o):
    base = pl.multiple_of(info[BASE], 16)
    small = [taken(place, near, far, f, slice(0, 16)).astype(F32) for f in range(8)]
    ln = jnp.concatenate([s[0:1, :96] for s in small], axis=1)
    ln_o[...] = ln
    ob_o[...] = jnp.concatenate([s[3:4, :96] for s in small], axis=1)
    gain_o[...] = jnp.concatenate(([s[1:2, :8] for s in small] * 2) + ([s[2:3, :8] for s in small] * 2), axis=1)
    mb = jnp.concatenate([s[4 + n : 5 + n, :] for s in small for n in range(3)], axis=1)
    for j in range(3):
        rows = [jnp.concatenate([mb[:, u : u + n] for u, n in unit_ranges(cc, j)], axis=1) for cc in range(2)]
        mb_o[j : j + 1, :] = jnp.where(place[CORE] == 0, rows[0], rows[1])

    def copy(source, i, to):
        rows = pl.ds(pl.multiple_of(i * BLK, 16), BLK)
        to = pl.ds(pl.multiple_of(to, 16), BLK)
        v = source[0, rows, :].astype(F32)
        center = v - jnp.mean(v, axis=1, keepdims=True)
        spread = jnp.mean(center * center, axis=1, keepdims=True)
        nrm[to, :] = (center * lax.rsqrt(spread + EPS) * ln).astype(BF)
        cot[to, :] = source[1, rows, :]

    def from_own(i, carry):
        copy(own, i, i * BLK)
        return carry

    def from_other(i, carry):
        copy(other, i, base + i * BLK)
        return carry

    lax.fori_loop(0, info[BLOCKS_A], from_own, 0)
    lax.fori_loop(0, info[BLOCKS_B], from_other, 0)
    end = pl.ds(pl.multiple_of(base + info[BLOCKS_B] * BLK, 16), RB)
    nrm[end, :] = jnp.zeros((RB, D), BF)
    cot[end, :] = jnp.zeros((RB, D), BF)


def combine(info, place, own, other, near, far, after=()):
    sds = jax.ShapeDtypeStruct
    outs = (sds((ROOM, D), BF),) * 2 + (sds((1, D), F32),) * 2 + (sds((1, 256), F32), sds((3, U), F32))
    return call(combine_body, outs, [], (info, place, own, other, near, far), [SCALARS] * 2 + [ANYWHERE] * 4,
                cost=(0, 18 * 10**6), after=after, tick=True)


def rows_body(info, x_h, a_h, b_h, vector, out, x, a, b, held, pad, sems, *, gradient):
    moves = []
    for i in range(CAN // BLK):
        rows = pl.ds(i * BLK, BLK)
        pairs = [(x_h.at[0, rows, :], x.at[0, rows, :]), (a_h.at[rows, :], a.at[rows, :]), (b_h.at[rows, :], b.at[rows, :])]
        if gradient:
            pairs.append((x_h.at[1, rows, :], x.at[1, rows, :]))
        moves.append([pltpu.make_async_copy(p, q, sems.at[n, i]) for n, (p, q) in enumerate(pairs)])
        for move in moves[-1]:
            move.start()
    pad[...] = jnp.zeros_like(pad)
    for i in range(CAN // BLK):
        for move in moves[i]:
            move.wait()
        rows = pl.ds(i * BLK, BLK)
        v = x[0, rows, :].astype(F32)
        total = a[rows, :].astype(F32) + b[rows, :].astype(F32)
        if gradient:
            center = v - jnp.mean(v, axis=1, keepdims=True)
            r = lax.rsqrt(jnp.mean(center * center, axis=1, keepdims=True) + EPS)
            xh = center * r
            g = total * vector[...]
            gx = r * (g - jnp.mean(g, axis=1, keepdims=True) - xh * jnp.mean(g * xh, axis=1, keepdims=True))
            held[rows, :] = (x[1, rows, :].astype(F32) + gx).astype(BF)
        else:
            held[rows, :] = (v + (total + vector[...])).astype(BF)
    apart = lax.broadcasted_iota(jnp.int32, (WINDOW, BLK), 0) - lax.broadcasted_iota(jnp.int32, (WINDOW, BLK), 1)
    col = lax.broadcasted_iota(jnp.int32, (WINDOW, BLK), 1)

    def move(at, slot, n):
        window, shift = window_of(slot)
        pick = ((apart == shift) & (col < n)).astype(BF)
        pad[window, :] += dot_nn(pick, held[pl.ds(at, BLK), :]).astype(BF)

    each_image(info, move)
    out[...] = pad[: out.shape[0], :]


def last_rows(info, x, a, b, vector, cap, gradient, after=()):
    v = pltpu.VMEM
    scratch = [v((2, CAN, D), BF), v((CAN, D), BF), v((CAN, D), BF), v((CAN, D), BF), v((CAN + 16, D), BF),
               pltpu.SemaphoreType.DMA((4, CAN // BLK))]
    hbm = pl.BlockSpec(memory_space=pl.ANY)
    return call(functools.partial(rows_body, gradient=gradient), jax.ShapeDtypeStruct((cap, D), BF), scratch, (info, x, a, b, vector),
                [SCALARS] + [hbm] * 3 + [ANYWHERE], cost=(4 * 10**9, 12 * 10**6), after=after, tick=True)


def head_rows_body(place, a, b, mine, theirs):
    for yy in range(2):

        @pl.when(place[Y] == yy)
        def _():
            lo, hi = (a, b) if yy == 0 else (b, a)
            for cc in range(2):

                @pl.when(place[CORE] == cc)
                def _():
                    first, second = (mine, theirs) if cc == 0 else (theirs, mine)
                    for n in range(3):
                        lanes = slice(128 * n, 128 * n + 128)
                        at = PARTS + 480 * n
                        first[:, lanes] = lo[at : at + 384, :]
                        second[0:96, lanes] = lo[at + 384 : at + 480, :]
                        second[96:384, lanes] = hi[at : at + 288, :]


def head_rows(place, a, b):
    sds = jax.ShapeDtypeStruct
    return call(head_rows_body, (sds((384, 384), BF),) * 2, [], (place, a, b), [SCALARS, ANYWHERE, ANYWHERE], cost=(0, 10**6))


PARTS = 4 * 304


def attention_body(info, place, nrm_h, cot_h, near, far, wo_a, wo_b, gain, *refs, pairs):
    refs = list(refs)
    last = len(pairs) > 1
    if last:
        dw_0, dwo_0, dg_0 = refs[:3]
        refs = refs[3:]
    att_o, dqkv_o, w_o, wo_o, dg_o, dwo_o = refs[:6]
    if last:
        dwo_send, near_o, far_o = refs[6:9]
        refs = refs[9:]
    else:
        dw_o = refs[6]
        refs = refs[7:]
    nrm, cot, sems, qa, kb, vv, qp, do, xh, rr, dqk, dv, dw, dwo, dws = refs
    step = pl.program_id(0)
    nb = info[NB]

    def incoming(i):
        rows = pl.ds(pl.multiple_of(i * RB, RB), RB)
        return (pltpu.make_async_copy(nrm_h.at[rows, :], nrm.at[rows, :], sems.at[0, i]),
                pltpu.make_async_copy(cot_h.at[rows, :], cot.at[rows, :], sems.at[1, i]))

    @pl.when(step == 0)
    def _():
        def begin(i, carry):
            for move in incoming(i):
                move.start()
            return carry

        lax.fori_loop(0, nb, begin, 0)
        if last:
            dg_o[...] = dg_0[...]
        else:
            dg_o[...] = jnp.zeros_like(dg_o)

    lane = lax.broadcasted_iota(jnp.int32, (1, 128), 1)
    first = lane < HD
    same = lax.broadcasted_iota(jnp.int32, (256, 256), 0) // HD == lax.broadcasted_iota(jnp.int32, (256, 256), 1) // HD
    mean_m = jnp.where(same, 1.0 / HD, 0.0).astype(BF)
    sum_m = jnp.where(same[:, :128] | same[:, 128:], 1.0, 0.0).astype(BF)
    c_exp = 1.4426950408889634 / 8.0

    for f in range(8):
        side, at = slot_of(place, f)
        if pairs[0] == 0:
            rows = pl.ds(pl.multiple_of(304 * at, 16), 288)
            piece = jnp.where(side == 0, near[rows, :], far[rows, :])
        else:
            rows = pl.ds(pl.multiple_of(288 * step, 16), 288)
            piece = jnp.where(side == 0, near[at, rows, :], far[at, rows, :])
        for n in range(3):
            w_o[96 * f : 96 * f + 96, 128 * n : 128 * n + 128] = piece[96 * n : 96 * n + 96]
    rows = pl.ds(pl.multiple_of(128 * (pairs[0] + step), 16), 128)
    mine, theirs = wo_a[rows, :], wo_b[rows, :]
    wo_o[:, :384] = jnp.where(place[CORE] == 0, mine, theirs)
    wo_o[:, 384:] = jnp.where(place[CORE] == 0, theirs, mine)

    def mean(x):
        return dot_nn(x.astype(BF), mean_m)

    def project(i, carry):
        @pl.when(step == 0)
        def _():
            for move in incoming(i):
                move.wait()

        rows = pl.ds(pl.multiple_of(i * RB, RB), RB)
        y = dot_nn(nrm[rows, :], w_o[...])
        qk, v = y[:, :256], y[:, 256:]
        center = qk - mean(qk)
        r = lax.rsqrt(mean(center * center) + EPS)
        x = center * r
        xh[rows, :] = x
        rr[rows, :] = r
        qk = (x * gain[...]).astype(BF)
        q = qk[:, :128]
        qp[rows, :] = q
        hi, lo = two_parts(q.astype(F32) * c_exp)
        hi, lo = hi.astype(F32), lo.astype(F32)
        qa[0, rows, :] = jnp.where(first, hi, pltpu.roll(lo, HD, 1)).astype(BF)
        qa[1, rows, :] = jnp.where(first, pltpu.roll(hi, HD, 1), lo).astype(BF)
        kf = qk[:, 128:].astype(F32)
        kr = pltpu.roll(kf, HD, 1)
        kb[0, rows, :] = jnp.where(first, kf, kr).astype(BF)
        kb[1, rows, :] = jnp.where(first, kr, kf).astype(BF)
        vv[0, rows, :] = jnp.where(first, v, 1.0).astype(BF)
        vv[1, rows, :] = jnp.where(first, 1.0, v).astype(BF)
        do[rows, :] = dot_nt(cot[rows, :], wo_o[...]).astype(BF)
        dqk[rows, :] = jnp.zeros((RB, 256), F32)
        dv[rows, :] = jnp.zeros((RB, 128), F32)
        att_o[rows, :] = jnp.zeros((RB, 128), BF)
        return carry

    lax.fori_loop(0, nb, project, 0)

    def blocks(items, masked, add):
        both = [(i, h) for i in range(len(items)) for h in range(2)]
        ql = [[qa[h, it[0], :] for h in range(2)] for it in items]
        kl = [[kb[h, it[1], :] for h in range(2)] for it in items]
        vl = [[vv[h, it[1], :] for h in range(2)] for it in items]
        grads = [do[it[0], :].astype(F32) for it in items]
        plain = [qp[it[0], :] for it in items]
        p, pb, xs = {}, {}, {}
        for i, h in both:
            e = jnp.exp2(dot_nt(ql[i][h], kl[i][h]))
            if masked:
                e = jnp.where(lax.broadcasted_iota(jnp.int32, e.shape, 1) < SMALL, e, 0.0)
            p[i, h] = e
            pb[i, h] = e.astype(BF)
        for i, h in both:
            xs[i, h] = dot_nn(pb[i, h], vl[i][h])
        outs, scaled, lefts = [], [], {}
        for i in range(len(items)):
            total = jnp.where(first, pltpu.roll(xs[i, 0], HD, 1), pltpu.roll(xs[i, 1], HD, 1))
            inverse = 1.0 / total
            out = jnp.where(first, xs[i, 0], xs[i, 1]) * inverse
            outs.append(out.astype(BF))
            hi, lo = two_parts(grads[i] * out)
            inner = dot_nn(jnp.concatenate([hi, lo], axis=1), sum_m) * inverse
            s = (grads[i] * inverse).astype(BF)
            scaled.append(s)
            sf = s.astype(F32)
            hi, lo = two_parts(inner)
            hi, lo = pltpu.roll(hi.astype(F32), HD, 1), pltpu.roll(lo.astype(F32), HD, 1)
            for h in range(2):
                own = first if h == 0 else jnp.logical_not(first)
                at = HD * (1 - h)
                side = jnp.where(lane == at, -hi, jnp.where(lane == at + 1, -lo, 0.0))
                lefts[i, h] = jnp.where(own, sf, side).astype(BF)
        ds = {}
        for i, h in both:
            ds[i, h] = (p[i, h] * dot_nt(lefts[i, h], vl[i][h])).astype(BF)
        dq = {t: dot_nn(ds[t], kl[t[0]][t[1]]) for t in both}
        turned = [(jnp.transpose(a.astype(F32)).astype(BF), jnp.transpose(b.astype(F32)).astype(BF)) for a, b in zip(plain, scaled)]
        dk = {(i, h): dot_nn(turned[i][0][HD * h : HD * h + HD], ds[i, h]) for i, h in both}
        dvs = {(i, h): dot_nn(turned[i][1][HD * h : HD * h + HD], pb[i, h]) for i, h in both}
        for i, (q_rows, k_rows) in enumerate(items):
            att_o[q_rows, :] = outs[i]
            dqk[q_rows, :128] = jnp.where(first, dq[i, 0], dq[i, 1])
            new_k = jnp.transpose(jnp.concatenate([dk[i, 0], dk[i, 1]], axis=0))
            new_v = jnp.transpose(jnp.concatenate([dvs[i, 0], dvs[i, 1]], axis=0))
            if add:
                dqk[k_rows, 128:] += new_k
                dv[k_rows, :] += new_v
            else:
                dqk[k_rows, 128:] = new_k
                dv[k_rows, :] = new_v

    count_a, count_b = info[SMALL_A], info[SMALL_B]

    def small_rows(i):
        row_a = BIG * info[LARGE_A] + BLK * i
        row_b = info[BASE] + BIG * info[LARGE_B] + BLK * (i - count_a)
        row = jnp.where(i < count_a, row_a, jnp.where(i < count_a + count_b, row_b, ROWS))
        return pl.ds(pl.multiple_of(row, 16), BLK)

    def smalls(i, carry):
        rows = [small_rows(3 * i + n) for n in range(3)]
        blocks([(r, r) for r in rows], True, False)
        return carry

    lax.fori_loop(0, (count_a + count_b + 2) // 3, smalls, 0)

    def large_block(i, carry):
        base = jnp.where(i < 2 * info[LARGE_A], 0, info[BASE])
        k_rows = pl.ds(pl.multiple_of(base, 16), BIG)
        blocks([(pl.ds(pl.multiple_of(base + (i & 1) * 512, 16), 512), k_rows)], False, True)
        return carry

    lax.fori_loop(0, 2 * (info[LARGE_A] + info[LARGE_B]), large_block, 0)

    dw[...] = jnp.zeros_like(dw)
    dwo[...] = jnp.zeros_like(dwo)

    def finish(i, carry):
        rows = pl.ds(pl.multiple_of(i * RB, RB), RB)
        g_out = dqk[rows, :] * 0.125
        x = xh[rows, :]
        dg_o[...] += jnp.sum(g_out * x, axis=0, keepdims=True)
        g = g_out * gain[...]
        g = rr[rows, :] * (g - mean(g) - x * mean(g * x))
        g = jnp.concatenate([g.astype(BF), dv[rows, :].astype(BF)], axis=1)
        dqkv_o[rows, :] = g
        dw[...] += dot_tn(g, nrm[rows, :])
        dwo[...] += dot_tn(att_o[rows, :], cot[rows, :])
        return carry

    lax.fori_loop(0, nb, finish, 0)
    if not last:
        dwo_o[...] = dwo[...].astype(BF)
        dw_o[...] = dw[...].astype(BF)
        return
    dwo_o[pl.ds(pl.multiple_of(128 + 128 * step, 16), 128), :] = dwo[...].astype(BF)

    @pl.when(step == 0)
    def _():
        dws[...] = dw[...]
        dwo_o[0:128, :] = dwo_0[...]

    @pl.when(step == len(pairs) - 1)
    def _():
        dwo_send[...] = jnp.where(place[CORE] == 0, dwo_o[240:384, :], dwo_o[96:240, :])
        full = [jnp.transpose(d).astype(BF) for d in (dw_0[...].astype(F32), dws[...], dw[...])]
        for f in range(8):

            def fill(ref, f=f):
                for q in range(3):
                    for n in range(3):
                        at = 288 * q + 96 * n
                        ref[at : at + 96, :] = full[q][96 * f : 96 * f + 96, 128 * n : 128 * n + 128]

            put(place, near_o, far_o, f, fill)


def attention(info, place, nrm, cot, near, far, wo_a, wo_b, gain, pairs, before=(), after=()):
    sds = jax.ShapeDtypeStruct
    bs = pl.BlockSpec
    n, more = len(pairs), ROWS + 256
    outs = [sds((n, more, 128), BF), sds((n, ROWS, 384), BF), sds((n, D, 384), BF), sds((n, 128, D), BF), sds((1, 256), F32)]
    by_pair = lambda p: (p, 0, 0)
    fixed = lambda a: bs(a.shape, lambda p: (0,) * len(a.shape))
    specs = [bs((None, *o.shape[1:]), by_pair) for o in outs[:4]] + [fixed(outs[4])]
    if n > 1:
        rest = [sds((384, D), BF), sds((144, D), BF), sds((4, 864, 128), BF), sds((4, 864, 128), BF)]
    else:
        rest = [sds((128, D), BF), sds((384, D), BF)]
    outs, specs = outs + rest, specs + [fixed(o) for o in rest]
    v = pltpu.VMEM
    scratch = [v((ROWS, D), BF)] * 2 + [pltpu.SemaphoreType.DMA((2, NRB))] + [v((2, more, 128), BF)] * 3 + [
        v((more, 128), BF)] * 2 + [v((ROWS, 256), F32)] * 2 + [v((more, 256), F32), v((more, 128), F32), v((384, D), F32), v((128, D), F32), v((384, D), F32)]
    hbm = bs(memory_space=pl.ANY)
    given = (near, far, wo_a, wo_b, gain, *before)
    return call(functools.partial(attention_body, pairs=pairs), tuple(outs), scratch, (info, place, nrm, cot, *given),
                [SCALARS] * 2 + [hbm] * 2 + [fixed(g) for g in given], tuple(specs), grid=(n,),
                cost=(n * 12 * 10**9, n * 14 * 10**6), after=after, tick=True, vmem=60)


def mlp_body(info, place, nrm_h, cot_h, near_a, near_b, far_a, far_b, mb, dwo, came, *refs, chunk):
    refs = list(refs)
    last = chunk == 2
    if last:
        gob, dg, db_0, db_1 = refs[:4]
        refs = refs[4:]
    act_h, gm_h, win_h, wout_h, near_o, far_o, db = refs[:7]
    nrm, cot, act, gm, win, wout, dwin, dwout, held, sems, out_sems, piece_sems, weight_sems = refs[7:]
    nb = info[NB]

    def incoming(i):
        rows = pl.ds(pl.multiple_of(i * RB, RB), RB)
        return (pltpu.make_async_copy(nrm_h.at[rows, :], nrm.at[rows, :], sems.at[0, i]),
                pltpu.make_async_copy(cot_h.at[rows, :], cot.at[rows, :], sems.at[1, i]))

    def outgoing(i):
        rows = pl.ds(pl.multiple_of(i * RB, RB), RB)
        return (pltpu.make_async_copy(act.at[rows, :], act_h.at[rows, :], out_sems.at[0, i]),
                pltpu.make_async_copy(gm.at[rows, :], gm_h.at[rows, :], out_sems.at[1, i]))

    def over(body):
        def step(i, carry):
            body(i)
            return carry

        lax.fori_loop(0, nb, step, 0)

    pieces = [pltpu.make_async_copy(p.at[:, chunk], held.at[pl.ds(2 * n, 2)], piece_sems.at[n])
              for n, p in enumerate((near_a, near_b, far_a, far_b))]
    weights = [pltpu.make_async_copy(win, win_h, weight_sems.at[0]), pltpu.make_async_copy(wout, wout_h, weight_sems.at[1])]
    for move in pieces:
        move.start()
    over(lambda i: [move.start() for move in incoming(i)])
    dwin[...] = jnp.zeros_like(dwin)
    dwout[...] = jnp.zeros_like(dwout)
    db[...] = jnp.zeros_like(db)
    for move in pieces:
        move.wait()
    for f in range(8):
        side, at = slot_of(place, f)
        piece = held[4 * side + at]
        for n in range(2):
            win[96 * f : 96 * f + 96, 256 * n : 256 * n + 256] = piece[96 * n : 96 * n + 96]
        for t in range(3):
            part = piece[192 + 80 * t : 272 + 80 * t]
            lanes = slice(256 * t, 256 * t + 256)
            if f == 1:
                wout[0:32, lanes] = part[48:]
            elif f > 1:
                wout[80 * f - 128 : 80 * f - 48, lanes] = part
    for move in weights:
        move.start()

    c0 = 0.7978845608028654
    c1 = 0.044715 * c0

    def step(i, carry):
        rows = pl.ds(pl.multiple_of(i * RB, RB), RB)
        for move in incoming(i):
            move.wait()
        pre = dot_nn(nrm[rows, :], win[...]) + mb[chunk : chunk + 1, :]
        ga = dot_nt(cot[rows, :], wout[...])
        sq = pre * pre
        t = jnp.tanh(pre * (c0 + c1 * sq))
        half = 0.5 * pre
        up = 1.0 + t
        act[rows, :] = (half * up).astype(BF)
        slope = 0.5 * up + half * (1.0 - t * t) * (c0 + 3.0 * c1 * sq)
        gmf = ga * slope
        gm[rows, :] = gmf.astype(BF)
        db[...] += jnp.sum(gmf, axis=0, keepdims=True)
        dwout[...] += dot_tn(act[rows, :], cot[rows, :])
        dwin[...] += dot_tn(gm[rows, :], nrm[rows, :])
        for move in outgoing(i):
            move.start()
        return carry

    lax.fori_loop(0, nb, step, 0)
    full = jnp.transpose(dwin[...]).astype(BF)
    core = place[CORE] == 0
    first, second = slice(80 * chunk, 80 * chunk + 80), slice(48 * chunk, 48 * chunk + 48)
    both = jnp.concatenate([came[...], dwo[0:96, :]])
    zero_rows = jnp.where(core, dwo[first, :], both[first])
    one_rows = jnp.where(core, came[second, :], dwo[240 + 48 * chunk : 288 + 48 * chunk, :])
    if last:
        ob = gob[...]
        qs = dg[:, :HD] + dg[:, HD : 2 * HD]
        ks = dg[:, 2 * HD : 3 * HD] + dg[:, 3 * HD :]
        parts = {}
        for j, units in enumerate((db_0[...], db_1[...], db[...])):
            for cc in range(2):
                own = jnp.where(place[CORE] == cc, units, 0.0)
                done = 0
                for u, n in unit_ranges(cc, j):
                    parts[u] = own[:, done : done + n]
                    done += n
        hidden = jnp.concatenate([parts[u] for u in sorted(parts)], axis=1)
    for f in range(8):

        def fill(ref, f=f):
            for n in range(2):
                ref[96 * n : 96 * n + 96, :] = full[96 * f : 96 * f + 96, 256 * n : 256 * n + 256]
            for t in range(3):
                lanes = slice(256 * t, 256 * t + 256)
                at = 192 + 80 * t
                if f == 0:
                    ref[at : at + 80, :] = zero_rows[:, lanes]
                elif f == 1:
                    ref[at : at + 48, :] = one_rows[:, lanes]
                    ref[at + 48 : at + 80, :] = dwout[0:32, lanes].astype(BF)
                else:
                    ref[at : at + 80, :] = dwout[80 * f - 128 : 80 * f - 48, lanes].astype(BF)
            if last:
                blank = lambda n: jnp.zeros((1, n), F32)
                rows = [hidden[:, 384 * f : 384 * f + 256],
                        jnp.concatenate([hidden[:, 384 * f + 256 : 384 * f + 384], ob[:, 96 * f : 96 * f + 96], blank(32)], axis=1),
                        jnp.concatenate([qs[:, 8 * f : 8 * f + 8], blank(120), ks[:, 8 * f : 8 * f + 8], blank(120)], axis=1)]
                ref[432:448, :] = jnp.concatenate([*rows, jnp.zeros((13, 256), F32)]).astype(BF)

        put(place, near_o, far_o, f, fill)
    for move in weights:
        move.wait()
    over(lambda i: [move.wait() for move in outgoing(i)])


def clamp(i, info, *_):
    return (jnp.minimum(i, info[NB] - 1), 0)


def whole(i, *_):
    return (0, 0)


def whole3(i, *_):
    return (0, 0, 0)


def mlp(info, place, nrm, cot, pieces, mb, dwo, came, vectors, chunk, after=()):
    sds = jax.ShapeDtypeStruct
    rows = 448 if chunk == 2 else 432
    outs = (sds((ROWS, U), BF), sds((ROWS, U), BF), sds((D, U), BF), sds((U, D), BF), sds((4, rows, 256), BF),
            sds((4, rows, 256), BF), sds((1, U), F32))
    hbm = pl.BlockSpec(memory_space=pl.ANY)
    v = pltpu.VMEM
    dma = pltpu.SemaphoreType.DMA
    scratch = [v((ROWS, D), BF)] * 2 + [v((ROWS, U), BF)] * 2 + [v((D, U), BF), v((U, D), BF), v((U, D), F32), v((U, D), F32),
               v((8, 432, 256), BF), dma((2, NRB)), dma((2, NRB)), dma((4,)), dma((2,))]
    given = (mb, dwo, came, *vectors)
    return call(functools.partial(mlp_body, chunk=chunk), outs, scratch, (info, place, nrm, cot, *pieces, *given),
                [SCALARS] * 2 + [hbm] * 6 + [ANYWHERE] * len(given), (hbm,) * 4 + (ANYWHERE,) * 3, vmem=60,
                cost=(10 * 10**9, 18 * 10**6), after=after, tick=True)


def sums_body(info, *refs, n, transposed):
    i = pl.program_id(0)
    lefts, rights, own, other, left, right, held, sems = refs[:n], refs[n : 2 * n], *refs[2 * n :]

    @pl.when(i == 0)
    def _():
        at = 0
        for b in rights:
            k = b.shape[1] if transposed else b.shape[0]
            if transposed:
                right[:, at : at + k] = b[...]
            else:
                right[at : at + k, :] = b[...]
            at += k

    @pl.when(i < info[NB])
    def _():
        at = 0
        for a in lefts:
            left[:, at : at + a.shape[1]] = a[...]
            at += a.shape[1]
        total = dot_nt(left[...], right[...]) if transposed else dot_nn(left[...], right[...])
        held[pl.ds(pl.multiple_of(i * RB, RB), RB), :] = total.astype(BF)

    @pl.when(i >= info[NB])
    def _():
        held[pl.ds(pl.multiple_of(i * RB, RB), RB), :] = jnp.zeros((RB, D), BF)

    move_own = pltpu.make_async_copy(held.at[pl.ds(0, CAN), :], own, sems.at[0])

    @pl.when(i == (CAN - 1) // RB)
    def _():
        move_own.start()

    @pl.when(i == pl.num_programs(0) - 1)
    def _():
        move_other = pltpu.make_async_copy(held.at[pl.ds(pl.multiple_of(info[BASE], 16), CAN), :], other, sems.at[1])
        move_other.start()
        move_own.wait()
        move_other.wait()


def sums(info, lefts, rights, transposed, after=()):
    n = len(lefts)
    bs = pl.BlockSpec
    sds = jax.ShapeDtypeStruct

    def rows_of(a, p):
        if p is None:
            return bs((RB, a.shape[1]), clamp)
        return bs((None, RB, a.shape[2]), lambda i, info: (p, jnp.minimum(i, info[NB] - 1), 0))

    def all_of(b, p):
        return bs(b.shape, whole) if p is None else bs((None, *b.shape[1:]), lambda i, info: (p, 0, 0))

    in_specs = [rows_of(*a) for a in lefts] + [all_of(*b) for b in rights]
    lefts, rights = [a for a, _ in lefts], [b for b, _ in rights]
    k = sum(a.shape[-1] for a in lefts)
    v = pltpu.VMEM
    scratch = [v((RB, k), BF), v((D, k) if transposed else (k, D), BF), v((ROWS, D), BF), pltpu.SemaphoreType.DMA((2,))]
    hbm = bs(memory_space=pl.ANY)
    return call(functools.partial(sums_body, n=n, transposed=transposed), (sds((CAN, D), BF),) * 2, scratch,
                (info, *lefts, *rights), in_specs, (hbm,) * 2, grid=(NRB,), prefetch=1,
                vmem=60, cost=(2 * 2304 * k * D, 2 * 2304 * (k + D)), after=after, tick=True)


def adds_body(*refs, counts, kinds):
    given = list(refs[: sum(counts)])
    outs = list(refs[sum(counts) :])
    for count, kind in zip(counts, kinds):
        terms = [given.pop(0) for _ in range(count)]
        if kind == "four":
            total = terms[0][...].astype(F32) + terms[1][...].astype(F32)
            for i in range(4):
                outs.pop(0)[...] = total[i : i + 1].astype(BF)
        else:
            total = terms[0][...].astype(F32)
            for t in terms[1:]:
                total = total + t[...].astype(F32)
            out = outs.pop(0)
            out[...] = total.astype(out.dtype)


def adds(items, after, vmem=VMEM_MIB):
    sds = jax.ShapeDtypeStruct
    outs = []
    for terms, kind in items:
        a = terms[0]
        shape = (1, *a.shape[1:]) if kind == "four" else a.shape
        outs += [sds(shape, F32 if kind == "float" else BF)] * (4 if kind == "four" else 1)
    args = [t for terms, _ in items for t in terms]
    body = functools.partial(adds_body, counts=[len(t) for t, _ in items], kinds=[k for _, k in items])
    *done, tick = call(body, tuple(outs), [], args, [ANYWHERE] * len(args), cost=(0, 3 * 10**6), after=after, tick=True, vmem=vmem)
    results = []
    for _, kind in items:
        results.append([done.pop(0) for _ in range(4)] if kind == "four" else done.pop(0))
    return *results, tick


def final_body(place, w_in, ln, *refs):
    own, other = refs[:4], refs[4:8]
    gin, gout, gln, gqs, gks, gmb, gob = refs[8:]
    c, f = place[CORE], place[FSDP]
    for cc in range(2):
        sources = [jnp.where(c == cc, a[0], b[0]) for a, b in zip(own, other)]
        for p in range(3):
            for n in range(3):
                at = D * n + 384 * cc + 128 * p
                gin[:, at : at + 128] = sources[0][288 * p + 96 * n : 288 * p + 96 * n + 96, :]
        for j in range(3):
            s = sources[1 + j]
            m = jnp.concatenate([s[0:96], s[96:192]], axis=1)
            done = 0
            for u, n in unit_ranges(cc, j):
                gin[:, 3 * D + u : 3 * D + u + n] = m[:, done : done + n]
                done += n
            for t in range(3):
                lanes = slice(256 * t, 256 * t + 256)
                part = s[192 + 80 * t : 272 + 80 * t]

                @pl.when(f != 1)
                def _():
                    gout[240 * cc + 80 * j : 240 * cc + 80 * j + 80, lanes] = part

                @pl.when(f == 1)
                def _():
                    a, b = 144 * cc + 48 * j, 288 + 96 * cc + 32 * j
                    gout[a : a + 48, lanes] = part[:48]
                    gout[b : b + 32, lanes] = part[48:]
    total = jnp.sum(w_in[...].astype(F32) * gin[...], axis=1, keepdims=True)
    gln[...] = jnp.transpose(jnp.broadcast_to(total, (96, 128)))[0:1, :] / ln[...]
    vec = own[3][0, 432:440, :] + other[3][0, 432:440, :]
    gmb[...] = jnp.concatenate([vec[0:1, :], vec[1:2, :128]], axis=1)
    gob[...] = vec[1:2, 128:224]
    gqs[...] = vec[2:3, 0:8]
    gks[...] = vec[2:3, 128:136]


def final(place, w_in, ln, own, other, after=()):
    sds = jax.ShapeDtypeStruct
    outs = (sds((96, 7 * D), F32), sds((480, D), F32), sds((1, 96), F32), sds((1, 8), F32), sds((1, 8), F32),
            sds((1, 384), F32), sds((1, 96), F32))
    return call(final_body, outs, [], (place, w_in, ln, *own, *other), [SCALARS] + [ANYWHERE] * 10, cost=(0, 10**7), after=after)


def routes():
    places = [(x, c, z, y) for x in range(2) for c in range(2) for z in range(4) for y in range(2)]
    number = lambda x, c, z, y: (x * 2 + c) * 8 + z * 2 + y
    pairs = lambda move: [(number(*p), number(*move(*p))) for p in places]
    out = {
        "core": pairs(lambda x, c, z, y: (x, 1 - c, z, y)),
        "x": pairs(lambda x, c, z, y: (1 - x, c, z, y)),
        "y": pairs(lambda x, c, z, y: (x, c, z, 1 - y)),
        "z1": pairs(lambda x, c, z, y: (x, c, z ^ 1, y)),
        "z2": pairs(lambda x, c, z, y: (x, c, z ^ 2, y)),
        "z3": pairs(lambda x, c, z, y: (x, c, z ^ 3, y)),
    }
    at = lambda n: (n % 8) // 2
    out["z2_up"] = [(a, b) for a, b in out["z2"] if at(a) == 0]
    out["z1_up"] = [(a, b) for a, b in out["z1"] if at(a) % 2 == 0]
    return out


def per_device_paired(
    tokens, lengths, assign, w_in, w_out, ln_scale, q_scale, k_scale, mlp_bias, out_bias, cotangent
):
    way = routes()
    go = lambda v, name: lax.ppermute(v, ("rep", "fsdp"), way[name])
    rep, f = lax.axis_index("rep"), lax.axis_index("fsdp")
    c, y, z = rep % 2, f % 2, f // 2
    cap = tokens.shape[0]
    device = rep * 8 + f
    place = jnp.stack([c, f, y, z, device, device + 8 - 16 * c, rep // 2]).astype(jnp.int32)

    late = lambda v, tick: v if tick is None else v + tick[0].astype(v.dtype)
    first = lambda piece, tick=None: jnp.stack([piece, late(go(piece, "z2"), tick)])
    second = lambda two, tick=None: jnp.concatenate([two, late(go(two, "z1"), tick)])
    third = lambda four: (four, go(four, "y"))
    vectors = (v.reshape(1, -1) for v in (ln_scale, q_scale, k_scale, mlp_bias, out_bias))
    info, a, b, wo = plan(place, lengths, assign, w_in, w_out, *vectors)
    a_b, wo_b = go(a, "z2"), go(wo, "z2_up")
    wo = jnp.where(z == 0, wo, wo_b)
    near = jnp.concatenate([a, a_b, wo])
    b_b = go(b, "z2")
    own, gob, tick = prepare(info, tokens, cotangent, (near,))
    far = late(go(near, "z1"), tick)
    m, own = split(place, w_in, w_out, own, (far,))
    wo = jnp.where(z % 2 == 0, wo, far[608:])
    near = jnp.concatenate([near[:608], far[:608], wo])
    vectors = third(near[:PARTS].reshape(4, 304, 128)[:, 288:])
    other = go(own, "core")
    far = go(near, "y")
    b = jnp.stack([b, late(b_b, tick)])
    b_b = go(b, "z1")
    m_b = go(m, "z2")
    nrm, cot, ln, ob, gain, mb, tick = combine(info, place, own, other, *vectors)
    far = late(far, tick)
    wo_a, wo_b = head_rows(place, near, far)
    wo_b = go(wo_b, "core")
    b = jnp.concatenate([b, late(b_b, tick)])
    m = jnp.stack([m, late(m_b, tick)])

    def heads(pairs, g, before, after):
        return attention(info, place, nrm, cot, *g, wo_a, wo_b, gain, pairs, before, after)

    att_0, dqkv_0, w_0, wo_0, dg, dwo, dw, tick = heads((0,), (near, far), (), (b, m))
    m_b = late(go(m, "z1"), tick)
    att_1, dqkv_1, w_1, wo_1, dg, dwo, send, *g_h, tick = heads((1, 2), (b, go(b, "y")), (dw, dwo, dg), (m_b,))
    pieces = (m, m_b, go(m, "y"), go(m_b, "y"))
    came = go(send, "core")
    att, dqkv, ws, wos = (((p, 0), (q, 0), (q, 1)) for p, q in ((att_0, att_1), (dqkv_0, dqkv_1), (w_0, w_1), (wo_0, wo_1)))

    def hidden(j, vectors, after):
        return mlp(info, place, nrm, cot, pieces, mb, dwo, came, vectors, j, after)

    step_y = lambda g: ((g[0], go(g[1], "y")), "four")
    step_z = lambda g: ((g[0], go(g[2], "z1"), go(g[1], "z2"), go(g[3], "z3")), "whole")
    step_x = lambda g: ((g, go(g, "x")), "float")

    *h0, tick = hidden(0, (), (tick,))
    g_h, tick = adds([step_y(g_h)], (tick,), 60)
    *h1, tick = hidden(1, (), (tick,))
    g_h, g_0, tick = adds([step_z(g_h), step_y(h0[4:6])], (tick,))
    *h2, tick = hidden(2, (gob, dg, h0[6], h1[6]), (tick,))
    act, gm, wins, wouts, _, _, _ = zip(h0, h1, h2)
    plain = lambda arrays: tuple((v, None) for v in arrays)

    g_h, g_0, g_1, tick = adds([step_x(g_h), step_z(g_0), step_y(h1[4:6])], (tick,))
    part, away, tick = sums(info, (*att, *plain(act)), (*wos, *plain(wouts)), False, (tick,))
    away = go(away, "core")
    g_0, g_1, g_2, tick = adds([step_x(g_0), step_z(g_1), step_y(h2[4:6])], (tick,))
    part_b, away_b, tick = sums(info, (*dqkv, *plain(gm)), (*ws, *plain(wins)), True, (tick,))
    away_b = go(away_b, "core")
    g_1, g_2, tick = adds([step_x(g_1), step_z(g_2)], (tick,))
    output, tick = last_rows(info, own, part, away, ob, cap, False, (tick,))
    g_2, tick = adds([step_x(g_2)], (tick,))
    grads = (g_h, g_0, g_1, g_2)
    others = [go(g, "core") for g in grads]
    grad_tokens, tick = last_rows(info, own, part_b, away_b, ln, cap, True, (tick,))
    others[-1] = late(others[-1], tick)
    g_win, g_wout, *small = final(place, w_in, ln_scale.astype(F32).reshape(1, 96), grads, others, (tick,))
    return (output, grad_tokens, g_win, g_wout, *(g.reshape(-1) for g in small))


HEADS = 12
epsilon = 1e-06


def layer_norm(values, weight_gain):
    center = values - jnp.mean(values, axis=-1, keepdims=True)
    spread = jnp.mean(center * center, axis=-1, keepdims=True)
    return center * lax.rsqrt(spread + epsilon) * weight_gain


def layout(lengths, assign, device, row_count):
    own = assign == device
    own_sizes = jnp.where(own, lengths, 0)
    own_ends = jnp.cumsum(own_sizes)
    own_starts = own_ends - own_sizes
    position = lax.broadcasted_iota(jnp.int32, (row_count, lengths.shape[0]), 0)
    number = lax.broadcasted_iota(jnp.int32, (row_count, lengths.shape[0]), 1)
    inside = (position >= own_starts[None, :]) & (position < own_ends[None, :])
    filled = jnp.any(inside, axis=1)
    segment = jnp.sum(jnp.where(inside, number, 0), axis=1)
    return (jnp.where(filled, segment, -1), filled)


def contract_rows(left, right):
    return lax.dot_general(
        left, right, (((0,), (0,)), ((), ())), preferred_element_type=jnp.float32
    )


def contract_cols(left, right):
    return lax.dot_general(
        left, right, (((1,), (1,)), ((), ())), preferred_element_type=jnp.float32
    )


def per_device(
    tokens, lengths, assign, w_in, w_out, ln_scale, q_scale, k_scale, mlp_bias, out_bias, cotangent
):
    row_count = tokens.shape[0]
    head_dim = HD
    head_count = HEADS
    width = head_dim * head_count
    factor = head_dim ** (-0.5)
    device = lax.axis_index("rep") * lax.axis_size("fsdp") + lax.axis_index("fsdp")
    segment, filled = layout(lengths, assign, device, row_count)
    allowed = segment[:, None] == segment[None, :]
    params = (w_in, w_out, ln_scale, q_scale, k_scale, mlp_bias, out_bias)
    full = (
        lax.all_gather(params[0], "fsdp", axis=0, tiled=True),
        lax.all_gather(params[1], "fsdp", axis=0, tiled=True),
        lax.all_gather(params[2], "fsdp", axis=0, tiled=True),
        lax.all_gather(params[3], "fsdp", axis=0, tiled=True),
        lax.all_gather(params[4], "fsdp", axis=0, tiled=True),
        lax.all_gather(params[5], "fsdp", axis=0, tiled=True),
        lax.all_gather(params[6], "fsdp", axis=0, tiled=True),
    )
    win_full, wout_full = (full[0], full[1])
    small = [arr.astype(jnp.float32) for arr in full[2:]]
    ln_full, qs_full, ks_full, mb_full, ob_full = small
    inputs = tokens.astype(jnp.float32)
    normed_f, ln_pull = jax.vjp(layer_norm, inputs, ln_full)
    normed = normed_f.astype(jnp.bfloat16)
    joined = jnp.dot(normed, win_full, preferred_element_type=jnp.float32)
    q_pre = joined[:, :width].reshape(row_count, head_count, head_dim)
    k_pre = joined[:, width : 2 * width].reshape(row_count, head_count, head_dim)
    values = joined[:, 2 * width : 3 * width].astype(jnp.bfloat16)
    hidden_pre = joined[:, 3 * width :]
    q_norm, q_pull = jax.vjp(layer_norm, q_pre, qs_full)
    k_norm, k_pull = jax.vjp(layer_norm, k_pre, ks_full)
    queries = q_norm.reshape(row_count, width).astype(jnp.bfloat16)
    keys_all = k_norm.reshape(row_count, width).astype(jnp.bfloat16)

    def head_slice(array, head_index):
        return lax.dynamic_slice_in_dim(array, head_index * head_dim, head_dim, 1)

    def head_scores(head_index):
        raw = (
            contract_cols(head_slice(queries, head_index), head_slice(keys_all, head_index))
            * factor
        )
        return jnp.where(allowed, raw, -1e30)

    def head_forward(head_index):
        scores = head_scores(head_index)
        top = jnp.max(scores, axis=1, keepdims=True)
        expon = jnp.exp(scores - top)
        total = jnp.sum(expon, axis=1, keepdims=True)
        probs = (expon / total).astype(jnp.bfloat16)
        head_out = jnp.dot(
            probs, head_slice(values, head_index), preferred_element_type=jnp.float32
        )
        return (head_out, (top + jnp.log(total))[:, 0])

    head_outs, log_totals = lax.map(head_forward, jnp.arange(head_count))
    attended = jnp.transpose(head_outs, (1, 0, 2)).reshape(row_count, width)
    activated, gelu_pull = jax.vjp(lambda pre, bias: jax.nn.gelu(pre + bias), hidden_pre, mb_full)
    merged = jnp.concatenate([attended, activated], axis=1).astype(jnp.bfloat16)
    result = jnp.dot(merged, wout_full, preferred_element_type=jnp.float32) + ob_full
    output = jnp.where(filled[:, None], inputs + result, 0.0).astype(jnp.bfloat16)
    back = (
        lax.all_gather(params[0], "fsdp", axis=0, tiled=True),
        lax.all_gather(params[1], "fsdp", axis=0, tiled=True),
        lax.all_gather(params[2], "fsdp", axis=0, tiled=True),
        lax.all_gather(params[3], "fsdp", axis=0, tiled=True),
        lax.all_gather(params[4], "fsdp", axis=0, tiled=True),
        lax.all_gather(params[5], "fsdp", axis=0, tiled=True),
        lax.all_gather(params[6], "fsdp", axis=0, tiled=True),
    )
    win_back, wout_back = (back[0], back[1])
    grad_rows = jnp.where(filled[:, None], cotangent.astype(jnp.float32), 0.0)
    grad_low = grad_rows.astype(jnp.bfloat16)
    grad_ob = jnp.sum(grad_rows, axis=0)
    grad_wout = contract_rows(merged, grad_low)
    grad_merged = contract_cols(grad_low, wout_back)
    grad_attended = grad_merged[:, :width].astype(jnp.bfloat16)
    grad_m, grad_mb = gelu_pull(grad_merged[:, width:])

    def head_backward(head_index):
        scores = head_scores(head_index)
        probs_full = jnp.exp(scores - log_totals[head_index][:, None])
        probs = probs_full.astype(jnp.bfloat16)
        grad_head = head_slice(grad_attended, head_index)
        grad_probs = contract_cols(grad_head, head_slice(values, head_index))
        inner = jnp.sum(probs_full * grad_probs, axis=1, keepdims=True)
        grad_scores = (probs_full * (grad_probs - inner)).astype(jnp.bfloat16)
        grad_q = (
            jnp.dot(
                grad_scores, head_slice(keys_all, head_index), preferred_element_type=jnp.float32
            )
            * factor
        )
        grad_k = contract_rows(grad_scores, head_slice(queries, head_index)) * factor
        grad_v = contract_rows(probs, grad_head)
        return (grad_q, grad_k, grad_v)

    grad_qh, grad_kh, grad_vh = lax.map(head_backward, jnp.arange(head_count))
    grad_qn = jnp.transpose(grad_qh, (1, 0, 2))
    grad_kn = jnp.transpose(grad_kh, (1, 0, 2))
    grad_values = jnp.transpose(grad_vh, (1, 0, 2)).reshape(row_count, width)
    grad_q_pre, grad_qs = q_pull(grad_qn)
    grad_k_pre, grad_ks = k_pull(grad_kn)
    grad_joined = jnp.concatenate(
        [
            grad_q_pre.reshape(row_count, width),
            grad_k_pre.reshape(row_count, width),
            grad_values,
            grad_m,
        ],
        axis=1,
    ).astype(jnp.bfloat16)
    grad_win = contract_rows(normed, grad_joined)
    grad_normed = contract_cols(grad_joined, win_back)
    grad_x_norm, grad_ln = ln_pull(grad_normed)
    grad_tokens = (grad_rows + grad_x_norm).astype(jnp.bfloat16)
    grads = (grad_win, grad_wout, grad_ln, grad_qs, grad_ks, grad_mb, grad_ob)
    shares = (
        lax.psum_scatter(grads[0], "fsdp", scatter_dimension=0, tiled=True),
        lax.psum_scatter(grads[1], "fsdp", scatter_dimension=0, tiled=True),
        lax.psum_scatter(grads[2], "fsdp", scatter_dimension=0, tiled=True),
        lax.psum_scatter(grads[3], "fsdp", scatter_dimension=0, tiled=True),
        lax.psum_scatter(grads[4], "fsdp", scatter_dimension=0, tiled=True),
        lax.psum_scatter(grads[5], "fsdp", scatter_dimension=0, tiled=True),
        lax.psum_scatter(grads[6], "fsdp", scatter_dimension=0, tiled=True),
    )
    shares = lax.psum(
        (shares[0], shares[1], shares[2], shares[3], shares[4], shares[5], shares[6]), "rep"
    )
    return (
        output,
        grad_tokens,
        shares[0],
        shares[1],
        shares[2],
        shares[3],
        shares[4],
        shares[5],
        shares[6],
    )


def solution(mesh):
    in_specs = (
        P(("rep", "fsdp"), None),
        P(),
        P(),
        P("fsdp", None),
        P("fsdp", None),
        P("fsdp"),
        P("fsdp"),
        P("fsdp"),
        P("fsdp"),
        P("fsdp"),
        P(("rep", "fsdp"), None),
    )
    out_specs = (
        P(("rep", "fsdp"), None),
        P(("rep", "fsdp"), None),
        P("fsdp", None),
        P("fsdp", None),
        P("fsdp"),
        P("fsdp"),
        P("fsdp"),
        P("fsdp"),
        P("fsdp"),
    )
    paired = dict(mesh.shape) == {"rep": 4, "fsdp": 8}
    return jax.shard_map(
        per_device_paired if paired else per_device, mesh=mesh, in_specs=in_specs, out_specs=out_specs, check_vma=False
    )
```

```python
import functools

import jax
import jax.numpy as jnp
from jax import lax
from jax.experimental import pallas as pl
from jax.experimental.pallas import tpu as pltpu
from jax.sharding import PartitionSpec as P

D = 768
HD = 64
SMALL = 196
BIG = 1024
BLK = 208
CAN = 7 * BLK
ROWS = 3072
ROOM = 3584
RB = 512
NRB = ROWS // RB
U = 512
EPS = 1e-06
BF = jnp.bfloat16
F32 = jnp.float32
VMEM_MIB = 34
ANYWHERE = pl.BlockSpec(memory_space=pltpu.VMEM)
TICK = jax.ShapeDtypeStruct((1,), F32)
SCALARS = pl.BlockSpec(memory_space=pltpu.SMEM)


def dot_nn(a, b):
    return lax.dot_general(a, b, (((1,), (0,)), ((), ())), preferred_element_type=F32)


def dot_nt(a, b):
    return lax.dot_general(a, b, (((1,), (1,)), ((), ())), preferred_element_type=F32)


def dot_tn(a, b):
    return lax.dot_general(a, b, (((0,), (0,)), ((), ())), preferred_element_type=F32)


def two_parts(x):
    hi = x.astype(BF)
    return hi, (x - hi.astype(F32)).astype(BF)


def call(body, out_shape, scratch, args, in_specs, out_specs=None, grid=None, prefetch=0, cost=None, after=(), tick=False, alias=None, vmem=VMEM_MIB):
    if after:
        inner, n, skip = body, len(args), len(after)

        def body(*refs):
            inner(*refs[:n], *refs[n + skip :])

        args = (*args, *after)
        in_specs = [*in_specs] + [pl.BlockSpec(memory_space=pl.ANY)] * skip
    params = pltpu.CompilerParams(vmem_limit_bytes=vmem * 2**20)
    if out_specs is None:
        out_specs = jax.tree.map(lambda _: ANYWHERE, out_shape)
    if tick:
        many = isinstance(out_shape, tuple)
        out_shape = (*out_shape, TICK) if many else (out_shape, TICK)
        out_specs = (*out_specs, SCALARS) if many else (out_specs, SCALARS)
        untold, place = body, len(args) + len(out_shape) - 1

        def body(*refs):
            refs[place][0] = jnp.float32(0)
            untold(*refs[:place], *refs[place + 1 :])

    spec = pltpu.PrefetchScalarGridSpec(
        num_scalar_prefetch=prefetch,
        grid=grid or (),
        in_specs=in_specs,
        out_specs=out_specs,
        scratch_shapes=scratch,
    )
    estimate = None if cost is None else pl.CostEstimate(flops=20 * cost[0], bytes_accessed=20 * cost[1], transcendentals=0)
    return pl.pallas_call(body, grid_spec=spec, out_shape=out_shape, compiler_params=params, cost_estimate=estimate, input_output_aliases=alias or {})(*args)


NB, BLOCKS_A, LARGE_A, SMALL_A, BASE, BLOCKS_B, LARGE_B, SMALL_B, BEFORE = range(9)
CORE, FSDP, Y, Z, SELF, MATE, X = range(7)


def unit_ranges(c, j):
    first = [(96 * c + 32 * j, 32)]
    return first + [(192 + 480 * s + 240 * c + 80 * j, 80) for s in range(6)]


def pieces_body(place, w_in, w_out, heads, wo, sems):
    own = 384 * place[CORE]
    lanes = lambda at: pl.ds(pl.multiple_of(own + at, 128), 128)
    rows = lambda at: pl.ds(at, 96)
    half = pl.ds(pl.multiple_of(240 * place[X], 16), 240)
    moves = []
    for n in range(3):
        moves.append((w_out.at[half, lanes(128 * n)], wo.at[pl.ds(240 * n, 240), :]))
        for p in range(3):
            moves.append((w_in.at[:, lanes(D * n + 128 * p)], heads.at[rows(288 * p + 96 * n), :]))
    moves = [pltpu.make_async_copy(p, q, sems.at[i]) for i, (p, q) in enumerate(moves)]
    for move in moves:
        move.start()
    for move in moves:
        move.wait()


def pieces_of(place, w_in, w_out):
    sds = jax.ShapeDtypeStruct
    hbm = pl.BlockSpec(memory_space=pl.ANY)
    return call(pieces_body, (sds((864, 128), BF), sds((720, 128), BF)), [pltpu.SemaphoreType.DMA((12,))],
                (place, w_in, w_out), [SCALARS, hbm, hbm], (ANYWHERE,) * 2, vmem=60, cost=(0, 2 * 10**6), tick=True)


def plan_body(place, lengths, assign, ln, qs, ks, mb, ob, info, params):
    def count(i, carry):
        before, small_a, large_a, small_b, large_b = carry
        large = (lengths[i] == BIG).astype(jnp.int32)
        me = (assign[i] == place[SELF]).astype(jnp.int32)
        mate = (assign[i] == place[MATE]).astype(jnp.int32)
        before = jnp.where(me * large == 1, small_a, before)
        return before, small_a + me * (1 - large), large_a + me * large, small_b + mate * (1 - large), large_b + mate * large

    zero = jnp.int32(0)
    before, small_a, large_a, small_b, large_b = lax.fori_loop(0, lengths.shape[0], count, (zero,) * 5)
    blocks_a = jnp.where(large_a > 0, 7, small_a)
    blocks_b = jnp.where(large_b > 0, 7, small_b)
    info[NB] = (BLK * (blocks_a + blocks_b) + RB - 1) // RB
    info[BLOCKS_A], info[LARGE_A], info[SMALL_A] = blocks_a, large_a, small_a
    info[BASE] = BLK * blocks_a
    info[BLOCKS_B], info[LARGE_B], info[SMALL_B] = blocks_b, large_b, small_b
    info[BEFORE] = jnp.where(large_a > 0, before, small_a)
    params[...] = jnp.zeros_like(params)
    params[0:1, :96] = ln[...]
    params[1:2, :8] = qs[...]
    params[2:3, :8] = ks[...]
    params[3:4, :96] = ob[...]
    for n in range(3):
        params[4 + n : 5 + n, :] = mb[:, 128 * n : 128 * n + 128]


def plan(place, lengths, assign, *small, after):
    sds = jax.ShapeDtypeStruct
    return call(plan_body, (sds((16,), jnp.int32), sds((16, 128), BF)), [], (place, lengths, assign, *small),
                [SCALARS] * 3 + [ANYWHERE] * 5, (SCALARS, ANYWHERE), vmem=60, cost=(0, 10**5), after=after)


def split_body(place, w_in, w_out, own, m, own_o):
    c, f = place[CORE], place[FSDP]
    for cc in range(2):

        @pl.when(c == cc)
        def _():
            for j in range(3):
                cols = [w_in[:, 3 * D + u : 3 * D + u + n] for u, n in unit_ranges(cc, j)]
                half = jnp.concatenate(cols, axis=1)
                m[j, 0:96, :] = half[:, :256]
                m[j, 96:192, :] = half[:, 256:]
                for t in range(3):
                    lanes = slice(256 * t, 256 * t + 256)
                    at = 192 + 80 * t

                    @pl.when(f != 1)
                    def _():
                        m[j, at : at + 80, :] = w_out[240 * cc + 80 * j : 240 * cc + 80 * j + 80, lanes]

                    @pl.when(f == 1)
                    def _():
                        a, b = 144 * cc + 48 * j, 288 + 96 * cc + 32 * j
                        m[j, at : at + 48, :] = w_out[a : a + 48, lanes]
                        m[j, at + 48 : at + 80, :] = w_out[b : b + 32, lanes]


def split(place, w_in, w_out, own, after):
    sds = jax.ShapeDtypeStruct
    outs = (sds((3, 432, 256), BF), sds(own.shape, BF))
    hbm = pl.BlockSpec(memory_space=pl.ANY)
    return call(split_body, outs, [], (place, w_in, w_out, own), [SCALARS] + [ANYWHERE] * 2 + [hbm], (ANYWHERE, hbm),
                cost=(0, 4 * 10**6), after=after, alias={3: 1})


def slot_of(place, f):
    dz = place[Z] ^ (f >> 1)
    return place[Y] ^ (f & 1), ((dz & 1) << 1) | (dz >> 1)


def taken(place, near, far, f, rows):
    side, at = slot_of(place, f)
    return jnp.where(side == 0, near[at, rows, :], far[at, rows, :])


def put(place, near, far, f, fill):
    side, at = slot_of(place, f)

    @pl.when(side == 0)
    def _():
        fill(near.at[at])

    @pl.when(side != 0)
    def _():
        fill(far.at[at])


def each_image(info, move):
    start = SMALL * info[BEFORE]

    @pl.when(info[LARGE_A] == 1)
    def _():
        for t in range(5):
            move(BLK * t, start + BLK * t, min(BLK, BIG - BLK * t))

    def small(i, carry):
        large = BIG * info[LARGE_A]
        move(pl.multiple_of(large + BLK * i, 16), SMALL * i + jnp.where(i >= info[BEFORE], large, 0), SMALL)
        return carry

    lax.fori_loop(0, info[SMALL_A], small, 0)


WINDOW = BLK + 16


def window_of(slot):
    first = (slot // 16) * 16
    return pl.ds(pl.multiple_of(first, 16), WINDOW), slot - first


def prepare_body(info, tokens, cot, out, gob_o, pad_x, pad_g):
    cap = tokens.shape[0]
    for pad, held in ((pad_x, tokens), (pad_g, cot)):
        pad[0:cap, :] = held[...]
        pad[cap:, :] = jnp.zeros((pad.shape[0] - cap, D), BF)
    out[...] = jnp.zeros_like(out)
    gob_o[...] = jnp.zeros_like(gob_o)
    apart = lax.broadcasted_iota(jnp.int32, (BLK, WINDOW), 1) - lax.broadcasted_iota(jnp.int32, (BLK, WINDOW), 0)
    row = lax.broadcasted_iota(jnp.int32, (BLK, WINDOW), 0)

    def move(to, slot, n):
        window, shift = window_of(slot)
        pick = ((apart == shift) & (row < n)).astype(BF)
        rows = pl.ds(to, BLK)
        g = dot_nn(pick, pad_g[window, :])
        out[0, rows, :] = dot_nn(pick, pad_x[window, :]).astype(BF)
        out[1, rows, :] = g.astype(BF)
        gob_o[...] += jnp.sum(g, axis=0, keepdims=True)

    each_image(info, move)


def prepare(info, tokens, cot, after):
    sds = jax.ShapeDtypeStruct
    pad = pltpu.VMEM((CAN + 16, D), BF)
    return call(prepare_body, (sds((2, CAN, D), BF), sds((1, D), F32)), [pad, pad], (info, tokens, cot),
                [SCALARS] + [ANYWHERE] * 2, vmem=60, cost=(10**9, 9 * 10**6), after=after, tick=True)


def combine_body(info, place, own, other, near, far, nrm, cot, ln_o, ob_o, gain_o, mb_o, x, y, g, zero, sems, zero_sems):
    count_a, count_b = info[BLOCKS_A], info[BLOCKS_B]

    def copies(source, i, t):
        rows = pl.ds(pl.multiple_of(i * BLK, 16), BLK)
        to = pl.ds(pl.multiple_of(t * BLK, 16), BLK)
        return (lambda: pltpu.make_async_copy(source.at[0, rows, :], x.at[t], sems.at[0, t]),
                lambda: pltpu.make_async_copy(source.at[1, rows, :], g.at[t], sems.at[1, t]),
                lambda: pltpu.make_async_copy(g.at[t], cot.at[to, :], sems.at[3, t]),
                lambda: pltpu.make_async_copy(y.at[t], nrm.at[to, :], sems.at[2, t]))

    def over(body):
        def step_a(i, carry):
            body(i, *copies(own, i, i))
            return carry

        def step_b(i, carry):
            body(count_a + i, *copies(other, i, count_a + i))
            return carry

        lax.fori_loop(0, count_a, step_a, 0)
        lax.fori_loop(0, count_b, step_b, 0)

    def begin(t, to_x, to_g, to_cot, to_nrm):
        to_x().start()
        to_g().start()

    over(begin)
    zero[...] = jnp.zeros_like(zero)
    end = pl.ds(pl.multiple_of((count_a + count_b) * BLK, 16), RB)
    blanks = [pltpu.make_async_copy(zero, out.at[end, :], zero_sems.at[n]) for n, out in enumerate((nrm, cot))]
    for move in blanks:
        move.start()
    small = [taken(place, near, far, f, slice(0, 16)).astype(F32) for f in range(8)]
    ln = jnp.concatenate([s[0:1, :96] for s in small], axis=1)
    ln_o[...] = ln
    ob_o[...] = jnp.concatenate([s[3:4, :96] for s in small], axis=1)
    gain_o[...] = jnp.concatenate(([s[1:2, :8] for s in small] * 2) + ([s[2:3, :8] for s in small] * 2), axis=1)
    mb = jnp.concatenate([s[4 + n : 5 + n, :] for s in small for n in range(3)], axis=1)
    for j in range(3):
        rows = [jnp.concatenate([mb[:, u : u + n] for u, n in unit_ranges(cc, j)], axis=1) for cc in range(2)]
        mb_o[j : j + 1, :] = jnp.where(place[CORE] == 0, rows[0], rows[1])

    def norm(t, to_x, to_g, to_cot, to_nrm):
        to_x().wait()
        v = x[t].astype(F32)
        center = v - jnp.mean(v, axis=1, keepdims=True)
        spread = jnp.mean(center * center, axis=1, keepdims=True)
        y[t] = (center * lax.rsqrt(spread + EPS) * ln).astype(BF)
        to_nrm().start()
        to_g().wait()
        to_cot().start()

    over(norm)

    def finish(t, to_x, to_g, to_cot, to_nrm):
        to_cot().wait()
        to_nrm().wait()

    over(finish)
    for move in blanks:
        move.wait()


def combine(info, place, own, other, near, far, after=()):
    sds = jax.ShapeDtypeStruct
    outs = (sds((ROOM, D), BF),) * 2 + (sds((1, D), F32),) * 2 + (sds((1, 256), F32), sds((3, U), F32))
    hbm = pl.BlockSpec(memory_space=pl.ANY)
    v = pltpu.VMEM
    most = 2 * CAN // BLK
    scratch = [v((most, BLK, D), BF)] * 3 + [v((RB, D), BF), pltpu.SemaphoreType.DMA((4, most)), pltpu.SemaphoreType.DMA((2,))]
    return call(combine_body, outs, scratch, (info, place, own, other, near, far), [SCALARS] * 2 + [hbm] * 2 + [ANYWHERE] * 2,
                (hbm,) * 2 + (ANYWHERE,) * 4, vmem=60, cost=(0, 18 * 10**6), after=after, tick=True)


def rows_body(info, x_h, a_h, b_h, vector, out, x, a, b, held, pad, sems, *, gradient):
    moves = []
    for i in range(CAN // BLK):
        rows = pl.ds(i * BLK, BLK)
        pairs = [(x_h.at[0, rows, :], x.at[0, rows, :]), (a_h.at[rows, :], a.at[rows, :]), (b_h.at[rows, :], b.at[rows, :])]
        if gradient:
            pairs.append((x_h.at[1, rows, :], x.at[1, rows, :]))
        moves.append([pltpu.make_async_copy(p, q, sems.at[n, i]) for n, (p, q) in enumerate(pairs)])
        for move in moves[-1]:
            move.start()
    pad[...] = jnp.zeros_like(pad)
    for i in range(CAN // BLK):
        for move in moves[i]:
            move.wait()
        rows = pl.ds(i * BLK, BLK)
        v = x[0, rows, :].astype(F32)
        total = a[rows, :].astype(F32) + b[rows, :].astype(F32)
        if gradient:
            center = v - jnp.mean(v, axis=1, keepdims=True)
            r = lax.rsqrt(jnp.mean(center * center, axis=1, keepdims=True) + EPS)
            xh = center * r
            g = total * vector[...]
            gx = r * (g - jnp.mean(g, axis=1, keepdims=True) - xh * jnp.mean(g * xh, axis=1, keepdims=True))
            held[rows, :] = (x[1, rows, :].astype(F32) + gx).astype(BF)
        else:
            held[rows, :] = (v + (total + vector[...])).astype(BF)
    apart = lax.broadcasted_iota(jnp.int32, (WINDOW, BLK), 0) - lax.broadcasted_iota(jnp.int32, (WINDOW, BLK), 1)
    col = lax.broadcasted_iota(jnp.int32, (WINDOW, BLK), 1)

    def move(at, slot, n):
        window, shift = window_of(slot)
        pick = ((apart == shift) & (col < n)).astype(BF)
        pad[window, :] += dot_nn(pick, held[pl.ds(at, BLK), :]).astype(BF)

    each_image(info, move)
    out[...] = pad[: out.shape[0], :]


def last_rows(info, x, a, b, vector, cap, gradient, after=()):
    v = pltpu.VMEM
    scratch = [v((2, CAN, D), BF), v((CAN, D), BF), v((CAN, D), BF), v((CAN, D), BF), v((CAN + 16, D), BF),
               pltpu.SemaphoreType.DMA((4, CAN // BLK))]
    hbm = pl.BlockSpec(memory_space=pl.ANY)
    return call(functools.partial(rows_body, gradient=gradient), jax.ShapeDtypeStruct((cap, D), BF), scratch, (info, x, a, b, vector),
                [SCALARS] + [hbm] * 3 + [ANYWHERE], cost=(4 * 10**9, 12 * 10**6), after=after, tick=True)


def head_rows_body(place, near, far, cross, mine, theirs):
    rows = slice(PARTS, PARTS + 720)
    swap_y, swap_x, second_core = place[Y] != 0, place[X] != 0, place[CORE] != 0
    pick = lambda swap, a, b: (jnp.where(swap, b, a), jnp.where(swap, a, b))
    own = pick(swap_y, near[rows, :], far[rows, :])
    came = pick(swap_y, cross[0:720, :], cross[720:, :])
    (low, high), (low_1, high_1) = (pick(swap_x, a, b) for a, b in zip(own, came))
    for n in range(3):
        lanes = slice(128 * n, 128 * n + 128)
        at = 240 * n
        first = jnp.concatenate([low[at : at + 240], high[at : at + 144]])
        second = jnp.concatenate([high[at + 144 : at + 240], low_1[at : at + 240], high_1[at : at + 48]])
        mine[:, lanes], theirs[:, lanes] = pick(second_core, first, second)


def head_rows(place, near, far, cross, after):
    sds = jax.ShapeDtypeStruct
    return call(head_rows_body, (sds((384, 384), BF),) * 2, [], (place, near, far, cross), [SCALARS] + [ANYWHERE] * 3, cost=(0, 10**6),
                after=after, tick=True)


PARTS = 4 * 288


def attention_body(info, place, nrm_h, cot_h, near, far, wo_a, wo_b, gain, *refs, pairs):
    refs = list(refs)
    last = len(pairs) > 1
    if last:
        dw_0, dwo_0, dg_0 = refs[:3]
        refs = refs[3:]
    att_o, dqkv_o, w_o, wo_o, dg_o, dwo_o = refs[:6]
    if last:
        dwo_send, near_o, far_o = refs[6:9]
        refs = refs[9:]
    else:
        dw_o = refs[6]
        refs = refs[7:]
    nrm, cot, sems, vv, qp, kp, do, xh, rr, dqk, dv, dw, dwo, dws = refs
    step = pl.program_id(0)
    nb = info[NB]

    def incoming(i):
        rows = pl.ds(pl.multiple_of(i * RB, RB), RB)
        return (pltpu.make_async_copy(nrm_h.at[rows, :], nrm.at[rows, :], sems.at[0, i]),
                pltpu.make_async_copy(cot_h.at[rows, :], cot.at[rows, :], sems.at[1, i]))

    @pl.when(step == 0)
    def _():
        def begin(i, carry):
            for move in incoming(i):
                move.start()
            return carry

        lax.fori_loop(0, nb, begin, 0)
        if last:
            dg_o[...] = dg_0[...]
        else:
            dg_o[...] = jnp.zeros_like(dg_o)

    lane = lax.broadcasted_iota(jnp.int32, (1, 128), 1)
    first = lane < HD
    same = lax.broadcasted_iota(jnp.int32, (256, 256), 0) // HD == lax.broadcasted_iota(jnp.int32, (256, 256), 1) // HD
    mean_m = jnp.where(same, 1.0 / HD, 0.0).astype(BF)
    sum_m = jnp.where(same[:, :128] | same[:, 128:], 1.0, 0.0).astype(BF)
    c_exp = 1.4426950408889634 / 8.0
    masks = [jnp.where(first, 1.0, 0.0).astype(BF), jnp.where(first, 0.0, 1.0).astype(BF)]

    for f in range(8):
        side, at = slot_of(place, f)
        if pairs[0] == 0:
            rows = pl.ds(pl.multiple_of(288 * at, 16), 288)
            piece = jnp.where(side == 0, near[rows, :], far[rows, :])
        else:
            rows = pl.ds(pl.multiple_of(288 * step, 16), 288)
            piece = jnp.where(side == 0, near[at, rows, :], far[at, rows, :])
        for n in range(3):
            w_o[96 * f : 96 * f + 96, 128 * n : 128 * n + 128] = piece[96 * n : 96 * n + 96]
    rows = pl.ds(pl.multiple_of(128 * (pairs[0] + step), 16), 128)
    mine, theirs = wo_a[rows, :], wo_b[rows, :]
    wo_o[:, :384] = jnp.where(place[CORE] == 0, mine, theirs)
    wo_o[:, 384:] = jnp.where(place[CORE] == 0, theirs, mine)

    def mean(x):
        return dot_nn(x.astype(BF), mean_m)

    def project(i, carry):
        @pl.when(step == 0)
        def _():
            for move in incoming(i):
                move.wait()

        rows = pl.ds(pl.multiple_of(i * RB, RB), RB)
        y = dot_nn(nrm[rows, :], w_o[...])
        qk, v = y[:, :256], y[:, 256:]
        center = qk - mean(qk)
        r = lax.rsqrt(mean(center * center) + EPS)
        x = center * r
        xh[rows, :] = x
        rr[rows, :] = r
        qk = (x * gain[...]).astype(BF)
        qp[rows, :] = qk[:, :128]
        kp[rows, :] = qk[:, 128:]
        vv[0, rows, :] = jnp.where(first, v, 1.0).astype(BF)
        vv[1, rows, :] = jnp.where(first, 1.0, v).astype(BF)
        do[rows, :] = dot_nt(cot[rows, :], wo_o[...]).astype(BF)
        dqk[rows, :] = jnp.zeros((RB, 256), F32)
        dv[rows, :] = jnp.zeros((RB, 128), F32)
        att_o[rows, :] = jnp.zeros((RB, 128), BF)
        return carry

    lax.fori_loop(0, nb, project, 0)

    def blocks(items, masked, add):
        both = [(i, h) for i in range(len(items)) for h in range(2)]
        plain = [qp[it[0], :] for it in items]
        ql = [[q * m for m in masks] for q in plain]
        kl = [kp[it[1], :] for it in items]
        vl = [[vv[h, it[1], :] for h in range(2)] for it in items]
        grads = [do[it[0], :].astype(F32) for it in items]
        p, pb, xs = {}, {}, {}
        for i, h in both:
            e = jnp.exp2(dot_nt(ql[i][h], kl[i]) * c_exp)
            if masked:
                e = jnp.where(lax.broadcasted_iota(jnp.int32, e.shape, 1) < SMALL, e, 0.0)
            p[i, h] = e
            pb[i, h] = e.astype(BF)
        for i, h in both:
            xs[i, h] = dot_nn(pb[i, h], vl[i][h])
        outs, scaled, lefts = [], [], {}
        for i in range(len(items)):
            total = jnp.where(first, pltpu.roll(xs[i, 0], HD, 1), pltpu.roll(xs[i, 1], HD, 1))
            inverse = 1.0 / total
            out = jnp.where(first, xs[i, 0], xs[i, 1]) * inverse
            outs.append(out.astype(BF))
            hi, lo = two_parts(grads[i] * out)
            inner = dot_nn(jnp.concatenate([hi, lo], axis=1), sum_m) * inverse
            s = (grads[i] * inverse).astype(BF)
            scaled.append(s)
            sf = s.astype(F32)
            hi, lo = two_parts(inner)
            hi, lo = pltpu.roll(hi.astype(F32), HD, 1), pltpu.roll(lo.astype(F32), HD, 1)
            for h in range(2):
                own = first if h == 0 else jnp.logical_not(first)
                at = HD * (1 - h)
                side = jnp.where(lane == at, -hi, jnp.where(lane == at + 1, -lo, 0.0))
                lefts[i, h] = jnp.where(own, sf, side).astype(BF)
        ds = {}
        for i, h in both:
            ds[i, h] = (p[i, h] * dot_nt(lefts[i, h], vl[i][h])).astype(BF)
        dq = {t: dot_nn(ds[t], kl[t[0]]) for t in both}
        turned = [(jnp.transpose(a.astype(F32)).astype(BF), jnp.transpose(b.astype(F32)).astype(BF)) for a, b in zip(plain, scaled)]
        dk = {(i, h): dot_nn(turned[i][0][HD * h : HD * h + HD], ds[i, h]) for i, h in both}
        dvs = {(i, h): dot_nn(turned[i][1][HD * h : HD * h + HD], pb[i, h]) for i, h in both}
        for i, (q_rows, k_rows) in enumerate(items):
            att_o[q_rows, :] = outs[i]
            dqk[q_rows, :128] = jnp.where(first, dq[i, 0], dq[i, 1])
            new_k = jnp.transpose(jnp.concatenate([dk[i, 0], dk[i, 1]], axis=0))
            new_v = jnp.transpose(jnp.concatenate([dvs[i, 0], dvs[i, 1]], axis=0))
            if add:
                dqk[k_rows, 128:] += new_k
                dv[k_rows, :] += new_v
            else:
                dqk[k_rows, 128:] = new_k
                dv[k_rows, :] = new_v

    count_a, count_b = info[SMALL_A], info[SMALL_B]

    def small_rows(i):
        row_a = BIG * info[LARGE_A] + BLK * i
        row_b = info[BASE] + BIG * info[LARGE_B] + BLK * (i - count_a)
        row = jnp.where(i < count_a, row_a, jnp.where(i < count_a + count_b, row_b, ROWS))
        return pl.ds(pl.multiple_of(row, 16), BLK)

    def smalls(i, carry):
        rows = [small_rows(3 * i + n) for n in range(3)]
        blocks([(r, r) for r in rows], True, False)
        return carry

    lax.fori_loop(0, (count_a + count_b + 2) // 3, smalls, 0)

    def large_block(i, carry):
        base = jnp.where(i < 2 * info[LARGE_A], 0, info[BASE])
        k_rows = pl.ds(pl.multiple_of(base, 16), BIG)
        blocks([(pl.ds(pl.multiple_of(base + (i & 1) * 512, 16), 512), k_rows)], False, True)
        return carry

    lax.fori_loop(0, 2 * (info[LARGE_A] + info[LARGE_B]), large_block, 0)

    dw[...] = jnp.zeros_like(dw)
    dwo[...] = jnp.zeros_like(dwo)

    def pull(i):
        rows = pl.ds(pl.multiple_of(i * RB, RB), RB)
        g_out = dqk[rows, :]
        x = xh[rows, :]
        dg_o[...] += 0.125 * jnp.sum(g_out * x, axis=0, keepdims=True)
        g = g_out * (0.125 * gain[...])
        g = rr[rows, :] * (g - mean(g) - x * mean(g * x))
        dqkv_o[rows, :] = jnp.concatenate([g.astype(BF), dv[rows, :].astype(BF)], axis=1)

    def weigh(i):
        rows = pl.ds(pl.multiple_of(i * RB, RB), RB)
        dw[...] += dot_tn(dqkv_o[rows, :], nrm[rows, :])
        dwo[...] += dot_tn(att_o[rows, :], cot[rows, :])

    def finish(i, carry):
        weigh(i - 1)
        pull(i)
        return carry

    pull(0)
    lax.fori_loop(1, nb, finish, 0)
    weigh(nb - 1)
    if not last:
        dwo_o[...] = dwo[...].astype(BF)
        dw_o[...] = dw[...].astype(BF)
        return
    dwo_o[pl.ds(pl.multiple_of(128 + 128 * step, 16), 128), :] = dwo[...].astype(BF)

    @pl.when(step == 0)
    def _():
        dws[...] = dw[...]
        dwo_o[0:128, :] = dwo_0[...]

    @pl.when(step == len(pairs) - 1)
    def _():
        dwo_send[...] = jnp.where(place[CORE] == 0, dwo_o[240:384, :], dwo_o[96:240, :])
        full = [jnp.transpose(d).astype(BF) for d in (dw_0[...].astype(F32), dws[...], dw[...])]
        for f in range(8):

            def fill(ref, f=f):
                for q in range(3):
                    for n in range(3):
                        at = 288 * q + 96 * n
                        ref[at : at + 96, :] = full[q][96 * f : 96 * f + 96, 128 * n : 128 * n + 128]

            put(place, near_o, far_o, f, fill)


def attention(info, place, nrm, cot, near, far, wo_a, wo_b, gain, pairs, before=(), after=()):
    sds = jax.ShapeDtypeStruct
    bs = pl.BlockSpec
    n, more = len(pairs), ROWS + 256
    outs = [sds((n, more, 128), BF), sds((n, ROWS, 384), BF), sds((n, D, 384), BF), sds((n, 128, D), BF), sds((1, 256), F32)]
    by_pair = lambda p: (p, 0, 0)
    fixed = lambda a: bs(a.shape, lambda p: (0,) * len(a.shape))
    specs = [bs((None, *o.shape[1:]), by_pair) for o in outs[:4]] + [fixed(outs[4])]
    if n > 1:
        rest = [sds((384, D), BF), sds((144, D), BF), sds((4, 864, 128), BF), sds((4, 864, 128), BF)]
    else:
        rest = [sds((128, D), BF), sds((384, D), BF)]
    outs, specs = outs + rest, specs + [fixed(o) for o in rest]
    v = pltpu.VMEM
    scratch = [v((ROWS, D), BF)] * 2 + [pltpu.SemaphoreType.DMA((2, NRB))] + [v((2, more, 128), BF)] + [
        v((more, 128), BF)] * 3 + [v((ROWS, 256), F32)] * 2 + [v((more, 256), F32), v((more, 128), F32), v((384, D), F32), v((128, D), F32), v((384, D), F32)]
    hbm = bs(memory_space=pl.ANY)
    given = (near, far, wo_a, wo_b, gain, *before)
    return call(functools.partial(attention_body, pairs=pairs), tuple(outs), scratch, (info, place, nrm, cot, *given),
                [SCALARS] * 2 + [hbm] * 2 + [fixed(g) for g in given], tuple(specs), grid=(n,),
                cost=(n * 12 * 10**9, n * 14 * 10**6), after=after, tick=True, vmem=60)


def mlp_body(info, place, nrm_h, cot_h, near_a, near_b, far_a, far_b, mb, dwo, came, *refs, chunk):
    refs = list(refs)
    last = chunk == 2
    if last:
        gob, dg, db_0, db_1 = refs[:4]
        refs = refs[4:]
    act_h, gm_h, win_h, wout_h, near_o, far_o, db = refs[:7]
    nrm, cot, act, gm, win, wout, dwin, dwout, held, sems, out_sems, piece_sems, weight_sems = refs[7:]
    nb = info[NB]

    def incoming(i):
        rows = pl.ds(pl.multiple_of(i * RB, RB), RB)
        return (pltpu.make_async_copy(nrm_h.at[rows, :], nrm.at[rows, :], sems.at[0, i]),
                pltpu.make_async_copy(cot_h.at[rows, :], cot.at[rows, :], sems.at[1, i]))

    def outgoing(i):
        rows = pl.ds(pl.multiple_of(i * RB, RB), RB)
        return (pltpu.make_async_copy(act.at[rows, :], act_h.at[rows, :], out_sems.at[0, i]),
                pltpu.make_async_copy(gm.at[rows, :], gm_h.at[rows, :], out_sems.at[1, i]))

    def over(body):
        def step(i, carry):
            body(i)
            return carry

        lax.fori_loop(0, nb, step, 0)

    pieces = [pltpu.make_async_copy(p.at[:, chunk], held.at[pl.ds(2 * n, 2)], piece_sems.at[n])
              for n, p in enumerate((near_a, near_b, far_a, far_b))]
    weights = [pltpu.make_async_copy(win, win_h, weight_sems.at[0]), pltpu.make_async_copy(wout, wout_h, weight_sems.at[1])]
    for move in pieces:
        move.start()
    over(lambda i: [move.start() for move in incoming(i)])
    dwin[...] = jnp.zeros_like(dwin)
    dwout[...] = jnp.zeros_like(dwout)
    db[...] = jnp.zeros_like(db)
    for move in pieces:
        move.wait()
    for f in range(8):
        side, at = slot_of(place, f)
        piece = held[4 * side + at]
        for n in range(2):
            win[96 * f : 96 * f + 96, 256 * n : 256 * n + 256] = piece[96 * n : 96 * n + 96]
        for t in range(3):
            part = piece[192 + 80 * t : 272 + 80 * t]
            lanes = slice(256 * t, 256 * t + 256)
            if f == 1:
                wout[0:32, lanes] = part[48:]
            elif f > 1:
                wout[80 * f - 128 : 80 * f - 48, lanes] = part
    for move in weights:
        move.start()

    c0 = 0.7978845608028654
    c1 = 0.044715 * c0

    def step(i, carry):
        rows = pl.ds(pl.multiple_of(i * RB, RB), RB)
        for move in incoming(i):
            move.wait()
        pre = dot_nn(nrm[rows, :], win[...]) + mb[chunk : chunk + 1, :]
        ga = dot_nt(cot[rows, :], wout[...])
        sq = pre * pre
        t = jnp.tanh(pre * (c0 + c1 * sq))
        half = 0.5 * pre
        up = 1.0 + t
        act[rows, :] = (half * up).astype(BF)
        slope = 0.5 * up + half * (1.0 - t * t) * (c0 + 3.0 * c1 * sq)
        gmf = ga * slope
        gm[rows, :] = gmf.astype(BF)
        db[...] += jnp.sum(gmf, axis=0, keepdims=True)
        dwout[...] += dot_tn(act[rows, :], cot[rows, :])
        dwin[...] += dot_tn(gm[rows, :], nrm[rows, :])
        for move in outgoing(i):
            move.start()
        return carry

    lax.fori_loop(0, nb, step, 0)
    full = jnp.transpose(dwin[...]).astype(BF)
    core = place[CORE] == 0
    first, second = slice(80 * chunk, 80 * chunk + 80), slice(48 * chunk, 48 * chunk + 48)
    both = jnp.concatenate([came[...], dwo[0:96, :]])
    zero_rows = jnp.where(core, dwo[first, :], both[first])
    one_rows = jnp.where(core, came[second, :], dwo[240 + 48 * chunk : 288 + 48 * chunk, :])
    if last:
        ob = gob[...]
        qs = dg[:, :HD] + dg[:, HD : 2 * HD]
        ks = dg[:, 2 * HD : 3 * HD] + dg[:, 3 * HD :]
        parts = {}
        for j, units in enumerate((db_0[...], db_1[...], db[...])):
            for cc in range(2):
                own = jnp.where(place[CORE] == cc, units, 0.0)
                done = 0
                for u, n in unit_ranges(cc, j):
                    parts[u] = own[:, done : done + n]
                    done += n
        hidden = jnp.concatenate([parts[u] for u in sorted(parts)], axis=1)
    for f in range(8):

        def fill(ref, f=f):
            for n in range(2):
                ref[96 * n : 96 * n + 96, :] = full[96 * f : 96 * f + 96, 256 * n : 256 * n + 256]
            for t in range(3):
                lanes = slice(256 * t, 256 * t + 256)
                at = 192 + 80 * t
                if f == 0:
                    ref[at : at + 80, :] = zero_rows[:, lanes]
                elif f == 1:
                    ref[at : at + 48, :] = one_rows[:, lanes]
                    ref[at + 48 : at + 80, :] = dwout[0:32, lanes].astype(BF)
                else:
                    ref[at : at + 80, :] = dwout[80 * f - 128 : 80 * f - 48, lanes].astype(BF)
            if last:
                blank = lambda n: jnp.zeros((1, n), F32)
                rows = [hidden[:, 384 * f : 384 * f + 256],
                        jnp.concatenate([hidden[:, 384 * f + 256 : 384 * f + 384], ob[:, 96 * f : 96 * f + 96], blank(32)], axis=1),
                        jnp.concatenate([qs[:, 8 * f : 8 * f + 8], blank(120), ks[:, 8 * f : 8 * f + 8], blank(120)], axis=1)]
                ref[432:448, :] = jnp.concatenate([*rows, jnp.zeros((13, 256), F32)]).astype(BF)

        put(place, near_o, far_o, f, fill)
    for move in weights:
        move.wait()
    over(lambda i: [move.wait() for move in outgoing(i)])


def clamp(i, info, *_):
    return (jnp.minimum(i, info[NB] - 1), 0)


def whole(i, *_):
    return (0, 0)


def whole3(i, *_):
    return (0, 0, 0)


def mlp(info, place, nrm, cot, pieces, mb, dwo, came, vectors, chunk, after=()):
    sds = jax.ShapeDtypeStruct
    rows = 448 if chunk == 2 else 432
    outs = (sds((ROWS, U), BF), sds((ROWS, U), BF), sds((D, U), BF), sds((U, D), BF), sds((4, rows, 256), BF),
            sds((4, rows, 256), BF), sds((1, U), F32))
    hbm = pl.BlockSpec(memory_space=pl.ANY)
    v = pltpu.VMEM
    dma = pltpu.SemaphoreType.DMA
    scratch = [v((ROWS, D), BF)] * 2 + [v((ROWS, U), BF)] * 2 + [v((D, U), BF), v((U, D), BF), v((U, D), F32), v((U, D), F32),
               v((8, 432, 256), BF), dma((2, NRB)), dma((2, NRB)), dma((4,)), dma((2,))]
    given = (mb, dwo, came, *vectors)
    return call(functools.partial(mlp_body, chunk=chunk), outs, scratch, (info, place, nrm, cot, *pieces, *given),
                [SCALARS] * 2 + [hbm] * 6 + [ANYWHERE] * len(given), (hbm,) * 4 + (ANYWHERE,) * 3, vmem=60,
                cost=(10 * 10**9, 18 * 10**6), after=after, tick=True)


def sums_body(info, *refs, n, transposed):
    i = pl.program_id(0)
    lefts, rights, own, other, left, right, held, sems = refs[:n], refs[n : 2 * n], *refs[2 * n :]

    @pl.when(i == 0)
    def _():
        at = 0
        for b in rights:
            k = b.shape[1] if transposed else b.shape[0]
            if transposed:
                right[:, at : at + k] = b[...]
            else:
                right[at : at + k, :] = b[...]
            at += k

    @pl.when(i < info[NB])
    def _():
        at = 0
        for a in lefts:
            left[:, at : at + a.shape[1]] = a[...]
            at += a.shape[1]
        total = dot_nt(left[...], right[...]) if transposed else dot_nn(left[...], right[...])
        held[pl.ds(pl.multiple_of(i * RB, RB), RB), :] = total.astype(BF)

    @pl.when(i >= info[NB])
    def _():
        held[pl.ds(pl.multiple_of(i * RB, RB), RB), :] = jnp.zeros((RB, D), BF)

    move_own = pltpu.make_async_copy(held.at[pl.ds(0, CAN), :], own, sems.at[0])

    @pl.when(i == (CAN - 1) // RB)
    def _():
        move_own.start()

    @pl.when(i == pl.num_programs(0) - 1)
    def _():
        move_other = pltpu.make_async_copy(held.at[pl.ds(pl.multiple_of(info[BASE], 16), CAN), :], other, sems.at[1])
        move_other.start()
        move_own.wait()
        move_other.wait()


def sums(info, lefts, rights, transposed, after=()):
    n = len(lefts)
    bs = pl.BlockSpec
    sds = jax.ShapeDtypeStruct

    def rows_of(a, p):
        if p is None:
            return bs((RB, a.shape[1]), clamp)
        return bs((None, RB, a.shape[2]), lambda i, info: (p, jnp.minimum(i, info[NB] - 1), 0))

    def all_of(b, p):
        return bs(b.shape, whole) if p is None else bs((None, *b.shape[1:]), lambda i, info: (p, 0, 0))

    in_specs = [rows_of(*a) for a in lefts] + [all_of(*b) for b in rights]
    lefts, rights = [a for a, _ in lefts], [b for b, _ in rights]
    k = sum(a.shape[-1] for a in lefts)
    v = pltpu.VMEM
    scratch = [v((RB, k), BF), v((D, k) if transposed else (k, D), BF), v((ROWS, D), BF), pltpu.SemaphoreType.DMA((2,))]
    hbm = bs(memory_space=pl.ANY)
    return call(functools.partial(sums_body, n=n, transposed=transposed), (sds((CAN, D), BF),) * 2, scratch,
                (info, *lefts, *rights), in_specs, (hbm,) * 2, grid=(NRB,), prefetch=1,
                vmem=60, cost=(2 * 2304 * k * D, 2 * 2304 * (k + D)), after=after, tick=True)


def adds_body(*refs, counts, kinds):
    given = list(refs[: sum(counts)])
    outs = list(refs[sum(counts) :])
    for count, kind in zip(counts, kinds):
        terms = [given.pop(0) for _ in range(count)]
        if kind == "four":
            total = terms[0][...].astype(F32) + terms[1][...].astype(F32)
            for i in range(4):
                outs.pop(0)[...] = total[i : i + 1].astype(BF)
        else:
            total = terms[0][...].astype(F32)
            for t in terms[1:]:
                total = total + t[...].astype(F32)
            out = outs.pop(0)
            out[...] = total.astype(out.dtype)


def adds(items, after, vmem=VMEM_MIB):
    sds = jax.ShapeDtypeStruct
    outs = []
    for terms, kind in items:
        a = terms[0]
        shape = (1, *a.shape[1:]) if kind == "four" else a.shape
        outs += [sds(shape, F32 if kind == "float" else BF)] * (4 if kind == "four" else 1)
    args = [t for terms, _ in items for t in terms]
    body = functools.partial(adds_body, counts=[len(t) for t, _ in items], kinds=[k for _, k in items])
    *done, tick = call(body, tuple(outs), [], args, [ANYWHERE] * len(args), cost=(0, 3 * 10**6), after=after, tick=True, vmem=vmem)
    results = []
    for _, kind in items:
        results.append([done.pop(0) for _ in range(4)] if kind == "four" else done.pop(0))
    return *results, tick


def final_body(place, w_in, ln, *refs):
    own, other = refs[:4], refs[4:8]
    gin, gout, gln, gqs, gks, gmb, gob = refs[8:]
    c, f = place[CORE], place[FSDP]
    for cc in range(2):
        sources = [jnp.where(c == cc, a[0], b[0]) for a, b in zip(own, other)]
        for p in range(3):
            for n in range(3):
                at = D * n + 384 * cc + 128 * p
                gin[:, at : at + 128] = sources[0][288 * p + 96 * n : 288 * p + 96 * n + 96, :]
        for j in range(3):
            s = sources[1 + j]
            m = jnp.concatenate([s[0:96], s[96:192]], axis=1)
            done = 0
            for u, n in unit_ranges(cc, j):
                gin[:, 3 * D + u : 3 * D + u + n] = m[:, done : done + n]
                done += n
            for t in range(3):
                lanes = slice(256 * t, 256 * t + 256)
                part = s[192 + 80 * t : 272 + 80 * t]

                @pl.when(f != 1)
                def _():
                    gout[240 * cc + 80 * j : 240 * cc + 80 * j + 80, lanes] = part

                @pl.when(f == 1)
                def _():
                    a, b = 144 * cc + 48 * j, 288 + 96 * cc + 32 * j
                    gout[a : a + 48, lanes] = part[:48]
                    gout[b : b + 32, lanes] = part[48:]
    total = jnp.sum(w_in[...].astype(F32) * gin[...], axis=1, keepdims=True)
    gln[...] = jnp.transpose(jnp.broadcast_to(total, (96, 128)))[0:1, :] / ln[...]
    vec = own[3][0, 432:440, :] + other[3][0, 432:440, :]
    gmb[...] = jnp.concatenate([vec[0:1, :], vec[1:2, :128]], axis=1)
    gob[...] = vec[1:2, 128:224]
    gqs[...] = vec[2:3, 0:8]
    gks[...] = vec[2:3, 128:136]


def final(place, w_in, ln, own, other, after=()):
    sds = jax.ShapeDtypeStruct
    outs = (sds((96, 7 * D), F32), sds((480, D), F32), sds((1, 96), F32), sds((1, 8), F32), sds((1, 8), F32),
            sds((1, 384), F32), sds((1, 96), F32))
    return call(final_body, outs, [], (place, w_in, ln, *own, *other), [SCALARS] + [ANYWHERE] * 10, cost=(0, 10**7), after=after)


def routes():
    places = [(x, c, z, y) for x in range(2) for c in range(2) for z in range(4) for y in range(2)]
    number = lambda x, c, z, y: (x * 2 + c) * 8 + z * 2 + y
    pairs = lambda move: [(number(*p), number(*move(*p))) for p in places]
    out = {
        "core": pairs(lambda x, c, z, y: (x, 1 - c, z, y)),
        "x": pairs(lambda x, c, z, y: (1 - x, c, z, y)),
        "y": pairs(lambda x, c, z, y: (x, c, z, 1 - y)),
        "z1": pairs(lambda x, c, z, y: (x, c, z ^ 1, y)),
        "z2": pairs(lambda x, c, z, y: (x, c, z ^ 2, y)),
        "z3": pairs(lambda x, c, z, y: (x, c, z ^ 3, y)),
    }
    at = lambda n: (n % 8) // 2
    out["z2_up"] = [(a, b) for a, b in out["z2"] if at(a) == 0]
    out["z1_up"] = [(a, b) for a, b in out["z1"] if at(a) % 2 == 0]
    return out


def per_device_paired(
    tokens, lengths, assign, w_in, w_out, ln_scale, q_scale, k_scale, mlp_bias, out_bias, cotangent
):
    way = routes()
    go = lambda v, name: lax.ppermute(v, ("rep", "fsdp"), way[name])
    rep, f = lax.axis_index("rep"), lax.axis_index("fsdp")
    c, y, z = rep % 2, f % 2, f // 2
    cap = tokens.shape[0]
    device = rep * 8 + f
    place = jnp.stack([c, f, y, z, device, device + 8 - 16 * c, rep // 2]).astype(jnp.int32)

    late = lambda v, tick: v if tick is None else v + tick[0].astype(v.dtype)
    first = lambda piece, tick=None: jnp.stack([piece, late(go(piece, "z2"), tick)])
    second = lambda two, tick=None: jnp.concatenate([two, late(go(two, "z1"), tick)])
    third = lambda four: (four, go(four, "y"))
    vectors = (v.reshape(1, -1) for v in (ln_scale, q_scale, k_scale, mlp_bias, out_bias))
    a, wo, tick = pieces_of(place, w_in, w_out)
    a_b, wo_b = go(a, "z2"), go(wo, "z2_up")
    info, vectors = plan(place, lengths, assign, *vectors, after=(tick,))
    vectors = third(second(first(vectors)))
    wo = jnp.where(z == 0, wo, wo_b)
    near = jnp.concatenate([a[:288], a_b[:288], wo])
    b = jnp.concatenate([a[288:], a_b[288:]]).reshape(2, 576, 128)
    own, gob, tick = prepare(info, tokens, cotangent, (near, b, *vectors))
    far = late(go(near, "z1"), tick)
    m, own = split(place, w_in, w_out, own, (far,))
    wo = jnp.where(z % 2 == 0, wo, far[576:])
    near = jnp.concatenate([near[:576], far[:576], wo])
    far = go(near, "y")
    other = go(own, "core")
    b_b = go(b, "z1")
    m_b = go(m, "z2")
    cross = jnp.concatenate([wo, far[PARTS:]])
    nrm, cot, ln, ob, gain, mb, tick = combine(info, place, own, other, *vectors, after=(cross,))
    b = jnp.concatenate([b, late(b_b, tick)])
    wo_a, wo_b, tick = head_rows(place, near, far, go(cross, "x"), (b,))
    wo_b = go(wo_b, "core")
    m = jnp.stack([m, late(m_b, tick)])

    def heads(pairs, g, before, after):
        return attention(info, place, nrm, cot, *g, wo_a, wo_b, gain, pairs, before, after)

    att_0, dqkv_0, w_0, wo_0, dg, dwo, dw, tick = heads((0,), (near, far), (), (b, m))
    m_b = go(m, "z1")
    att_1, dqkv_1, w_1, wo_1, dg, dwo, send, *g_h, tick = heads((1, 2), (b, go(b, "y")), (dw, dwo, dg), (m_b,))
    pieces = (m, m_b, go(m, "y"), go(m_b, "y"))
    came = go(send, "core")
    att, dqkv, ws, wos = (((p, 0), (q, 0), (q, 1)) for p, q in ((att_0, att_1), (dqkv_0, dqkv_1), (w_0, w_1), (wo_0, wo_1)))

    def hidden(j, vectors, after):
        return mlp(info, place, nrm, cot, pieces, mb, dwo, came, vectors, j, after)

    step_y = lambda g: ((g[0], go(g[1], "y")), "four")
    step_z = lambda g: ((g[0], go(g[2], "z1"), go(g[1], "z2"), go(g[3], "z3")), "whole")
    step_x = lambda g: ((g, go(g, "x")), "float")

    *h0, tick = hidden(0, (), (tick,))
    g_h, tick = adds([step_y(g_h)], (tick,), 60)
    *h1, tick = hidden(1, (), (tick,))
    g_h, g_0, tick = adds([step_z(g_h), step_y(h0[4:6])], (tick,))
    *h2, tick = hidden(2, (gob, dg, h0[6], h1[6]), (tick,))
    act, gm, wins, wouts, _, _, _ = zip(h0, h1, h2)
    plain = lambda arrays: tuple((v, None) for v in arrays)

    g_h, g_0, g_1, tick = adds([step_x(g_h), step_z(g_0), step_y(h1[4:6])], (tick,))
    part, away, tick = sums(info, (*att, *plain(act)), (*wos, *plain(wouts)), False, (tick,))
    away = go(away, "core")
    g_0, g_1, g_2, tick = adds([step_x(g_0), step_z(g_1), step_y(h2[4:6])], (tick,))
    part_b, away_b, tick = sums(info, (*dqkv, *plain(gm)), (*ws, *plain(wins)), True, (tick,))
    away_b = go(away_b, "core")
    g_1, g_2, tick = adds([step_x(g_1), step_z(g_2)], (tick,))
    output, tick = last_rows(info, own, part, away, ob, cap, False, (tick,))
    g_2, tick = adds([step_x(g_2)], (tick,))
    grads = (g_h, g_0, g_1, g_2)
    others = [go(g, "core") for g in grads]
    grad_tokens, tick = last_rows(info, own, part_b, away_b, ln, cap, True, (tick,))
    g_win, g_wout, *small = final(place, w_in, ln_scale.astype(F32).reshape(1, 96), grads, others, (tick,))
    return (output, grad_tokens, g_win, g_wout, *(g.reshape(-1) for g in small))


HEADS = 12
epsilon = 1e-06


def layer_norm(values, weight_gain):
    center = values - jnp.mean(values, axis=-1, keepdims=True)
    spread = jnp.mean(center * center, axis=-1, keepdims=True)
    return center * lax.rsqrt(spread + epsilon) * weight_gain


def layout(lengths, assign, device, row_count):
    own = assign == device
    own_sizes = jnp.where(own, lengths, 0)
    own_ends = jnp.cumsum(own_sizes)
    own_starts = own_ends - own_sizes
    position = lax.broadcasted_iota(jnp.int32, (row_count, lengths.shape[0]), 0)
    number = lax.broadcasted_iota(jnp.int32, (row_count, lengths.shape[0]), 1)
    inside = (position >= own_starts[None, :]) & (position < own_ends[None, :])
    filled = jnp.any(inside, axis=1)
    segment = jnp.sum(jnp.where(inside, number, 0), axis=1)
    return (jnp.where(filled, segment, -1), filled)


def contract_rows(left, right):
    return lax.dot_general(
        left, right, (((0,), (0,)), ((), ())), preferred_element_type=jnp.float32
    )


def contract_cols(left, right):
    return lax.dot_general(
        left, right, (((1,), (1,)), ((), ())), preferred_element_type=jnp.float32
    )


def per_device(
    tokens, lengths, assign, w_in, w_out, ln_scale, q_scale, k_scale, mlp_bias, out_bias, cotangent
):
    row_count = tokens.shape[0]
    head_dim = HD
    head_count = HEADS
    width = head_dim * head_count
    factor = head_dim ** (-0.5)
    device = lax.axis_index("rep") * lax.axis_size("fsdp") + lax.axis_index("fsdp")
    segment, filled = layout(lengths, assign, device, row_count)
    allowed = segment[:, None] == segment[None, :]
    params = (w_in, w_out, ln_scale, q_scale, k_scale, mlp_bias, out_bias)
    full = (
        lax.all_gather(params[0], "fsdp", axis=0, tiled=True),
        lax.all_gather(params[1], "fsdp", axis=0, tiled=True),
        lax.all_gather(params[2], "fsdp", axis=0, tiled=True),
        lax.all_gather(params[3], "fsdp", axis=0, tiled=True),
        lax.all_gather(params[4], "fsdp", axis=0, tiled=True),
        lax.all_gather(params[5], "fsdp", axis=0, tiled=True),
        lax.all_gather(params[6], "fsdp", axis=0, tiled=True),
    )
    win_full, wout_full = (full[0], full[1])
    small = [arr.astype(jnp.float32) for arr in full[2:]]
    ln_full, qs_full, ks_full, mb_full, ob_full = small
    inputs = tokens.astype(jnp.float32)
    normed_f, ln_pull = jax.vjp(layer_norm, inputs, ln_full)
    normed = normed_f.astype(jnp.bfloat16)
    joined = jnp.dot(normed, win_full, preferred_element_type=jnp.float32)
    q_pre = joined[:, :width].reshape(row_count, head_count, head_dim)
    k_pre = joined[:, width : 2 * width].reshape(row_count, head_count, head_dim)
    values = joined[:, 2 * width : 3 * width].astype(jnp.bfloat16)
    hidden_pre = joined[:, 3 * width :]
    q_norm, q_pull = jax.vjp(layer_norm, q_pre, qs_full)
    k_norm, k_pull = jax.vjp(layer_norm, k_pre, ks_full)
    queries = q_norm.reshape(row_count, width).astype(jnp.bfloat16)
    keys_all = k_norm.reshape(row_count, width).astype(jnp.bfloat16)

    def head_slice(array, head_index):
        return lax.dynamic_slice_in_dim(array, head_index * head_dim, head_dim, 1)

    def head_scores(head_index):
        raw = (
            contract_cols(head_slice(queries, head_index), head_slice(keys_all, head_index))
            * factor
        )
        return jnp.where(allowed, raw, -1e30)

    def head_forward(head_index):
        scores = head_scores(head_index)
        top = jnp.max(scores, axis=1, keepdims=True)
        expon = jnp.exp(scores - top)
        total = jnp.sum(expon, axis=1, keepdims=True)
        probs = (expon / total).astype(jnp.bfloat16)
        head_out = jnp.dot(
            probs, head_slice(values, head_index), preferred_element_type=jnp.float32
        )
        return (head_out, (top + jnp.log(total))[:, 0])

    head_outs, log_totals = lax.map(head_forward, jnp.arange(head_count))
    attended = jnp.transpose(head_outs, (1, 0, 2)).reshape(row_count, width)
    activated, gelu_pull = jax.vjp(lambda pre, bias: jax.nn.gelu(pre + bias), hidden_pre, mb_full)
    merged = jnp.concatenate([attended, activated], axis=1).astype(jnp.bfloat16)
    result = jnp.dot(merged, wout_full, preferred_element_type=jnp.float32) + ob_full
    output = jnp.where(filled[:, None], inputs + result, 0.0).astype(jnp.bfloat16)
    back = (
        lax.all_gather(params[0], "fsdp", axis=0, tiled=True),
        lax.all_gather(params[1], "fsdp", axis=0, tiled=True),
        lax.all_gather(params[2], "fsdp", axis=0, tiled=True),
        lax.all_gather(params[3], "fsdp", axis=0, tiled=True),
        lax.all_gather(params[4], "fsdp", axis=0, tiled=True),
        lax.all_gather(params[5], "fsdp", axis=0, tiled=True),
        lax.all_gather(params[6], "fsdp", axis=0, tiled=True),
    )
    win_back, wout_back = (back[0], back[1])
    grad_rows = jnp.where(filled[:, None], cotangent.astype(jnp.float32), 0.0)
    grad_low = grad_rows.astype(jnp.bfloat16)
    grad_ob = jnp.sum(grad_rows, axis=0)
    grad_wout = contract_rows(merged, grad_low)
    grad_merged = contract_cols(grad_low, wout_back)
    grad_attended = grad_merged[:, :width].astype(jnp.bfloat16)
    grad_m, grad_mb = gelu_pull(grad_merged[:, width:])

    def head_backward(head_index):
        scores = head_scores(head_index)
        probs_full = jnp.exp(scores - log_totals[head_index][:, None])
        probs = probs_full.astype(jnp.bfloat16)
        grad_head = head_slice(grad_attended, head_index)
        grad_probs = contract_cols(grad_head, head_slice(values, head_index))
        inner = jnp.sum(probs_full * grad_probs, axis=1, keepdims=True)
        grad_scores = (probs_full * (grad_probs - inner)).astype(jnp.bfloat16)
        grad_q = (
            jnp.dot(
                grad_scores, head_slice(keys_all, head_index), preferred_element_type=jnp.float32
            )
            * factor
        )
        grad_k = contract_rows(grad_scores, head_slice(queries, head_index)) * factor
        grad_v = contract_rows(probs, grad_head)
        return (grad_q, grad_k, grad_v)

    grad_qh, grad_kh, grad_vh = lax.map(head_backward, jnp.arange(head_count))
    grad_qn = jnp.transpose(grad_qh, (1, 0, 2))
    grad_kn = jnp.transpose(grad_kh, (1, 0, 2))
    grad_values = jnp.transpose(grad_vh, (1, 0, 2)).reshape(row_count, width)
    grad_q_pre, grad_qs = q_pull(grad_qn)
    grad_k_pre, grad_ks = k_pull(grad_kn)
    grad_joined = jnp.concatenate(
        [
            grad_q_pre.reshape(row_count, width),
            grad_k_pre.reshape(row_count, width),
            grad_values,
            grad_m,
        ],
        axis=1,
    ).astype(jnp.bfloat16)
    grad_win = contract_rows(normed, grad_joined)
    grad_normed = contract_cols(grad_joined, win_back)
    grad_x_norm, grad_ln = ln_pull(grad_normed)
    grad_tokens = (grad_rows + grad_x_norm).astype(jnp.bfloat16)
    grads = (grad_win, grad_wout, grad_ln, grad_qs, grad_ks, grad_mb, grad_ob)
    shares = (
        lax.psum_scatter(grads[0], "fsdp", scatter_dimension=0, tiled=True),
        lax.psum_scatter(grads[1], "fsdp", scatter_dimension=0, tiled=True),
        lax.psum_scatter(grads[2], "fsdp", scatter_dimension=0, tiled=True),
        lax.psum_scatter(grads[3], "fsdp", scatter_dimension=0, tiled=True),
        lax.psum_scatter(grads[4], "fsdp", scatter_dimension=0, tiled=True),
        lax.psum_scatter(grads[5], "fsdp", scatter_dimension=0, tiled=True),
        lax.psum_scatter(grads[6], "fsdp", scatter_dimension=0, tiled=True),
    )
    shares = lax.psum(
        (shares[0], shares[1], shares[2], shares[3], shares[4], shares[5], shares[6]), "rep"
    )
    return (
        output,
        grad_tokens,
        shares[0],
        shares[1],
        shares[2],
        shares[3],
        shares[4],
        shares[5],
        shares[6],
    )


def solution(mesh):
    in_specs = (
        P(("rep", "fsdp"), None),
        P(),
        P(),
        P("fsdp", None),
        P("fsdp", None),
        P("fsdp"),
        P("fsdp"),
        P("fsdp"),
        P("fsdp"),
        P("fsdp"),
        P(("rep", "fsdp"), None),
    )
    out_specs = (
        P(("rep", "fsdp"), None),
        P(("rep", "fsdp"), None),
        P("fsdp", None),
        P("fsdp", None),
        P("fsdp"),
        P("fsdp"),
        P("fsdp"),
        P("fsdp"),
        P("fsdp"),
    )
    paired = dict(mesh.shape) == {"rep": 4, "fsdp": 8}
    return jax.shard_map(
        per_device_paired if paired else per_device, mesh=mesh, in_specs=in_specs, out_specs=out_specs, check_vma=False
    )
```

```python
import functools

import jax
import jax.numpy as jnp
from jax import lax
from jax.experimental import pallas as pl
from jax.experimental.pallas import tpu as pltpu
from jax.sharding import PartitionSpec as P

D = 768
HD = 64
SMALL = 196
BIG = 1024
BLK = 208
CAN = 7 * BLK
ROWS = 3072
ROOM = 3584
RB = 512
NRB = ROWS // RB
U = 512
EPS = 1e-06
BF = jnp.bfloat16
F32 = jnp.float32
VMEM_MIB = 34
ANYWHERE = pl.BlockSpec(memory_space=pltpu.VMEM)
TICK = jax.ShapeDtypeStruct((1,), F32)
SCALARS = pl.BlockSpec(memory_space=pltpu.SMEM)


def dot_nn(a, b):
    return lax.dot_general(a, b, (((1,), (0,)), ((), ())), preferred_element_type=F32)


def dot_nt(a, b):
    return lax.dot_general(a, b, (((1,), (1,)), ((), ())), preferred_element_type=F32)


def dot_tn(a, b):
    return lax.dot_general(a, b, (((0,), (0,)), ((), ())), preferred_element_type=F32)


def two_parts(x):
    hi = x.astype(BF)
    return hi, (x - hi.astype(F32)).astype(BF)


def call(body, out_shape, scratch, args, in_specs, out_specs=None, grid=None, prefetch=0, cost=None, after=(), tick=False, alias=None, vmem=VMEM_MIB):
    if after:
        inner, n, skip = body, len(args), len(after)

        def body(*refs):
            inner(*refs[:n], *refs[n + skip :])

        args = (*args, *after)
        in_specs = [*in_specs] + [pl.BlockSpec(memory_space=pl.ANY)] * skip
    params = pltpu.CompilerParams(vmem_limit_bytes=vmem * 2**20)
    if out_specs is None:
        out_specs = jax.tree.map(lambda _: ANYWHERE, out_shape)
    if tick:
        many = isinstance(out_shape, tuple)
        out_shape = (*out_shape, TICK) if many else (out_shape, TICK)
        out_specs = (*out_specs, SCALARS) if many else (out_specs, SCALARS)
        untold, place = body, len(args) + len(out_shape) - 1

        def body(*refs):
            refs[place][0] = jnp.float32(0)
            untold(*refs[:place], *refs[place + 1 :])

    spec = pltpu.PrefetchScalarGridSpec(
        num_scalar_prefetch=prefetch,
        grid=grid or (),
        in_specs=in_specs,
        out_specs=out_specs,
        scratch_shapes=scratch,
    )
    estimate = None if cost is None else pl.CostEstimate(flops=20 * cost[0], bytes_accessed=20 * cost[1], transcendentals=0)
    return pl.pallas_call(body, grid_spec=spec, out_shape=out_shape, compiler_params=params, cost_estimate=estimate, input_output_aliases=alias or {})(*args)


NB, BLOCKS_A, LARGE_A, SMALL_A, BASE, BLOCKS_B, LARGE_B, SMALL_B, BEFORE = range(9)
CORE, FSDP, Y, Z, SELF, MATE, X = range(7)


def unit_ranges(c, j):
    first = [(96 * c + 32 * j, 32)]
    return first + [(192 + 480 * s + 240 * c + 80 * j, 80) for s in range(6)]


def pieces_body(place, w_in, w_out, heads, wo, sems):
    own = 384 * place[CORE]
    lanes = lambda at: pl.ds(pl.multiple_of(own + at, 128), 128)
    rows = lambda at: pl.ds(at, 96)
    half = pl.ds(pl.multiple_of(240 * place[X], 16), 240)
    moves = []
    for n in range(3):
        moves.append((w_out.at[half, lanes(128 * n)], wo.at[pl.ds(240 * n, 240), :]))
        for p in range(3):
            moves.append((w_in.at[:, lanes(D * n + 128 * p)], heads.at[rows(288 * p + 96 * n), :]))
    moves = [pltpu.make_async_copy(p, q, sems.at[i]) for i, (p, q) in enumerate(moves)]
    for move in moves:
        move.start()
    for move in moves:
        move.wait()


def pieces_of(place, w_in, w_out):
    sds = jax.ShapeDtypeStruct
    hbm = pl.BlockSpec(memory_space=pl.ANY)
    return call(pieces_body, (sds((864, 128), BF), sds((720, 128), BF)), [pltpu.SemaphoreType.DMA((12,))],
                (place, w_in, w_out), [SCALARS, hbm, hbm], (ANYWHERE,) * 2, vmem=60, cost=(0, 2 * 10**6), tick=True)


def plan_body(place, lengths, assign, ln, qs, ks, mb, ob, info, params):
    def count(i, carry):
        before, small_a, large_a, small_b, large_b = carry
        large = (lengths[i] == BIG).astype(jnp.int32)
        me = (assign[i] == place[SELF]).astype(jnp.int32)
        mate = (assign[i] == place[MATE]).astype(jnp.int32)
        before = jnp.where(me * large == 1, small_a, before)
        return before, small_a + me * (1 - large), large_a + me * large, small_b + mate * (1 - large), large_b + mate * large

    zero = jnp.int32(0)
    before, small_a, large_a, small_b, large_b = lax.fori_loop(0, lengths.shape[0], count, (zero,) * 5)
    blocks_a = jnp.where(large_a > 0, 7, small_a)
    blocks_b = jnp.where(large_b > 0, 7, small_b)
    info[NB] = (BLK * (blocks_a + blocks_b) + RB - 1) // RB
    info[BLOCKS_A], info[LARGE_A], info[SMALL_A] = blocks_a, large_a, small_a
    info[BASE] = BLK * blocks_a
    info[BLOCKS_B], info[LARGE_B], info[SMALL_B] = blocks_b, large_b, small_b
    info[BEFORE] = jnp.where(large_a > 0, before, small_a)
    params[...] = jnp.zeros_like(params)
    params[0:1, :96] = ln[...]
    params[1:2, :8] = qs[...]
    params[2:3, :8] = ks[...]
    params[3:4, :96] = ob[...]
    for n in range(3):
        params[4 + n : 5 + n, :] = mb[:, 128 * n : 128 * n + 128]


def plan(place, lengths, assign, *small, after):
    sds = jax.ShapeDtypeStruct
    return call(plan_body, (sds((16,), jnp.int32), sds((16, 128), BF)), [], (place, lengths, assign, *small),
                [SCALARS] * 3 + [ANYWHERE] * 5, (SCALARS, ANYWHERE), vmem=60, cost=(0, 10**5), after=after)


def split_body(place, w_in, w_out, own, m, own_o):
    c, f = place[CORE], place[FSDP]
    for cc in range(2):

        @pl.when(c == cc)
        def _():
            for j in range(3):
                cols = [w_in[:, 3 * D + u : 3 * D + u + n] for u, n in unit_ranges(cc, j)]
                half = jnp.concatenate(cols, axis=1)
                m[j, 0:96, :] = half[:, :256]
                m[j, 96:192, :] = half[:, 256:]
                for t in range(3):
                    lanes = slice(256 * t, 256 * t + 256)
                    at = 192 + 80 * t

                    @pl.when(f != 1)
                    def _():
                        m[j, at : at + 80, :] = w_out[240 * cc + 80 * j : 240 * cc + 80 * j + 80, lanes]

                    @pl.when(f == 1)
                    def _():
                        a, b = 144 * cc + 48 * j, 288 + 96 * cc + 32 * j
                        m[j, at : at + 48, :] = w_out[a : a + 48, lanes]
                        m[j, at + 48 : at + 80, :] = w_out[b : b + 32, lanes]


def split(place, w_in, w_out, own, after):
    sds = jax.ShapeDtypeStruct
    outs = (sds((3, 432, 256), BF), sds(own.shape, BF))
    hbm = pl.BlockSpec(memory_space=pl.ANY)
    return call(split_body, outs, [], (place, w_in, w_out, own), [SCALARS] + [ANYWHERE] * 2 + [hbm], (ANYWHERE, hbm),
                cost=(0, 4 * 10**6), after=after, alias={3: 1})


def slot_of(place, f):
    dz = place[Z] ^ (f >> 1)
    return place[Y] ^ (f & 1), ((dz & 1) << 1) | (dz >> 1)


def taken(place, near, far, f, rows):
    side, at = slot_of(place, f)
    return jnp.where(side == 0, near[at, rows, :], far[at, rows, :])


def put(place, near, far, f, fill):
    side, at = slot_of(place, f)

    @pl.when(side == 0)
    def _():
        fill(near.at[at])

    @pl.when(side != 0)
    def _():
        fill(far.at[at])


def each_image(info, move):
    start = SMALL * info[BEFORE]

    @pl.when(info[LARGE_A] == 1)
    def _():
        for t in range(5):
            move(BLK * t, start + BLK * t, min(BLK, BIG - BLK * t))

    def small(i, carry):
        large = BIG * info[LARGE_A]
        move(pl.multiple_of(large + BLK * i, 16), SMALL * i + jnp.where(i >= info[BEFORE], large, 0), SMALL)
        return carry

    lax.fori_loop(0, info[SMALL_A], small, 0)


WINDOW = BLK + 16


def window_of(slot):
    first = (slot // 16) * 16
    return pl.ds(pl.multiple_of(first, 16), WINDOW), slot - first


def prepare_body(info, tokens, cot, out, gob_o, pad_x, pad_g):
    cap = tokens.shape[0]
    for pad, held in ((pad_x, tokens), (pad_g, cot)):
        pad[0:cap, :] = held[...]
        pad[cap:, :] = jnp.zeros((pad.shape[0] - cap, D), BF)
    out[...] = jnp.zeros_like(out)
    gob_o[...] = jnp.zeros_like(gob_o)
    apart = lax.broadcasted_iota(jnp.int32, (BLK, WINDOW), 1) - lax.broadcasted_iota(jnp.int32, (BLK, WINDOW), 0)
    row = lax.broadcasted_iota(jnp.int32, (BLK, WINDOW), 0)

    def move(to, slot, n):
        window, shift = window_of(slot)
        pick = ((apart == shift) & (row < n)).astype(BF)
        rows = pl.ds(to, BLK)
        g = dot_nn(pick, pad_g[window, :])
        out[0, rows, :] = dot_nn(pick, pad_x[window, :]).astype(BF)
        out[1, rows, :] = g.astype(BF)
        gob_o[...] += jnp.sum(g, axis=0, keepdims=True)

    each_image(info, move)


def prepare(info, tokens, cot, after):
    sds = jax.ShapeDtypeStruct
    pad = pltpu.VMEM((CAN + 16, D), BF)
    return call(prepare_body, (sds((2, CAN, D), BF), sds((1, D), F32)), [pad, pad], (info, tokens, cot),
                [SCALARS] + [ANYWHERE] * 2, vmem=60, cost=(10**9, 9 * 10**6), after=after, tick=True)


def combine_body(info, place, own, other, near, far, nrm, cot, ln_o, ob_o, gain_o, mb_o, x, y, g, zero, sems, zero_sems):
    count_a, count_b = info[BLOCKS_A], info[BLOCKS_B]

    def copies(source, i, t):
        rows = pl.ds(pl.multiple_of(i * BLK, 16), BLK)
        to = pl.ds(pl.multiple_of(t * BLK, 16), BLK)
        return (lambda: pltpu.make_async_copy(source.at[0, rows, :], x.at[t], sems.at[0, t]),
                lambda: pltpu.make_async_copy(source.at[1, rows, :], g.at[t], sems.at[1, t]),
                lambda: pltpu.make_async_copy(g.at[t], cot.at[to, :], sems.at[3, t]),
                lambda: pltpu.make_async_copy(y.at[t], nrm.at[to, :], sems.at[2, t]))

    def over(body):
        def step_a(i, carry):
            body(i, *copies(own, i, i))
            return carry

        def step_b(i, carry):
            body(count_a + i, *copies(other, i, count_a + i))
            return carry

        lax.fori_loop(0, count_a, step_a, 0)
        lax.fori_loop(0, count_b, step_b, 0)

    def begin(t, to_x, to_g, to_cot, to_nrm):
        to_x().start()
        to_g().start()

    over(begin)
    zero[...] = jnp.zeros_like(zero)
    end = pl.ds(pl.multiple_of((count_a + count_b) * BLK, 16), RB)
    blanks = [pltpu.make_async_copy(zero, out.at[end, :], zero_sems.at[n]) for n, out in enumerate((nrm, cot))]
    for move in blanks:
        move.start()
    small = [taken(place, near, far, f, slice(0, 16)).astype(F32) for f in range(8)]
    ln = jnp.concatenate([s[0:1, :96] for s in small], axis=1)
    ln_o[...] = ln
    ob_o[...] = jnp.concatenate([s[3:4, :96] for s in small], axis=1)
    gain_o[...] = jnp.concatenate(([s[1:2, :8] for s in small] * 2) + ([s[2:3, :8] for s in small] * 2), axis=1)
    mb = jnp.concatenate([s[4 + n : 5 + n, :] for s in small for n in range(3)], axis=1)
    for j in range(3):
        rows = [jnp.concatenate([mb[:, u : u + n] for u, n in unit_ranges(cc, j)], axis=1) for cc in range(2)]
        mb_o[j : j + 1, :] = jnp.where(place[CORE] == 0, rows[0], rows[1])

    def norm(t, to_x, to_g, to_cot, to_nrm):
        to_x().wait()
        v = x[t].astype(F32)
        center = v - jnp.mean(v, axis=1, keepdims=True)
        spread = jnp.mean(center * center, axis=1, keepdims=True)
        y[t] = (center * lax.rsqrt(spread + EPS) * ln).astype(BF)
        to_nrm().start()
        to_g().wait()
        to_cot().start()

    over(norm)

    def finish(t, to_x, to_g, to_cot, to_nrm):
        to_cot().wait()
        to_nrm().wait()

    over(finish)
    for move in blanks:
        move.wait()


def combine(info, place, own, other, near, far, after=()):
    sds = jax.ShapeDtypeStruct
    outs = (sds((ROOM, D), BF),) * 2 + (sds((1, D), F32),) * 2 + (sds((1, 256), F32), sds((3, U), F32))
    hbm = pl.BlockSpec(memory_space=pl.ANY)
    v = pltpu.VMEM
    most = 2 * CAN // BLK
    scratch = [v((most, BLK, D), BF)] * 3 + [v((RB, D), BF), pltpu.SemaphoreType.DMA((4, most)), pltpu.SemaphoreType.DMA((2,))]
    return call(combine_body, outs, scratch, (info, place, own, other, near, far), [SCALARS] * 2 + [hbm] * 2 + [ANYWHERE] * 2,
                (hbm,) * 2 + (ANYWHERE,) * 4, vmem=60, cost=(0, 18 * 10**6), after=after, tick=True)


def rows_body(info, x_h, a_h, b_h, vector, out, x, a, b, held, pad, sems, *, gradient):
    moves = []
    for i in range(CAN // BLK):
        rows = pl.ds(i * BLK, BLK)
        pairs = [(x_h.at[0, rows, :], x.at[0, rows, :]), (a_h.at[rows, :], a.at[rows, :]), (b_h.at[rows, :], b.at[rows, :])]
        if gradient:
            pairs.append((x_h.at[1, rows, :], x.at[1, rows, :]))
        moves.append([pltpu.make_async_copy(p, q, sems.at[n, i]) for n, (p, q) in enumerate(pairs)])
        for move in moves[-1]:
            move.start()
    pad[...] = jnp.zeros_like(pad)
    for i in range(CAN // BLK):
        for move in moves[i]:
            move.wait()
        rows = pl.ds(i * BLK, BLK)
        v = x[0, rows, :].astype(F32)
        total = a[rows, :].astype(F32) + b[rows, :].astype(F32)
        if gradient:
            center = v - jnp.mean(v, axis=1, keepdims=True)
            r = lax.rsqrt(jnp.mean(center * center, axis=1, keepdims=True) + EPS)
            xh = center * r
            g = total * vector[...]
            gx = r * (g - jnp.mean(g, axis=1, keepdims=True) - xh * jnp.mean(g * xh, axis=1, keepdims=True))
            held[rows, :] = (x[1, rows, :].astype(F32) + gx).astype(BF)
        else:
            held[rows, :] = (v + (total + vector[...])).astype(BF)
    apart = lax.broadcasted_iota(jnp.int32, (WINDOW, BLK), 0) - lax.broadcasted_iota(jnp.int32, (WINDOW, BLK), 1)
    col = lax.broadcasted_iota(jnp.int32, (WINDOW, BLK), 1)

    def move(at, slot, n):
        window, shift = window_of(slot)
        pick = ((apart == shift) & (col < n)).astype(BF)
        pad[window, :] += dot_nn(pick, held[pl.ds(at, BLK), :]).astype(BF)

    each_image(info, move)
    out[...] = pad[: out.shape[0], :]


def last_rows(info, x, a, b, vector, cap, gradient, after=()):
    v = pltpu.VMEM
    scratch = [v((2, CAN, D), BF), v((CAN, D), BF), v((CAN, D), BF), v((CAN, D), BF), v((CAN + 16, D), BF),
               pltpu.SemaphoreType.DMA((4, CAN // BLK))]
    hbm = pl.BlockSpec(memory_space=pl.ANY)
    return call(functools.partial(rows_body, gradient=gradient), jax.ShapeDtypeStruct((cap, D), BF), scratch, (info, x, a, b, vector),
                [SCALARS] + [hbm] * 3 + [ANYWHERE], cost=(4 * 10**9, 12 * 10**6), after=after, tick=True)


def head_rows_body(place, near, far, cross, mine, theirs):
    rows = slice(PARTS, PARTS + 720)
    swap_y, swap_x, second_core = place[Y] != 0, place[X] != 0, place[CORE] != 0
    pick = lambda swap, a, b: (jnp.where(swap, b, a), jnp.where(swap, a, b))
    own = pick(swap_y, near[rows, :], far[rows, :])
    came = pick(swap_y, cross[0:720, :], cross[720:, :])
    (low, high), (low_1, high_1) = (pick(swap_x, a, b) for a, b in zip(own, came))
    for n in range(3):
        lanes = slice(128 * n, 128 * n + 128)
        at = 240 * n
        first = jnp.concatenate([low[at : at + 240], high[at : at + 144]])
        second = jnp.concatenate([high[at + 144 : at + 240], low_1[at : at + 240], high_1[at : at + 48]])
        mine[:, lanes], theirs[:, lanes] = pick(second_core, first, second)


def head_rows(place, near, far, cross, after):
    sds = jax.ShapeDtypeStruct
    return call(head_rows_body, (sds((384, 384), BF),) * 2, [], (place, near, far, cross), [SCALARS] + [ANYWHERE] * 3, cost=(0, 10**6),
                after=after, tick=True)


PARTS = 4 * 288


def attention_body(info, place, nrm_h, cot_h, near, far, wo_a, wo_b, gain, *refs, pairs):
    refs = list(refs)
    last = len(pairs) > 1
    if last:
        dw_0, dwo_0, dg_0 = refs[:3]
        refs = refs[3:]
    att_o, dqkv_o, w_o, wo_o, dg_o, dwo_o = refs[:6]
    if last:
        dwo_send, near_o, far_o = refs[6:9]
        refs = refs[9:]
    else:
        dw_o = refs[6]
        refs = refs[7:]
    nrm, cot, sems, vv, qp, kp, do, xh, rr, dqk, dv, dw, dwo, dws = refs
    step = pl.program_id(0)
    nb = info[NB]

    def incoming(i):
        rows = pl.ds(pl.multiple_of(i * RB, RB), RB)
        return (pltpu.make_async_copy(nrm_h.at[rows, :], nrm.at[rows, :], sems.at[0, i]),
                pltpu.make_async_copy(cot_h.at[rows, :], cot.at[rows, :], sems.at[1, i]))

    @pl.when(step == 0)
    def _():
        def begin(i, carry):
            for move in incoming(i):
                move.start()
            return carry

        lax.fori_loop(0, nb, begin, 0)

        @pl.when(nb % 2 == 1)
        def _():
            rest = pl.ds(pl.multiple_of(nb * RB, RB), RB)
            nrm[rest, :] = jnp.zeros((RB, D), BF)
            cot[rest, :] = jnp.zeros((RB, D), BF)

        if last:
            dg_o[...] = dg_0[...]
        else:
            dg_o[...] = jnp.zeros_like(dg_o)

    lane = lax.broadcasted_iota(jnp.int32, (1, 128), 1)
    first = lane < HD
    same = lax.broadcasted_iota(jnp.int32, (256, 256), 0) // HD == lax.broadcasted_iota(jnp.int32, (256, 256), 1) // HD
    mean_m = jnp.where(same, 1.0 / HD, 0.0).astype(BF)
    sum_m = jnp.where(same[:, :128] | same[:, 128:], 1.0, 0.0).astype(BF)
    c_exp = 1.4426950408889634 / 8.0
    masks = [jnp.where(first, 1.0, 0.0).astype(BF), jnp.where(first, 0.0, 1.0).astype(BF)]

    for f in range(8):
        side, at = slot_of(place, f)
        if pairs[0] == 0:
            rows = pl.ds(pl.multiple_of(288 * at, 16), 288)
            piece = jnp.where(side == 0, near[rows, :], far[rows, :])
        else:
            rows = pl.ds(pl.multiple_of(288 * step, 16), 288)
            piece = jnp.where(side == 0, near[at, rows, :], far[at, rows, :])
        for n in range(3):
            w_o[96 * f : 96 * f + 96, 128 * n : 128 * n + 128] = piece[96 * n : 96 * n + 96]
    rows = pl.ds(pl.multiple_of(128 * (pairs[0] + step), 16), 128)
    mine, theirs = wo_a[rows, :], wo_b[rows, :]
    wo_o[:, :384] = jnp.where(place[CORE] == 0, mine, theirs)
    wo_o[:, 384:] = jnp.where(place[CORE] == 0, theirs, mine)

    def mean(x):
        return dot_nn(x.astype(BF), mean_m)

    def project(i, carry):
        @pl.when(step == 0)
        def _():
            for move in incoming(2 * i):
                move.wait()

            @pl.when(2 * i + 1 < nb)
            def _():
                for move in incoming(2 * i + 1):
                    move.wait()

        rows = pl.ds(pl.multiple_of(i * 2 * RB, 2 * RB), 2 * RB)
        y = dot_nn(nrm[rows, :], w_o[...])
        qk, v = y[:, :256], y[:, 256:]
        center = qk - mean(qk)
        r = lax.rsqrt(mean(center * center) + EPS)
        x = center * r
        xh[rows, :] = x
        rr[rows, :] = r
        qk = (x * gain[...]).astype(BF)
        qp[rows, :] = qk[:, :128]
        kp[rows, :] = qk[:, 128:]
        vv[0, rows, :] = jnp.where(first, v, 1.0).astype(BF)
        vv[1, rows, :] = jnp.where(first, 1.0, v).astype(BF)
        do[rows, :] = dot_nt(cot[rows, :], wo_o[...]).astype(BF)
        dqk[rows, :] = jnp.zeros((2 * RB, 256), F32)
        dv[rows, :] = jnp.zeros((2 * RB, 128), F32)
        att_o[rows, :] = jnp.zeros((2 * RB, 128), BF)
        return carry

    lax.fori_loop(0, (nb + 1) // 2, project, 0)

    def blocks(items, masked, add):
        both = [(i, h) for i in range(len(items)) for h in range(2)]
        plain = [qp[it[0], :] for it in items]
        ql = [[q * m for m in masks] for q in plain]
        kl = [kp[it[1], :] for it in items]
        vl = [[vv[h, it[1], :] for h in range(2)] for it in items]
        grads = [do[it[0], :].astype(F32) for it in items]
        p, pb, xs = {}, {}, {}
        for i, h in both:
            e = jnp.exp2(dot_nt(ql[i][h], kl[i]) * c_exp)
            if masked:
                e = jnp.where(lax.broadcasted_iota(jnp.int32, e.shape, 1) < SMALL, e, 0.0)
            p[i, h] = e
            pb[i, h] = e.astype(BF)
        for i, h in both:
            xs[i, h] = dot_nn(pb[i, h], vl[i][h])
        outs, scaled, lefts = [], [], {}
        for i in range(len(items)):
            total = jnp.where(first, pltpu.roll(xs[i, 0], HD, 1), pltpu.roll(xs[i, 1], HD, 1))
            inverse = 1.0 / total
            out = jnp.where(first, xs[i, 0], xs[i, 1]) * inverse
            outs.append(out.astype(BF))
            hi, lo = two_parts(grads[i] * out)
            inner = dot_nn(jnp.concatenate([hi, lo], axis=1), sum_m) * inverse
            s = (grads[i] * inverse).astype(BF)
            scaled.append(s)
            sf = s.astype(F32)
            hi, lo = two_parts(inner)
            hi, lo = pltpu.roll(hi.astype(F32), HD, 1), pltpu.roll(lo.astype(F32), HD, 1)
            for h in range(2):
                own = first if h == 0 else jnp.logical_not(first)
                at = HD * (1 - h)
                side = jnp.where(lane == at, -hi, jnp.where(lane == at + 1, -lo, 0.0))
                lefts[i, h] = jnp.where(own, sf, side).astype(BF)
        ds = {}
        for i, h in both:
            ds[i, h] = (p[i, h] * dot_nt(lefts[i, h], vl[i][h])).astype(BF)
        dq = {t: dot_nn(ds[t], kl[t[0]]) for t in both}
        turned = [(jnp.transpose(a.astype(F32)).astype(BF), jnp.transpose(b.astype(F32)).astype(BF)) for a, b in zip(plain, scaled)]
        dk = {(i, h): dot_nn(turned[i][0][HD * h : HD * h + HD], ds[i, h]) for i, h in both}
        dvs = {(i, h): dot_nn(turned[i][1][HD * h : HD * h + HD], pb[i, h]) for i, h in both}
        for i, (q_rows, k_rows) in enumerate(items):
            att_o[q_rows, :] = outs[i]
            dqk[q_rows, :128] = jnp.where(first, dq[i, 0], dq[i, 1])
            new_k = jnp.transpose(jnp.concatenate([dk[i, 0], dk[i, 1]], axis=0))
            new_v = jnp.transpose(jnp.concatenate([dvs[i, 0], dvs[i, 1]], axis=0))
            if add:
                dqk[k_rows, 128:] += new_k
                dv[k_rows, :] += new_v
            else:
                dqk[k_rows, 128:] = new_k
                dv[k_rows, :] = new_v

    count_a, count_b = info[SMALL_A], info[SMALL_B]

    def small_rows(i):
        row_a = BIG * info[LARGE_A] + BLK * i
        row_b = info[BASE] + BIG * info[LARGE_B] + BLK * (i - count_a)
        row = jnp.where(i < count_a, row_a, jnp.where(i < count_a + count_b, row_b, ROWS))
        return pl.ds(pl.multiple_of(row, 16), BLK)

    def smalls(i, carry):
        rows = [small_rows(2 * i + n) for n in range(2)]
        blocks([(r, r) for r in rows], True, False)
        return carry

    lax.fori_loop(0, (count_a + count_b + 1) // 2, smalls, 0)

    def large_block(i, carry):
        base = jnp.where(i < 2 * info[LARGE_A], 0, info[BASE])
        k_rows = pl.ds(pl.multiple_of(base, 16), BIG)
        blocks([(pl.ds(pl.multiple_of(base + (i & 1) * 512, 16), 512), k_rows)], False, True)
        return carry

    lax.fori_loop(0, 2 * (info[LARGE_A] + info[LARGE_B]), large_block, 0)

    dw[...] = jnp.zeros_like(dw)
    dwo[...] = jnp.zeros_like(dwo)

    def pull(i):
        rows = pl.ds(pl.multiple_of(i * 2 * RB, 2 * RB), 2 * RB)
        g_out = dqk[rows, :]
        x = xh[rows, :]
        dg_o[...] += 0.125 * jnp.sum(g_out * x, axis=0, keepdims=True)
        g = g_out * (0.125 * gain[...])
        g = rr[rows, :] * (g - mean(g) - x * mean(g * x))
        dqkv_o[rows, :] = jnp.concatenate([g.astype(BF), dv[rows, :].astype(BF)], axis=1)

    def weigh(i):
        rows = pl.ds(pl.multiple_of(i * 2 * RB, 2 * RB), 2 * RB)
        dw[...] += dot_tn(dqkv_o[rows, :], nrm[rows, :])
        dwo[...] += dot_tn(att_o[rows, :], cot[rows, :])

    def finish(i, carry):
        weigh(i - 1)
        pull(i)
        return carry

    pull(0)
    lax.fori_loop(1, (nb + 1) // 2, finish, 0)
    weigh((nb + 1) // 2 - 1)
    if not last:
        dwo_o[...] = dwo[...].astype(BF)
        dw_o[...] = dw[...].astype(BF)
        return
    dwo_o[pl.ds(pl.multiple_of(128 + 128 * step, 16), 128), :] = dwo[...].astype(BF)

    @pl.when(step == 0)
    def _():
        dws[...] = dw[...]
        dwo_o[0:128, :] = dwo_0[...]

    @pl.when(step == len(pairs) - 1)
    def _():
        dwo_send[...] = jnp.where(place[CORE] == 0, dwo_o[240:384, :], dwo_o[96:240, :])
        full = [jnp.transpose(d).astype(BF) for d in (dw_0[...].astype(F32), dws[...], dw[...])]
        for f in range(8):

            def fill(ref, f=f):
                for q in range(3):
                    for n in range(3):
                        at = 288 * q + 96 * n
                        ref[at : at + 96, :] = full[q][96 * f : 96 * f + 96, 128 * n : 128 * n + 128]

            put(place, near_o, far_o, f, fill)


def attention(info, place, nrm, cot, near, far, wo_a, wo_b, gain, pairs, before=(), after=()):
    sds = jax.ShapeDtypeStruct
    bs = pl.BlockSpec
    n, more = len(pairs), ROWS + 256
    outs = [sds((n, more, 128), BF), sds((n, ROWS, 384), BF), sds((n, D, 384), BF), sds((n, 128, D), BF), sds((1, 256), F32)]
    by_pair = lambda p: (p, 0, 0)
    fixed = lambda a: bs(a.shape, lambda p: (0,) * len(a.shape))
    specs = [bs((None, *o.shape[1:]), by_pair) for o in outs[:4]] + [fixed(outs[4])]
    if n > 1:
        rest = [sds((384, D), BF), sds((144, D), BF), sds((4, 864, 128), BF), sds((4, 864, 128), BF)]
    else:
        rest = [sds((128, D), BF), sds((384, D), BF)]
    outs, specs = outs + rest, specs + [fixed(o) for o in rest]
    v = pltpu.VMEM
    scratch = [v((ROWS, D), BF)] * 2 + [pltpu.SemaphoreType.DMA((2, NRB))] + [v((2, more, 128), BF)] + [
        v((more, 128), BF)] * 3 + [v((ROWS, 256), F32)] * 2 + [v((more, 256), F32), v((more, 128), F32), v((384, D), F32), v((128, D), F32), v((384, D), F32)]
    hbm = bs(memory_space=pl.ANY)
    given = (near, far, wo_a, wo_b, gain, *before)
    return call(functools.partial(attention_body, pairs=pairs), tuple(outs), scratch, (info, place, nrm, cot, *given),
                [SCALARS] * 2 + [hbm] * 2 + [fixed(g) for g in given], tuple(specs), grid=(n,),
                cost=(n * 12 * 10**9, n * 14 * 10**6), after=after, tick=True, vmem=60)


def mlp_body(info, place, nrm_h, cot_h, near_a, near_b, far_a, far_b, mb, dwo, came, *refs, chunk):
    refs = list(refs)
    last = chunk == 2
    if last:
        gob, dg, db_0, db_1 = refs[:4]
        refs = refs[4:]
    act_h, gm_h, win_h, wout_h, near_o, far_o, db = refs[:7]
    nrm, cot, act, gm, win, wout, dwin, dwout, held, sems, out_sems, piece_sems, weight_sems = refs[7:]
    nb = info[NB]

    def incoming(i):
        rows = pl.ds(pl.multiple_of(i * RB, RB), RB)
        return (pltpu.make_async_copy(nrm_h.at[rows, :], nrm.at[rows, :], sems.at[0, i]),
                pltpu.make_async_copy(cot_h.at[rows, :], cot.at[rows, :], sems.at[1, i]))

    def outgoing(i):
        rows = pl.ds(pl.multiple_of(i * RB, RB), RB)
        return (pltpu.make_async_copy(act.at[rows, :], act_h.at[rows, :], out_sems.at[0, i]),
                pltpu.make_async_copy(gm.at[rows, :], gm_h.at[rows, :], out_sems.at[1, i]))

    def over(body):
        def step(i, carry):
            body(i)
            return carry

        lax.fori_loop(0, nb, step, 0)

    pieces = [pltpu.make_async_copy(p.at[:, chunk], held.at[pl.ds(2 * n, 2)], piece_sems.at[n])
              for n, p in enumerate((near_a, near_b, far_a, far_b))]
    weights = [pltpu.make_async_copy(win, win_h, weight_sems.at[0]), pltpu.make_async_copy(wout, wout_h, weight_sems.at[1])]
    for move in pieces:
        move.start()
    over(lambda i: [move.start() for move in incoming(i)])
    dwin[...] = jnp.zeros_like(dwin)
    dwout[...] = jnp.zeros_like(dwout)
    db[...] = jnp.zeros_like(db)
    for move in pieces:
        move.wait()
    for f in range(8):
        side, at = slot_of(place, f)
        piece = held[4 * side + at]
        for n in range(2):
            win[96 * f : 96 * f + 96, 256 * n : 256 * n + 256] = piece[96 * n : 96 * n + 96]
        for t in range(3):
            part = piece[192 + 80 * t : 272 + 80 * t]
            lanes = slice(256 * t, 256 * t + 256)
            if f == 1:
                wout[0:32, lanes] = part[48:]
            elif f > 1:
                wout[80 * f - 128 : 80 * f - 48, lanes] = part
    for move in weights:
        move.start()

    c0 = 0.7978845608028654
    c1 = 0.044715 * c0

    def step(i, carry):
        rows = pl.ds(pl.multiple_of(i * RB, RB), RB)
        for move in incoming(i):
            move.wait()
        pre = dot_nn(nrm[rows, :], win[...]) + mb[chunk : chunk + 1, :]
        ga = dot_nt(cot[rows, :], wout[...])
        sq = pre * pre
        t = jnp.tanh(pre * (c0 + c1 * sq))
        up = 0.5 + 0.5 * t
        done = pre * up
        act[rows, :] = done.astype(BF)
        gmf = ga * (up + done * (1.0 - up) * (2.0 * c0 + 6.0 * c1 * sq))
        gm[rows, :] = gmf.astype(BF)
        db[...] += jnp.sum(gmf, axis=0, keepdims=True)
        dwout[...] += dot_tn(act[rows, :], cot[rows, :])
        dwin[...] += dot_tn(gm[rows, :], nrm[rows, :])
        for move in outgoing(i):
            move.start()
        return carry

    lax.fori_loop(0, nb, step, 0)
    full = jnp.transpose(dwin[...]).astype(BF)
    core = place[CORE] == 0
    first, second = slice(80 * chunk, 80 * chunk + 80), slice(48 * chunk, 48 * chunk + 48)
    both = jnp.concatenate([came[...], dwo[0:96, :]])
    zero_rows = jnp.where(core, dwo[first, :], both[first])
    one_rows = jnp.where(core, came[second, :], dwo[240 + 48 * chunk : 288 + 48 * chunk, :])
    if last:
        ob = gob[...]
        qs = dg[:, :HD] + dg[:, HD : 2 * HD]
        ks = dg[:, 2 * HD : 3 * HD] + dg[:, 3 * HD :]
        parts = {}
        for j, units in enumerate((db_0[...], db_1[...], db[...])):
            for cc in range(2):
                own = jnp.where(place[CORE] == cc, units, 0.0)
                done = 0
                for u, n in unit_ranges(cc, j):
                    parts[u] = own[:, done : done + n]
                    done += n
        hidden = jnp.concatenate([parts[u] for u in sorted(parts)], axis=1)
    for f in range(8):

        def fill(ref, f=f):
            for n in range(2):
                ref[96 * n : 96 * n + 96, :] = full[96 * f : 96 * f + 96, 256 * n : 256 * n + 256]
            for t in range(3):
                lanes = slice(256 * t, 256 * t + 256)
                at = 192 + 80 * t
                if f == 0:
                    ref[at : at + 80, :] = zero_rows[:, lanes]
                elif f == 1:
                    ref[at : at + 48, :] = one_rows[:, lanes]
                    ref[at + 48 : at + 80, :] = dwout[0:32, lanes].astype(BF)
                else:
                    ref[at : at + 80, :] = dwout[80 * f - 128 : 80 * f - 48, lanes].astype(BF)
            if last:
                blank = lambda n: jnp.zeros((1, n), F32)
                rows = [hidden[:, 384 * f : 384 * f + 256],
                        jnp.concatenate([hidden[:, 384 * f + 256 : 384 * f + 384], ob[:, 96 * f : 96 * f + 96], blank(32)], axis=1),
                        jnp.concatenate([qs[:, 8 * f : 8 * f + 8], blank(120), ks[:, 8 * f : 8 * f + 8], blank(120)], axis=1)]
                ref[432:448, :] = jnp.concatenate([*rows, jnp.zeros((13, 256), F32)]).astype(BF)

        put(place, near_o, far_o, f, fill)
    for move in weights:
        move.wait()
    over(lambda i: [move.wait() for move in outgoing(i)])


def clamp(i, info, *_):
    return (jnp.minimum(i, info[NB] - 1), 0)


def whole(i, *_):
    return (0, 0)


def whole3(i, *_):
    return (0, 0, 0)


def mlp(info, place, nrm, cot, pieces, mb, dwo, came, vectors, chunk, after=()):
    sds = jax.ShapeDtypeStruct
    rows = 448 if chunk == 2 else 432
    outs = (sds((ROWS, U), BF), sds((ROWS, U), BF), sds((D, U), BF), sds((U, D), BF), sds((4, rows, 256), BF),
            sds((4, rows, 256), BF), sds((1, U), F32))
    hbm = pl.BlockSpec(memory_space=pl.ANY)
    v = pltpu.VMEM
    dma = pltpu.SemaphoreType.DMA
    scratch = [v((ROWS, D), BF)] * 2 + [v((ROWS, U), BF)] * 2 + [v((D, U), BF), v((U, D), BF), v((U, D), F32), v((U, D), F32),
               v((8, 432, 256), BF), dma((2, NRB)), dma((2, NRB)), dma((4,)), dma((2,))]
    given = (mb, dwo, came, *vectors)
    return call(functools.partial(mlp_body, chunk=chunk), outs, scratch, (info, place, nrm, cot, *pieces, *given),
                [SCALARS] * 2 + [hbm] * 6 + [ANYWHERE] * len(given), (hbm,) * 4 + (ANYWHERE,) * 3, vmem=60,
                cost=(10 * 10**9, 18 * 10**6), after=after, tick=True)


def sums_body(info, *refs, n, transposed):
    i = pl.program_id(0)
    lefts, rights, own, other, left, right, held, sems = refs[:n], refs[n : 2 * n], *refs[2 * n :]

    @pl.when(i == 0)
    def _():
        at = 0
        for b in rights:
            k = b.shape[1] if transposed else b.shape[0]
            if transposed:
                right[:, at : at + k] = b[...]
            else:
                right[at : at + k, :] = b[...]
            at += k

    @pl.when(i < info[NB])
    def _():
        at = 0
        for a in lefts:
            left[:, at : at + a.shape[1]] = a[...]
            at += a.shape[1]
        total = dot_nt(left[...], right[...]) if transposed else dot_nn(left[...], right[...])
        held[pl.ds(pl.multiple_of(i * RB, RB), RB), :] = total.astype(BF)

    @pl.when(i >= info[NB])
    def _():
        held[pl.ds(pl.multiple_of(i * RB, RB), RB), :] = jnp.zeros((RB, D), BF)

    move_own = pltpu.make_async_copy(held.at[pl.ds(0, CAN), :], own, sems.at[0])

    @pl.when(i == (CAN - 1) // RB)
    def _():
        move_own.start()

    @pl.when(i == pl.num_programs(0) - 1)
    def _():
        move_other = pltpu.make_async_copy(held.at[pl.ds(pl.multiple_of(info[BASE], 16), CAN), :], other, sems.at[1])
        move_other.start()
        move_own.wait()
        move_other.wait()


def sums(info, lefts, rights, transposed, after=()):
    n = len(lefts)
    bs = pl.BlockSpec
    sds = jax.ShapeDtypeStruct

    def rows_of(a, p):
        if p is None:
            return bs((RB, a.shape[1]), clamp)
        return bs((None, RB, a.shape[2]), lambda i, info: (p, jnp.minimum(i, info[NB] - 1), 0))

    def all_of(b, p):
        return bs(b.shape, whole) if p is None else bs((None, *b.shape[1:]), lambda i, info: (p, 0, 0))

    in_specs = [rows_of(*a) for a in lefts] + [all_of(*b) for b in rights]
    lefts, rights = [a for a, _ in lefts], [b for b, _ in rights]
    k = sum(a.shape[-1] for a in lefts)
    v = pltpu.VMEM
    scratch = [v((RB, k), BF), v((D, k) if transposed else (k, D), BF), v((ROWS, D), BF), pltpu.SemaphoreType.DMA((2,))]
    hbm = bs(memory_space=pl.ANY)
    return call(functools.partial(sums_body, n=n, transposed=transposed), (sds((CAN, D), BF),) * 2, scratch,
                (info, *lefts, *rights), in_specs, (hbm,) * 2, grid=(NRB,), prefetch=1,
                vmem=60, cost=(2 * 2304 * k * D, 2 * 2304 * (k + D)), after=after, tick=True)


def adds_body(*refs, counts, kinds):
    given = list(refs[: sum(counts)])
    outs = list(refs[sum(counts) :])
    for count, kind in zip(counts, kinds):
        terms = [given.pop(0) for _ in range(count)]
        if kind == "four":
            total = terms[0][...].astype(F32) + terms[1][...].astype(F32)
            for i in range(4):
                outs.pop(0)[...] = total[i : i + 1].astype(BF)
        else:
            total = terms[0][...].astype(F32)
            for t in terms[1:]:
                total = total + t[...].astype(F32)
            out = outs.pop(0)
            out[...] = total.astype(out.dtype)


def adds(items, after, vmem=VMEM_MIB):
    sds = jax.ShapeDtypeStruct
    outs = []
    for terms, kind in items:
        a = terms[0]
        shape = (1, *a.shape[1:]) if kind == "four" else a.shape
        outs += [sds(shape, F32 if kind == "float" else BF)] * (4 if kind == "four" else 1)
    args = [t for terms, _ in items for t in terms]
    body = functools.partial(adds_body, counts=[len(t) for t, _ in items], kinds=[k for _, k in items])
    *done, tick = call(body, tuple(outs), [], args, [ANYWHERE] * len(args), cost=(0, 3 * 10**6), after=after, tick=True, vmem=vmem)
    results = []
    for _, kind in items:
        results.append([done.pop(0) for _ in range(4)] if kind == "four" else done.pop(0))
    return *results, tick


def final_body(place, w_in, ln, *refs):
    own, other, parts = refs[:3], refs[3:6], refs[6:10]
    gin, gout, gln, gqs, gks, gmb, gob = refs[10:]
    mine, along_x, mate, across = (p[0].astype(F32) for p in parts)
    last_own, last_other = mine + along_x, mate + across
    c, f = place[CORE], place[FSDP]
    for cc in range(2):
        sources = [jnp.where(c == cc, a[0], b[0]) for a, b in zip(own, other)] + [jnp.where(c == cc, last_own, last_other)]
        for p in range(3):
            for n in range(3):
                at = D * n + 384 * cc + 128 * p
                gin[:, at : at + 128] = sources[0][288 * p + 96 * n : 288 * p + 96 * n + 96, :]
        for j in range(3):
            s = sources[1 + j]
            m = jnp.concatenate([s[0:96], s[96:192]], axis=1)
            done = 0
            for u, n in unit_ranges(cc, j):
                gin[:, 3 * D + u : 3 * D + u + n] = m[:, done : done + n]
                done += n
            for t in range(3):
                lanes = slice(256 * t, 256 * t + 256)
                part = s[192 + 80 * t : 272 + 80 * t]

                @pl.when(f != 1)
                def _():
                    gout[240 * cc + 80 * j : 240 * cc + 80 * j + 80, lanes] = part

                @pl.when(f == 1)
                def _():
                    a, b = 144 * cc + 48 * j, 288 + 96 * cc + 32 * j
                    gout[a : a + 48, lanes] = part[:48]
                    gout[b : b + 32, lanes] = part[48:]
    total = jnp.sum(w_in[...].astype(F32) * gin[...], axis=1, keepdims=True)
    gln[...] = jnp.transpose(jnp.broadcast_to(total, (96, 128)))[0:1, :] / ln[...]
    vec = last_own[432:440, :] + last_other[432:440, :]
    gmb[...] = jnp.concatenate([vec[0:1, :], vec[1:2, :128]], axis=1)
    gob[...] = vec[1:2, 128:224]
    gqs[...] = vec[2:3, 0:8]
    gks[...] = vec[2:3, 128:136]


def final(place, w_in, ln, own, other, parts, after=()):
    sds = jax.ShapeDtypeStruct
    outs = (sds((96, 7 * D), F32), sds((480, D), F32), sds((1, 96), F32), sds((1, 8), F32), sds((1, 8), F32),
            sds((1, 384), F32), sds((1, 96), F32))
    return call(final_body, outs, [], (place, w_in, ln, *own, *other, *parts), [SCALARS] + [ANYWHERE] * 12, cost=(0, 10**7), after=after)


def routes():
    places = [(x, c, z, y) for x in range(2) for c in range(2) for z in range(4) for y in range(2)]
    number = lambda x, c, z, y: (x * 2 + c) * 8 + z * 2 + y
    pairs = lambda move: [(number(*p), number(*move(*p))) for p in places]
    out = {
        "core": pairs(lambda x, c, z, y: (x, 1 - c, z, y)),
        "x": pairs(lambda x, c, z, y: (1 - x, c, z, y)),
        "x_core": pairs(lambda x, c, z, y: (1 - x, 1 - c, z, y)),
        "y": pairs(lambda x, c, z, y: (x, c, z, 1 - y)),
        "z1": pairs(lambda x, c, z, y: (x, c, z ^ 1, y)),
        "z2": pairs(lambda x, c, z, y: (x, c, z ^ 2, y)),
        "z3": pairs(lambda x, c, z, y: (x, c, z ^ 3, y)),
    }
    at = lambda n: (n % 8) // 2
    out["z2_up"] = [(a, b) for a, b in out["z2"] if at(a) == 0]
    out["z1_up"] = [(a, b) for a, b in out["z1"] if at(a) % 2 == 0]
    return out


def per_device_paired(
    tokens, lengths, assign, w_in, w_out, ln_scale, q_scale, k_scale, mlp_bias, out_bias, cotangent
):
    way = routes()
    go = lambda v, name: lax.ppermute(v, ("rep", "fsdp"), way[name])
    rep, f = lax.axis_index("rep"), lax.axis_index("fsdp")
    c, y, z = rep % 2, f % 2, f // 2
    cap = tokens.shape[0]
    device = rep * 8 + f
    place = jnp.stack([c, f, y, z, device, device + 8 - 16 * c, rep // 2]).astype(jnp.int32)

    late = lambda v, tick: v if tick is None else v + tick[0].astype(v.dtype)
    first = lambda piece, tick=None: jnp.stack([piece, late(go(piece, "z2"), tick)])
    second = lambda two, tick=None: jnp.concatenate([two, late(go(two, "z1"), tick)])
    third = lambda four: (four, go(four, "y"))
    vectors = (v.reshape(1, -1) for v in (ln_scale, q_scale, k_scale, mlp_bias, out_bias))
    a, wo, tick = pieces_of(place, w_in, w_out)
    a_b, wo_b = go(a, "z2"), go(wo, "z2_up")
    info, vectors = plan(place, lengths, assign, *vectors, after=(tick,))
    vectors = third(second(first(vectors)))
    wo = jnp.where(z == 0, wo, wo_b)
    near = jnp.concatenate([a[:288], a_b[:288], wo])
    b = jnp.concatenate([a[288:], a_b[288:]]).reshape(2, 576, 128)
    own, gob, tick = prepare(info, tokens, cotangent, (near, b, *vectors))
    far = late(go(near, "z1"), tick)
    m, own = split(place, w_in, w_out, own, (far,))
    wo = jnp.where(z % 2 == 0, wo, far[576:])
    near = jnp.concatenate([near[:576], far[:576], wo])
    far = go(near, "y")
    other = go(own, "core")
    b_b = go(b, "z1")
    m_b = go(m, "z2")
    cross = jnp.concatenate([wo, far[PARTS:]])
    nrm, cot, ln, ob, gain, mb, tick = combine(info, place, own, other, *vectors, after=(cross,))
    b = jnp.concatenate([b, late(b_b, tick)])
    wo_a, wo_b, tick = head_rows(place, near, far, go(cross, "x"), (b,))
    wo_b = go(wo_b, "core")
    m = jnp.stack([m, late(m_b, tick)])

    def heads(pairs, g, before, after):
        return attention(info, place, nrm, cot, *g, wo_a, wo_b, gain, pairs, before, after)

    att_0, dqkv_0, w_0, wo_0, dg, dwo, dw, tick = heads((0,), (near, far), (), (b, m))
    m_b = go(m, "z1")
    att_1, dqkv_1, w_1, wo_1, dg, dwo, send, *g_h, tick = heads((1, 2), (b, go(b, "y")), (dw, dwo, dg), (m_b,))
    pieces = (m, m_b, go(m, "y"), go(m_b, "y"))
    came = go(send, "core")
    att, dqkv, ws, wos = (((p, 0), (q, 0), (q, 1)) for p, q in ((att_0, att_1), (dqkv_0, dqkv_1), (w_0, w_1), (wo_0, wo_1)))

    def hidden(j, vectors, after):
        return mlp(info, place, nrm, cot, pieces, mb, dwo, came, vectors, j, after)

    step_y = lambda g: ((g[0], go(g[1], "y")), "four")
    step_z = lambda g: ((g[0], go(g[2], "z1"), go(g[1], "z2"), go(g[3], "z3")), "whole")
    step_x = lambda g: ((g, go(g, "x")), "float")

    *h0, tick = hidden(0, (), (tick,))
    g_h, tick = adds([step_y(g_h)], (tick,), 60)
    *h1, tick = hidden(1, (), (tick,))
    g_h, g_0, tick = adds([step_z(g_h), step_y(h0[4:6])], (tick,))
    *h2, tick = hidden(2, (gob, dg, h0[6], h1[6]), (tick,))
    act, gm, wins, wouts, _, _, _ = zip(h0, h1, h2)
    plain = lambda arrays: tuple((v, None) for v in arrays)

    g_h, g_0, g_1, tick = adds([step_x(g_h), step_z(g_0), step_y(h1[4:6])], (tick,))
    part, away, tick = sums(info, (*att, *plain(act)), (*wos, *plain(wouts)), False, (tick,))
    away = go(away, "core")
    g_0, g_1, g_2, tick = adds([step_x(g_0), step_z(g_1), step_y(h2[4:6])], (tick,))
    part_b, away_b, tick = sums(info, (*dqkv, *plain(gm)), (*ws, *plain(wins)), True, (tick,))
    away_b = go(away_b, "core")
    g_1, g_2, tick = adds([step_x(g_1), step_z(g_2)], (tick,))
    output, tick = last_rows(info, own, part, away, ob, cap, False, (tick,))
    grads = (g_h, g_0, g_1)
    others = [go(g, "core") for g in grads]
    parts = (g_2, *(go(g_2, name) for name in ("x", "core", "x_core")))
    grad_tokens, tick = last_rows(info, own, part_b, away_b, ln, cap, True, (tick,))
    g_win, g_wout, *small = final(place, w_in, ln_scale.astype(F32).reshape(1, 96), grads, others, parts, (tick,))
    return (output, grad_tokens, g_win, g_wout, *(g.reshape(-1) for g in small))


HEADS = 12
epsilon = 1e-06


def layer_norm(values, weight_gain):
    center = values - jnp.mean(values, axis=-1, keepdims=True)
    spread = jnp.mean(center * center, axis=-1, keepdims=True)
    return center * lax.rsqrt(spread + epsilon) * weight_gain


def layout(lengths, assign, device, row_count):
    own = assign == device
    own_sizes = jnp.where(own, lengths, 0)
    own_ends = jnp.cumsum(own_sizes)
    own_starts = own_ends - own_sizes
    position = lax.broadcasted_iota(jnp.int32, (row_count, lengths.shape[0]), 0)
    number = lax.broadcasted_iota(jnp.int32, (row_count, lengths.shape[0]), 1)
    inside = (position >= own_starts[None, :]) & (position < own_ends[None, :])
    filled = jnp.any(inside, axis=1)
    segment = jnp.sum(jnp.where(inside, number, 0), axis=1)
    return (jnp.where(filled, segment, -1), filled)


def contract_rows(left, right):
    return lax.dot_general(
        left, right, (((0,), (0,)), ((), ())), preferred_element_type=jnp.float32
    )


def contract_cols(left, right):
    return lax.dot_general(
        left, right, (((1,), (1,)), ((), ())), preferred_element_type=jnp.float32
    )


def per_device(
    tokens, lengths, assign, w_in, w_out, ln_scale, q_scale, k_scale, mlp_bias, out_bias, cotangent
):
    row_count = tokens.shape[0]
    head_dim = HD
    head_count = HEADS
    width = head_dim * head_count
    factor = head_dim ** (-0.5)
    device = lax.axis_index("rep") * lax.axis_size("fsdp") + lax.axis_index("fsdp")
    segment, filled = layout(lengths, assign, device, row_count)
    allowed = segment[:, None] == segment[None, :]
    params = (w_in, w_out, ln_scale, q_scale, k_scale, mlp_bias, out_bias)
    full = (
        lax.all_gather(params[0], "fsdp", axis=0, tiled=True),
        lax.all_gather(params[1], "fsdp", axis=0, tiled=True),
        lax.all_gather(params[2], "fsdp", axis=0, tiled=True),
        lax.all_gather(params[3], "fsdp", axis=0, tiled=True),
        lax.all_gather(params[4], "fsdp", axis=0, tiled=True),
        lax.all_gather(params[5], "fsdp", axis=0, tiled=True),
        lax.all_gather(params[6], "fsdp", axis=0, tiled=True),
    )
    win_full, wout_full = (full[0], full[1])
    small = [arr.astype(jnp.float32) for arr in full[2:]]
    ln_full, qs_full, ks_full, mb_full, ob_full = small
    inputs = tokens.astype(jnp.float32)
    normed_f, ln_pull = jax.vjp(layer_norm, inputs, ln_full)
    normed = normed_f.astype(jnp.bfloat16)
    joined = jnp.dot(normed, win_full, preferred_element_type=jnp.float32)
    q_pre = joined[:, :width].reshape(row_count, head_count, head_dim)
    k_pre = joined[:, width : 2 * width].reshape(row_count, head_count, head_dim)
    values = joined[:, 2 * width : 3 * width].astype(jnp.bfloat16)
    hidden_pre = joined[:, 3 * width :]
    q_norm, q_pull = jax.vjp(layer_norm, q_pre, qs_full)
    k_norm, k_pull = jax.vjp(layer_norm, k_pre, ks_full)
    queries = q_norm.reshape(row_count, width).astype(jnp.bfloat16)
    keys_all = k_norm.reshape(row_count, width).astype(jnp.bfloat16)

    def head_slice(array, head_index):
        return lax.dynamic_slice_in_dim(array, head_index * head_dim, head_dim, 1)

    def head_scores(head_index):
        raw = (
            contract_cols(head_slice(queries, head_index), head_slice(keys_all, head_index))
            * factor
        )
        return jnp.where(allowed, raw, -1e30)

    def head_forward(head_index):
        scores = head_scores(head_index)
        top = jnp.max(scores, axis=1, keepdims=True)
        expon = jnp.exp(scores - top)
        total = jnp.sum(expon, axis=1, keepdims=True)
        probs = (expon / total).astype(jnp.bfloat16)
        head_out = jnp.dot(
            probs, head_slice(values, head_index), preferred_element_type=jnp.float32
        )
        return (head_out, (top + jnp.log(total))[:, 0])

    head_outs, log_totals = lax.map(head_forward, jnp.arange(head_count))
    attended = jnp.transpose(head_outs, (1, 0, 2)).reshape(row_count, width)
    activated, gelu_pull = jax.vjp(lambda pre, bias: jax.nn.gelu(pre + bias), hidden_pre, mb_full)
    merged = jnp.concatenate([attended, activated], axis=1).astype(jnp.bfloat16)
    result = jnp.dot(merged, wout_full, preferred_element_type=jnp.float32) + ob_full
    output = jnp.where(filled[:, None], inputs + result, 0.0).astype(jnp.bfloat16)
    back = (
        lax.all_gather(params[0], "fsdp", axis=0, tiled=True),
        lax.all_gather(params[1], "fsdp", axis=0, tiled=True),
        lax.all_gather(params[2], "fsdp", axis=0, tiled=True),
        lax.all_gather(params[3], "fsdp", axis=0, tiled=True),
        lax.all_gather(params[4], "fsdp", axis=0, tiled=True),
        lax.all_gather(params[5], "fsdp", axis=0, tiled=True),
        lax.all_gather(params[6], "fsdp", axis=0, tiled=True),
    )
    win_back, wout_back = (back[0], back[1])
    grad_rows = jnp.where(filled[:, None], cotangent.astype(jnp.float32), 0.0)
    grad_low = grad_rows.astype(jnp.bfloat16)
    grad_ob = jnp.sum(grad_rows, axis=0)
    grad_wout = contract_rows(merged, grad_low)
    grad_merged = contract_cols(grad_low, wout_back)
    grad_attended = grad_merged[:, :width].astype(jnp.bfloat16)
    grad_m, grad_mb = gelu_pull(grad_merged[:, width:])

    def head_backward(head_index):
        scores = head_scores(head_index)
        probs_full = jnp.exp(scores - log_totals[head_index][:, None])
        probs = probs_full.astype(jnp.bfloat16)
        grad_head = head_slice(grad_attended, head_index)
        grad_probs = contract_cols(grad_head, head_slice(values, head_index))
        inner = jnp.sum(probs_full * grad_probs, axis=1, keepdims=True)
        grad_scores = (probs_full * (grad_probs - inner)).astype(jnp.bfloat16)
        grad_q = (
            jnp.dot(
                grad_scores, head_slice(keys_all, head_index), preferred_element_type=jnp.float32
            )
            * factor
        )
        grad_k = contract_rows(grad_scores, head_slice(queries, head_index)) * factor
        grad_v = contract_rows(probs, grad_head)
        return (grad_q, grad_k, grad_v)

    grad_qh, grad_kh, grad_vh = lax.map(head_backward, jnp.arange(head_count))
    grad_qn = jnp.transpose(grad_qh, (1, 0, 2))
    grad_kn = jnp.transpose(grad_kh, (1, 0, 2))
    grad_values = jnp.transpose(grad_vh, (1, 0, 2)).reshape(row_count, width)
    grad_q_pre, grad_qs = q_pull(grad_qn)
    grad_k_pre, grad_ks = k_pull(grad_kn)
    grad_joined = jnp.concatenate(
        [
            grad_q_pre.reshape(row_count, width),
            grad_k_pre.reshape(row_count, width),
            grad_values,
            grad_m,
        ],
        axis=1,
    ).astype(jnp.bfloat16)
    grad_win = contract_rows(normed, grad_joined)
    grad_normed = contract_cols(grad_joined, win_back)
    grad_x_norm, grad_ln = ln_pull(grad_normed)
    grad_tokens = (grad_rows + grad_x_norm).astype(jnp.bfloat16)
    grads = (grad_win, grad_wout, grad_ln, grad_qs, grad_ks, grad_mb, grad_ob)
    shares = (
        lax.psum_scatter(grads[0], "fsdp", scatter_dimension=0, tiled=True),
        lax.psum_scatter(grads[1], "fsdp", scatter_dimension=0, tiled=True),
        lax.psum_scatter(grads[2], "fsdp", scatter_dimension=0, tiled=True),
        lax.psum_scatter(grads[3], "fsdp", scatter_dimension=0, tiled=True),
        lax.psum_scatter(grads[4], "fsdp", scatter_dimension=0, tiled=True),
        lax.psum_scatter(grads[5], "fsdp", scatter_dimension=0, tiled=True),
        lax.psum_scatter(grads[6], "fsdp", scatter_dimension=0, tiled=True),
    )
    shares = lax.psum(
        (shares[0], shares[1], shares[2], shares[3], shares[4], shares[5], shares[6]), "rep"
    )
    return (
        output,
        grad_tokens,
        shares[0],
        shares[1],
        shares[2],
        shares[3],
        shares[4],
        shares[5],
        shares[6],
    )


def solution(mesh):
    in_specs = (
        P(("rep", "fsdp"), None),
        P(),
        P(),
        P("fsdp", None),
        P("fsdp", None),
        P("fsdp"),
        P("fsdp"),
        P("fsdp"),
        P("fsdp"),
        P("fsdp"),
        P(("rep", "fsdp"), None),
    )
    out_specs = (
        P(("rep", "fsdp"), None),
        P(("rep", "fsdp"), None),
        P("fsdp", None),
        P("fsdp", None),
        P("fsdp"),
        P("fsdp"),
        P("fsdp"),
        P("fsdp"),
        P("fsdp"),
    )
    paired = dict(mesh.shape) == {"rep": 4, "fsdp": 8}
    return jax.shard_map(
        per_device_paired if paired else per_device, mesh=mesh, in_specs=in_specs, out_specs=out_specs, check_vma=False
    )
```

```python
import functools

import jax
import jax.numpy as jnp
from jax import lax
from jax.experimental import pallas as pl
from jax.experimental.pallas import tpu as pltpu
from jax.sharding import PartitionSpec as P

D = 768
HD = 64
SMALL = 196
BIG = 1024
BLK = 208
CAN = 7 * BLK
ROWS = 3072
ROOM = 3584
RB = 512
NRB = ROWS // RB
U = 512
EPS = 1e-06
BF = jnp.bfloat16
F32 = jnp.float32
VMEM_MIB = 34
ANYWHERE = pl.BlockSpec(memory_space=pltpu.VMEM)
TICK = jax.ShapeDtypeStruct((1,), F32)
SCALARS = pl.BlockSpec(memory_space=pltpu.SMEM)


def dot_nn(a, b):
    return lax.dot_general(a, b, (((1,), (0,)), ((), ())), preferred_element_type=F32)


def dot_nt(a, b):
    return lax.dot_general(a, b, (((1,), (1,)), ((), ())), preferred_element_type=F32)


def dot_tn(a, b):
    return lax.dot_general(a, b, (((0,), (0,)), ((), ())), preferred_element_type=F32)


def two_parts(x):
    hi = x.astype(BF)
    return hi, (x - hi.astype(F32)).astype(BF)


def call(body, out_shape, scratch, args, in_specs, out_specs=None, grid=None, prefetch=0, cost=None, after=(), tick=False, alias=None, vmem=VMEM_MIB):
    if after:
        inner, n, skip = body, len(args), len(after)

        def body(*refs):
            inner(*refs[:n], *refs[n + skip :])

        args = (*args, *after)
        in_specs = [*in_specs] + [pl.BlockSpec(memory_space=pl.ANY)] * skip
    params = pltpu.CompilerParams(vmem_limit_bytes=vmem * 2**20)
    if out_specs is None:
        out_specs = jax.tree.map(lambda _: ANYWHERE, out_shape)
    if tick:
        many = isinstance(out_shape, tuple)
        out_shape = (*out_shape, TICK) if many else (out_shape, TICK)
        out_specs = (*out_specs, SCALARS) if many else (out_specs, SCALARS)
        untold, place = body, len(args) + len(out_shape) - 1

        def body(*refs):
            refs[place][0] = jnp.float32(0)
            untold(*refs[:place], *refs[place + 1 :])

    spec = pltpu.PrefetchScalarGridSpec(
        num_scalar_prefetch=prefetch,
        grid=grid or (),
        in_specs=in_specs,
        out_specs=out_specs,
        scratch_shapes=scratch,
    )
    estimate = None if cost is None else pl.CostEstimate(flops=20 * cost[0], bytes_accessed=20 * cost[1], transcendentals=0)
    return pl.pallas_call(body, grid_spec=spec, out_shape=out_shape, compiler_params=params, cost_estimate=estimate, input_output_aliases=alias or {})(*args)


NB, BLOCKS_A, LARGE_A, SMALL_A, BASE, BLOCKS_B, LARGE_B, SMALL_B, BEFORE = range(9)
CORE, FSDP, Y, Z, SELF, MATE, X = range(7)


def unit_ranges(c, j):
    first = [(96 * c + 32 * j, 32)]
    return first + [(192 + 480 * s + 240 * c + 80 * j, 80) for s in range(6)]


def pieces_body(place, w_in, w_out, heads, wo, sems):
    own = 384 * place[CORE]
    lanes = lambda at: pl.ds(pl.multiple_of(own + at, 128), 128)
    rows = lambda at: pl.ds(at, 96)
    half = pl.ds(pl.multiple_of(240 * place[X], 16), 240)
    moves = []
    for n in range(3):
        moves.append((w_out.at[half, lanes(128 * n)], wo.at[pl.ds(240 * n, 240), :]))
        for p in range(3):
            moves.append((w_in.at[:, lanes(D * n + 128 * p)], heads.at[rows(288 * p + 96 * n), :]))
    moves = [pltpu.make_async_copy(p, q, sems.at[i]) for i, (p, q) in enumerate(moves)]
    for move in moves:
        move.start()
    for move in moves:
        move.wait()


def pieces_of(place, w_in, w_out):
    sds = jax.ShapeDtypeStruct
    hbm = pl.BlockSpec(memory_space=pl.ANY)
    return call(pieces_body, (sds((864, 128), BF), sds((720, 128), BF)), [pltpu.SemaphoreType.DMA((12,))],
                (place, w_in, w_out), [SCALARS, hbm, hbm], (ANYWHERE,) * 2, vmem=60, cost=(0, 2 * 10**6), tick=True)


def plan_body(place, lengths, assign, ln, qs, ks, mb, ob, info, params):
    def count(i, carry):
        before, small_a, large_a, small_b, large_b = carry
        large = (lengths[i] == BIG).astype(jnp.int32)
        me = (assign[i] == place[SELF]).astype(jnp.int32)
        mate = (assign[i] == place[MATE]).astype(jnp.int32)
        before = jnp.where(me * large == 1, small_a, before)
        return before, small_a + me * (1 - large), large_a + me * large, small_b + mate * (1 - large), large_b + mate * large

    zero = jnp.int32(0)
    before, small_a, large_a, small_b, large_b = lax.fori_loop(0, lengths.shape[0], count, (zero,) * 5)
    blocks_a = jnp.where(large_a > 0, 7, small_a)
    blocks_b = jnp.where(large_b > 0, 7, small_b)
    info[NB] = (BLK * (blocks_a + blocks_b) + RB - 1) // RB
    info[BLOCKS_A], info[LARGE_A], info[SMALL_A] = blocks_a, large_a, small_a
    info[BASE] = BLK * blocks_a
    info[BLOCKS_B], info[LARGE_B], info[SMALL_B] = blocks_b, large_b, small_b
    info[BEFORE] = jnp.where(large_a > 0, before, small_a)
    params[...] = jnp.zeros_like(params)
    params[0:1, :96] = ln[...]
    params[1:2, :8] = qs[...]
    params[2:3, :8] = ks[...]
    params[3:4, :96] = ob[...]
    for n in range(3):
        params[4 + n : 5 + n, :] = mb[:, 128 * n : 128 * n + 128]


def plan(place, lengths, assign, *small, after):
    sds = jax.ShapeDtypeStruct
    return call(plan_body, (sds((16,), jnp.int32), sds((16, 128), BF)), [], (place, lengths, assign, *small),
                [SCALARS] * 3 + [ANYWHERE] * 5, (SCALARS, ANYWHERE), vmem=60, cost=(0, 10**5), after=after)


def split_body(place, w_in, w_out, own, m, own_o):
    c, f = place[CORE], place[FSDP]
    for cc in range(2):

        @pl.when(c == cc)
        def _():
            for j in range(3):
                cols = [w_in[:, 3 * D + u : 3 * D + u + n] for u, n in unit_ranges(cc, j)]
                half = jnp.concatenate(cols, axis=1)
                m[j, 0:96, :] = half[:, :256]
                m[j, 96:192, :] = half[:, 256:]
                for t in range(3):
                    lanes = slice(256 * t, 256 * t + 256)
                    at = 192 + 80 * t

                    @pl.when(f != 1)
                    def _():
                        m[j, at : at + 80, :] = w_out[240 * cc + 80 * j : 240 * cc + 80 * j + 80, lanes]

                    @pl.when(f == 1)
                    def _():
                        a, b = 144 * cc + 48 * j, 288 + 96 * cc + 32 * j
                        m[j, at : at + 48, :] = w_out[a : a + 48, lanes]
                        m[j, at + 48 : at + 80, :] = w_out[b : b + 32, lanes]


def split(place, w_in, w_out, own, after):
    sds = jax.ShapeDtypeStruct
    outs = (sds((3, 432, 256), BF), sds(own.shape, BF))
    hbm = pl.BlockSpec(memory_space=pl.ANY)
    return call(split_body, outs, [], (place, w_in, w_out, own), [SCALARS] + [ANYWHERE] * 2 + [hbm], (ANYWHERE, hbm),
                cost=(0, 4 * 10**6), after=after, alias={3: 1})


def slot_of(place, f):
    dz = place[Z] ^ (f >> 1)
    return place[Y] ^ (f & 1), ((dz & 1) << 1) | (dz >> 1)


def taken(place, near, far, f, rows):
    side, at = slot_of(place, f)
    return jnp.where(side == 0, near[at, rows, :], far[at, rows, :])


def put(place, near, far, f, fill):
    side, at = slot_of(place, f)

    @pl.when(side == 0)
    def _():
        fill(near.at[at])

    @pl.when(side != 0)
    def _():
        fill(far.at[at])


def each_image(info, move):
    start = SMALL * info[BEFORE]

    @pl.when(info[LARGE_A] == 1)
    def _():
        for t in range(5):
            move(BLK * t, start + BLK * t, min(BLK, BIG - BLK * t))

    def small(i, carry):
        large = BIG * info[LARGE_A]
        move(pl.multiple_of(large + BLK * i, 16), SMALL * i + jnp.where(i >= info[BEFORE], large, 0), SMALL)
        return carry

    lax.fori_loop(0, info[SMALL_A], small, 0)


WINDOW = BLK + 16


def window_of(slot):
    first = (slot // 16) * 16
    return pl.ds(pl.multiple_of(first, 16), WINDOW), slot - first


def prepare_body(info, tokens, cot, out, gob_o, pad_x, pad_g):
    cap = tokens.shape[0]
    for pad, held in ((pad_x, tokens), (pad_g, cot)):
        pad[0:cap, :] = held[...]
        pad[cap:, :] = jnp.zeros((pad.shape[0] - cap, D), BF)
    out[...] = jnp.zeros_like(out)
    gob_o[...] = jnp.zeros_like(gob_o)
    apart = lax.broadcasted_iota(jnp.int32, (BLK, WINDOW), 1) - lax.broadcasted_iota(jnp.int32, (BLK, WINDOW), 0)
    row = lax.broadcasted_iota(jnp.int32, (BLK, WINDOW), 0)

    def move(to, slot, n):
        window, shift = window_of(slot)
        pick = ((apart == shift) & (row < n)).astype(BF)
        rows = pl.ds(to, BLK)
        g = dot_nn(pick, pad_g[window, :])
        out[0, rows, :] = dot_nn(pick, pad_x[window, :]).astype(BF)
        out[1, rows, :] = g.astype(BF)
        gob_o[...] += jnp.sum(g, axis=0, keepdims=True)

    each_image(info, move)


def prepare(info, tokens, cot, after):
    sds = jax.ShapeDtypeStruct
    pad = pltpu.VMEM((CAN + 16, D), BF)
    return call(prepare_body, (sds((2, CAN, D), BF), sds((1, D), F32)), [pad, pad], (info, tokens, cot),
                [SCALARS] + [ANYWHERE] * 2, vmem=60, cost=(10**9, 9 * 10**6), after=after, tick=True)


def combine_body(info, place, own, other, near, far, nrm, cot, ln_o, ob_o, gain_o, mb_o, x, y, g, zero, sems, zero_sems):
    count_a, count_b = info[BLOCKS_A], info[BLOCKS_B]

    def copies(source, i, t):
        rows = pl.ds(pl.multiple_of(i * BLK, 16), BLK)
        to = pl.ds(pl.multiple_of(t * BLK, 16), BLK)
        return (lambda: pltpu.make_async_copy(source.at[0, rows, :], x.at[t], sems.at[0, t]),
                lambda: pltpu.make_async_copy(source.at[1, rows, :], g.at[t], sems.at[1, t]),
                lambda: pltpu.make_async_copy(g.at[t], cot.at[to, :], sems.at[3, t]),
                lambda: pltpu.make_async_copy(y.at[t], nrm.at[to, :], sems.at[2, t]))

    def over(body):
        def step_a(i, carry):
            body(i, *copies(own, i, i))
            return carry

        def step_b(i, carry):
            body(count_a + i, *copies(other, i, count_a + i))
            return carry

        lax.fori_loop(0, count_a, step_a, 0)
        lax.fori_loop(0, count_b, step_b, 0)

    def begin(t, to_x, to_g, to_cot, to_nrm):
        to_x().start()
        to_g().start()

    over(begin)
    zero[...] = jnp.zeros_like(zero)
    end = pl.ds(pl.multiple_of((count_a + count_b) * BLK, 16), RB)
    blanks = [pltpu.make_async_copy(zero, out.at[end, :], zero_sems.at[n]) for n, out in enumerate((nrm, cot))]
    for move in blanks:
        move.start()
    small = [taken(place, near, far, f, slice(0, 16)).astype(F32) for f in range(8)]
    ln = jnp.concatenate([s[0:1, :96] for s in small], axis=1)
    ln_o[...] = ln
    ob_o[...] = jnp.concatenate([s[3:4, :96] for s in small], axis=1)
    gain_o[...] = jnp.concatenate(([s[1:2, :8] for s in small] * 2) + ([s[2:3, :8] for s in small] * 2), axis=1)
    mb = jnp.concatenate([s[4 + n : 5 + n, :] for s in small for n in range(3)], axis=1)
    for j in range(3):
        rows = [jnp.concatenate([mb[:, u : u + n] for u, n in unit_ranges(cc, j)], axis=1) for cc in range(2)]
        mb_o[j : j + 1, :] = jnp.where(place[CORE] == 0, rows[0], rows[1])

    def norm(t, to_x, to_g, to_cot, to_nrm):
        to_x().wait()
        v = x[t].astype(F32)
        center = v - jnp.mean(v, axis=1, keepdims=True)
        spread = jnp.mean(center * center, axis=1, keepdims=True)
        y[t] = (center * lax.rsqrt(spread + EPS) * ln).astype(BF)
        to_nrm().start()
        to_g().wait()
        to_cot().start()

    over(norm)

    def finish(t, to_x, to_g, to_cot, to_nrm):
        to_cot().wait()
        to_nrm().wait()

    over(finish)
    for move in blanks:
        move.wait()


def combine(info, place, own, other, near, far, after=()):
    sds = jax.ShapeDtypeStruct
    outs = (sds((ROOM, D), BF),) * 2 + (sds((1, D), F32),) * 2 + (sds((1, 256), F32), sds((3, U), F32))
    hbm = pl.BlockSpec(memory_space=pl.ANY)
    v = pltpu.VMEM
    most = 2 * CAN // BLK
    scratch = [v((most, BLK, D), BF)] * 3 + [v((RB, D), BF), pltpu.SemaphoreType.DMA((4, most)), pltpu.SemaphoreType.DMA((2,))]
    return call(combine_body, outs, scratch, (info, place, own, other, near, far), [SCALARS] * 2 + [hbm] * 2 + [ANYWHERE] * 2,
                (hbm,) * 2 + (ANYWHERE,) * 4, vmem=60, cost=(0, 18 * 10**6), after=after, tick=True)


def rows_body(info, x_h, a, b, vector, out, x, held, pad, sems, *, gradient):
    moves = []
    for i in range(CAN // BLK):
        rows = pl.ds(i * BLK, BLK)
        pairs = [(x_h.at[0, rows, :], x.at[0, rows, :])]
        if gradient:
            pairs.append((x_h.at[1, rows, :], x.at[1, rows, :]))
        moves.append([pltpu.make_async_copy(p, q, sems.at[n, i]) for n, (p, q) in enumerate(pairs)])
        for move in moves[-1]:
            move.start()
    pad[...] = jnp.zeros_like(pad)
    for i in range(CAN // BLK):
        for move in moves[i]:
            move.wait()
        rows = pl.ds(i * BLK, BLK)
        v = x[0, rows, :].astype(F32)
        total = a[rows, :].astype(F32) + b[rows, :].astype(F32)
        if gradient:
            center = v - jnp.mean(v, axis=1, keepdims=True)
            r = lax.rsqrt(jnp.mean(center * center, axis=1, keepdims=True) + EPS)
            xh = center * r
            g = total * vector[...]
            gx = r * (g - jnp.mean(g, axis=1, keepdims=True) - xh * jnp.mean(g * xh, axis=1, keepdims=True))
            held[rows, :] = (x[1, rows, :].astype(F32) + gx).astype(BF)
        else:
            held[rows, :] = (v + (total + vector[...])).astype(BF)
    apart = lax.broadcasted_iota(jnp.int32, (WINDOW, BLK), 0) - lax.broadcasted_iota(jnp.int32, (WINDOW, BLK), 1)
    col = lax.broadcasted_iota(jnp.int32, (WINDOW, BLK), 1)

    def move(at, slot, n):
        window, shift = window_of(slot)
        pick = ((apart == shift) & (col < n)).astype(BF)
        pad[window, :] += dot_nn(pick, held[pl.ds(at, BLK), :]).astype(BF)

    each_image(info, move)
    out[...] = pad[: out.shape[0], :]


def last_rows(info, x, a, b, vector, cap, gradient, after=()):
    v = pltpu.VMEM
    scratch = [v((2, CAN, D), BF), v((CAN, D), BF), v((CAN + 16, D), BF), pltpu.SemaphoreType.DMA((2, CAN // BLK))]
    hbm = pl.BlockSpec(memory_space=pl.ANY)
    return call(functools.partial(rows_body, gradient=gradient), jax.ShapeDtypeStruct((cap, D), BF), scratch, (info, x, a, b, vector),
                [SCALARS, hbm] + [ANYWHERE] * 3, cost=(4 * 10**9, 12 * 10**6), after=after, tick=True)


def head_rows_body(place, near, far, cross, mine, theirs):
    rows = slice(PARTS, PARTS + 720)
    swap_y, swap_x, second_core = place[Y] != 0, place[X] != 0, place[CORE] != 0
    pick = lambda swap, a, b: (jnp.where(swap, b, a), jnp.where(swap, a, b))
    own = pick(swap_y, near[rows, :], far[rows, :])
    came = pick(swap_y, cross[0:720, :], cross[720:, :])
    (low, high), (low_1, high_1) = (pick(swap_x, a, b) for a, b in zip(own, came))
    for n in range(3):
        lanes = slice(128 * n, 128 * n + 128)
        at = 240 * n
        first = jnp.concatenate([low[at : at + 240], high[at : at + 144]])
        second = jnp.concatenate([high[at + 144 : at + 240], low_1[at : at + 240], high_1[at : at + 48]])
        mine[:, lanes], theirs[:, lanes] = pick(second_core, first, second)


def head_rows(place, near, far, cross, after):
    sds = jax.ShapeDtypeStruct
    return call(head_rows_body, (sds((384, 384), BF),) * 2, [], (place, near, far, cross), [SCALARS] + [ANYWHERE] * 3, cost=(0, 10**6),
                after=after, tick=True)


PARTS = 4 * 288


def attention_body(info, place, nrm_h, cot_h, near, far, wo_a, wo_b, gain, *refs, pairs):
    refs = list(refs)
    last = len(pairs) > 1
    if last:
        dw_0, dwo_0, dg_0 = refs[:3]
        refs = refs[3:]
    att_o, dqkv_o, w_o, wo_o, dg_o, dwo_o = refs[:6]
    if last:
        dwo_send, near_o, far_o = refs[6:9]
        refs = refs[9:]
    else:
        dw_o = refs[6]
        refs = refs[7:]
    nrm, cot, sems, vv, qp, kp, do, xh, rr, dqk, dv, dw, dwo, dws = refs
    step = pl.program_id(0)
    nb = info[NB]

    def incoming(i):
        rows = pl.ds(pl.multiple_of(i * RB, RB), RB)
        return (pltpu.make_async_copy(nrm_h.at[rows, :], nrm.at[rows, :], sems.at[0, i]),
                pltpu.make_async_copy(cot_h.at[rows, :], cot.at[rows, :], sems.at[1, i]))

    @pl.when(step == 0)
    def _():
        def begin(i, carry):
            for move in incoming(i):
                move.start()
            return carry

        lax.fori_loop(0, nb, begin, 0)

        @pl.when(nb % 2 == 1)
        def _():
            rest = pl.ds(pl.multiple_of(nb * RB, RB), RB)
            nrm[rest, :] = jnp.zeros((RB, D), BF)
            cot[rest, :] = jnp.zeros((RB, D), BF)

        if last:
            dg_o[...] = dg_0[...]
        else:
            dg_o[...] = jnp.zeros_like(dg_o)

    lane = lax.broadcasted_iota(jnp.int32, (1, 128), 1)
    first = lane < HD
    same = lax.broadcasted_iota(jnp.int32, (256, 256), 0) // HD == lax.broadcasted_iota(jnp.int32, (256, 256), 1) // HD
    mean_m = jnp.where(same, 1.0 / HD, 0.0).astype(BF)
    sum_m = jnp.where(same[:, :128] | same[:, 128:], 1.0, 0.0).astype(BF)
    c_exp = 1.4426950408889634 / 8.0
    masks = [jnp.where(first, 1.0, 0.0).astype(BF), jnp.where(first, 0.0, 1.0).astype(BF)]

    for f in range(8):
        side, at = slot_of(place, f)
        if pairs[0] == 0:
            rows = pl.ds(pl.multiple_of(288 * at, 16), 288)
            piece = jnp.where(side == 0, near[rows, :], far[rows, :])
        else:
            rows = pl.ds(pl.multiple_of(288 * step, 16), 288)
            piece = jnp.where(side == 0, near[at, rows, :], far[at, rows, :])
        for n in range(3):
            w_o[96 * f : 96 * f + 96, 128 * n : 128 * n + 128] = piece[96 * n : 96 * n + 96]
    rows = pl.ds(pl.multiple_of(128 * (pairs[0] + step), 16), 128)
    mine, theirs = wo_a[rows, :], wo_b[rows, :]
    wo_o[:, :384] = jnp.where(place[CORE] == 0, mine, theirs)
    wo_o[:, 384:] = jnp.where(place[CORE] == 0, theirs, mine)

    def mean(x):
        return dot_nn(x.astype(BF), mean_m)

    def project(i, carry):
        @pl.when(step == 0)
        def _():
            for move in incoming(2 * i):
                move.wait()

            @pl.when(2 * i + 1 < nb)
            def _():
                for move in incoming(2 * i + 1):
                    move.wait()

        rows = pl.ds(pl.multiple_of(i * 2 * RB, 2 * RB), 2 * RB)
        y = dot_nn(nrm[rows, :], w_o[...])
        qk, v = y[:, :256], y[:, 256:]
        center = qk - mean(qk)
        r = lax.rsqrt(mean(center * center) + EPS)
        x = center * r
        xh[rows, :] = x
        rr[rows, :] = r
        qk = (x * gain[...]).astype(BF)
        qp[rows, :] = qk[:, :128]
        kp[rows, :] = qk[:, 128:]
        vv[0, rows, :] = jnp.where(first, v, 1.0).astype(BF)
        vv[1, rows, :] = jnp.where(first, 1.0, v).astype(BF)
        do[rows, :] = dot_nt(cot[rows, :], wo_o[...]).astype(BF)
        dqk[rows, :] = jnp.zeros((2 * RB, 256), F32)
        dv[rows, :] = jnp.zeros((2 * RB, 128), F32)
        att_o[rows, :] = jnp.zeros((2 * RB, 128), BF)
        return carry

    lax.fori_loop(0, (nb + 1) // 2, project, 0)

    def blocks(items, masked, add):
        both = [(i, h) for i in range(len(items)) for h in range(2)]
        plain = [qp[it[0], :] for it in items]
        ql = [[q * m for m in masks] for q in plain]
        kl = [kp[it[1], :] for it in items]
        vl = [[vv[h, it[1], :] for h in range(2)] for it in items]
        grads = [do[it[0], :].astype(F32) for it in items]
        p, pb, xs = {}, {}, {}
        for i, h in both:
            e = jnp.exp2(dot_nt(ql[i][h], kl[i]) * c_exp)
            if masked:
                e = jnp.where(lax.broadcasted_iota(jnp.int32, e.shape, 1) < SMALL, e, 0.0)
            p[i, h] = e
            pb[i, h] = e.astype(BF)
        for i, h in both:
            xs[i, h] = dot_nn(pb[i, h], vl[i][h])
        outs, scaled, lefts = [], [], {}
        for i in range(len(items)):
            total = jnp.where(first, pltpu.roll(xs[i, 0], HD, 1), pltpu.roll(xs[i, 1], HD, 1))
            inverse = 1.0 / total
            out = jnp.where(first, xs[i, 0], xs[i, 1]) * inverse
            outs.append(out.astype(BF))
            hi, lo = two_parts(grads[i] * out)
            inner = dot_nn(jnp.concatenate([hi, lo], axis=1), sum_m) * inverse
            s = (grads[i] * inverse).astype(BF)
            scaled.append(s)
            sf = s.astype(F32)
            hi, lo = two_parts(inner)
            hi, lo = pltpu.roll(hi.astype(F32), HD, 1), pltpu.roll(lo.astype(F32), HD, 1)
            for h in range(2):
                own = first if h == 0 else jnp.logical_not(first)
                at = HD * (1 - h)
                side = jnp.where(lane == at, -hi, jnp.where(lane == at + 1, -lo, 0.0))
                lefts[i, h] = jnp.where(own, sf, side).astype(BF)
        ds = {}
        for i, h in both:
            ds[i, h] = (p[i, h] * dot_nt(lefts[i, h], vl[i][h])).astype(BF)
        dq = {t: dot_nn(ds[t], kl[t[0]]) for t in both}
        turned = [(jnp.transpose(a.astype(F32)).astype(BF), jnp.transpose(b.astype(F32)).astype(BF)) for a, b in zip(plain, scaled)]
        dk = {(i, h): dot_nn(turned[i][0][HD * h : HD * h + HD], ds[i, h]) for i, h in both}
        dvs = {(i, h): dot_nn(turned[i][1][HD * h : HD * h + HD], pb[i, h]) for i, h in both}
        for i, (q_rows, k_rows) in enumerate(items):
            att_o[q_rows, :] = outs[i]
            dqk[q_rows, :128] = jnp.where(first, dq[i, 0], dq[i, 1])
            new_k = jnp.transpose(jnp.concatenate([dk[i, 0], dk[i, 1]], axis=0))
            new_v = jnp.transpose(jnp.concatenate([dvs[i, 0], dvs[i, 1]], axis=0))
            if add:
                dqk[k_rows, 128:] += new_k
                dv[k_rows, :] += new_v
            else:
                dqk[k_rows, 128:] = new_k
                dv[k_rows, :] = new_v

    count_a, count_b = info[SMALL_A], info[SMALL_B]

    def small_rows(i):
        row_a = BIG * info[LARGE_A] + BLK * i
        row_b = info[BASE] + BIG * info[LARGE_B] + BLK * (i - count_a)
        row = jnp.where(i < count_a, row_a, jnp.where(i < count_a + count_b, row_b, ROWS))
        return pl.ds(pl.multiple_of(row, 16), BLK)

    def smalls(i, carry):
        rows = [small_rows(2 * i + n) for n in range(2)]
        blocks([(r, r) for r in rows], True, False)
        return carry

    lax.fori_loop(0, (count_a + count_b + 1) // 2, smalls, 0)

    def large_block(i, carry):
        base = jnp.where(i < 2 * info[LARGE_A], 0, info[BASE])
        k_rows = pl.ds(pl.multiple_of(base, 16), BIG)
        blocks([(pl.ds(pl.multiple_of(base + (i & 1) * 512, 16), 512), k_rows)], False, True)
        return carry

    lax.fori_loop(0, 2 * (info[LARGE_A] + info[LARGE_B]), large_block, 0)

    dw[...] = jnp.zeros_like(dw)
    dwo[...] = jnp.zeros_like(dwo)

    def pull(i):
        rows = pl.ds(pl.multiple_of(i * 2 * RB, 2 * RB), 2 * RB)
        g_out = dqk[rows, :]
        x = xh[rows, :]
        dg_o[...] += 0.125 * jnp.sum(g_out * x, axis=0, keepdims=True)
        g = g_out * (0.125 * gain[...])
        g = rr[rows, :] * (g - mean(g) - x * mean(g * x))
        dqkv_o[rows, :] = jnp.concatenate([g.astype(BF), dv[rows, :].astype(BF)], axis=1)

    def weigh(i):
        rows = pl.ds(pl.multiple_of(i * 2 * RB, 2 * RB), 2 * RB)
        dw[...] += dot_tn(dqkv_o[rows, :], nrm[rows, :])
        dwo[...] += dot_tn(att_o[rows, :], cot[rows, :])

    def finish(i, carry):
        weigh(i - 1)
        pull(i)
        return carry

    pull(0)
    lax.fori_loop(1, (nb + 1) // 2, finish, 0)
    weigh((nb + 1) // 2 - 1)
    if not last:
        dwo_o[...] = dwo[...].astype(BF)
        dw_o[...] = dw[...].astype(BF)
        return
    dwo_o[pl.ds(pl.multiple_of(128 + 128 * step, 16), 128), :] = dwo[...].astype(BF)

    @pl.when(step == 0)
    def _():
        dws[...] = dw[...]
        dwo_o[0:128, :] = dwo_0[...]

    @pl.when(step == len(pairs) - 1)
    def _():
        dwo_send[...] = jnp.where(place[CORE] == 0, dwo_o[240:384, :], dwo_o[96:240, :])
        full = [jnp.transpose(d).astype(BF) for d in (dw_0[...].astype(F32), dws[...], dw[...])]
        for f in range(8):

            def fill(ref, f=f):
                for q in range(3):
                    for n in range(3):
                        at = 288 * q + 96 * n
                        ref[at : at + 96, :] = full[q][96 * f : 96 * f + 96, 128 * n : 128 * n + 128]

            put(place, near_o, far_o, f, fill)


def attention(info, place, nrm, cot, near, far, wo_a, wo_b, gain, pairs, before=(), after=()):
    sds = jax.ShapeDtypeStruct
    bs = pl.BlockSpec
    n, more = len(pairs), ROWS + 256
    outs = [sds((n, more, 128), BF), sds((n, ROWS, 384), BF), sds((n, D, 384), BF), sds((n, 128, D), BF), sds((1, 256), F32)]
    by_pair = lambda p: (p, 0, 0)
    fixed = lambda a: bs(a.shape, lambda p: (0,) * len(a.shape))
    specs = [bs((None, *o.shape[1:]), by_pair) for o in outs[:4]] + [fixed(outs[4])]
    if n > 1:
        rest = [sds((384, D), BF), sds((144, D), BF), sds((4, 864, 128), BF), sds((4, 864, 128), BF)]
    else:
        rest = [sds((128, D), BF), sds((384, D), BF)]
    outs, specs = outs + rest, specs + [fixed(o) for o in rest]
    v = pltpu.VMEM
    scratch = [v((ROWS, D), BF)] * 2 + [pltpu.SemaphoreType.DMA((2, NRB))] + [v((2, more, 128), BF)] + [
        v((more, 128), BF)] * 3 + [v((ROWS, 256), F32)] * 2 + [v((more, 256), F32), v((more, 128), F32), v((384, D), F32), v((128, D), F32), v((384, D), F32)]
    hbm = bs(memory_space=pl.ANY)
    given = (near, far, wo_a, wo_b, gain, *before)
    return call(functools.partial(attention_body, pairs=pairs), tuple(outs), scratch, (info, place, nrm, cot, *given),
                [SCALARS] * 2 + [hbm] * 2 + [fixed(g) for g in given], tuple(specs), grid=(n,),
                cost=(n * 12 * 10**9, n * 14 * 10**6), after=after, tick=True, vmem=60)


def mlp_body(info, place, nrm_h, cot_h, near_a, near_b, far_a, far_b, mb, dwo, came, *refs, chunk):
    refs = list(refs)
    last = chunk == 2
    if last:
        gob, dg, db_0, db_1 = refs[:4]
        refs = refs[4:]
    act_h, gm_h, win_h, wout_h, near_o, far_o, db = refs[:7]
    nrm, cot, act, gm, win, wout, dwin, dwout, held, sems, out_sems, piece_sems, weight_sems = refs[7:]
    nb = info[NB]

    def incoming(i):
        rows = pl.ds(pl.multiple_of(i * RB, RB), RB)
        return (pltpu.make_async_copy(nrm_h.at[rows, :], nrm.at[rows, :], sems.at[0, i]),
                pltpu.make_async_copy(cot_h.at[rows, :], cot.at[rows, :], sems.at[1, i]))

    def outgoing(i):
        rows = pl.ds(pl.multiple_of(i * RB, RB), RB)
        return (pltpu.make_async_copy(act.at[rows, :], act_h.at[rows, :], out_sems.at[0, i]),
                pltpu.make_async_copy(gm.at[rows, :], gm_h.at[rows, :], out_sems.at[1, i]))

    def over(body):
        def step(i, carry):
            body(i)
            return carry

        lax.fori_loop(0, nb, step, 0)

    pieces = [pltpu.make_async_copy(p.at[:, chunk], held.at[pl.ds(2 * n, 2)], piece_sems.at[n])
              for n, p in enumerate((near_a, near_b, far_a, far_b))]
    weights = [pltpu.make_async_copy(win, win_h, weight_sems.at[0]), pltpu.make_async_copy(wout, wout_h, weight_sems.at[1])]
    for move in pieces:
        move.start()
    over(lambda i: [move.start() for move in incoming(i)])
    dwin[...] = jnp.zeros_like(dwin)
    dwout[...] = jnp.zeros_like(dwout)
    db[...] = jnp.zeros_like(db)
    for move in pieces:
        move.wait()
    for f in range(8):
        side, at = slot_of(place, f)
        piece = held[4 * side + at]
        for n in range(2):
            win[96 * f : 96 * f + 96, 256 * n : 256 * n + 256] = piece[96 * n : 96 * n + 96]
        for t in range(3):
            part = piece[192 + 80 * t : 272 + 80 * t]
            lanes = slice(256 * t, 256 * t + 256)
            if f == 1:
                wout[0:32, lanes] = part[48:]
            elif f > 1:
                wout[80 * f - 128 : 80 * f - 48, lanes] = part
    for move in weights:
        move.start()

    c0 = 0.7978845608028654
    c1 = 0.044715 * c0

    def step(i, carry):
        rows = pl.ds(pl.multiple_of(i * RB, RB), RB)
        for move in incoming(i):
            move.wait()
        pre = dot_nn(nrm[rows, :], win[...]) + mb[chunk : chunk + 1, :]
        ga = dot_nt(cot[rows, :], wout[...])
        sq = pre * pre
        t = jnp.tanh(pre * (c0 + c1 * sq))
        up = 0.5 + 0.5 * t
        done = pre * up
        act[rows, :] = done.astype(BF)
        gmf = ga * (up + done * (1.0 - up) * (2.0 * c0 + 6.0 * c1 * sq))
        gm[rows, :] = gmf.astype(BF)
        db[...] += jnp.sum(gmf, axis=0, keepdims=True)
        dwout[...] += dot_tn(act[rows, :], cot[rows, :])
        dwin[...] += dot_tn(gm[rows, :], nrm[rows, :])
        for move in outgoing(i):
            move.start()
        return carry

    lax.fori_loop(0, nb, step, 0)
    full = jnp.transpose(dwin[...]).astype(BF)
    core = place[CORE] == 0
    first, second = slice(80 * chunk, 80 * chunk + 80), slice(48 * chunk, 48 * chunk + 48)
    both = jnp.concatenate([came[...], dwo[0:96, :]])
    zero_rows = jnp.where(core, dwo[first, :], both[first])
    one_rows = jnp.where(core, came[second, :], dwo[240 + 48 * chunk : 288 + 48 * chunk, :])
    if last:
        ob = gob[...]
        qs = dg[:, :HD] + dg[:, HD : 2 * HD]
        ks = dg[:, 2 * HD : 3 * HD] + dg[:, 3 * HD :]
        parts = {}
        for j, units in enumerate((db_0[...], db_1[...], db[...])):
            for cc in range(2):
                own = jnp.where(place[CORE] == cc, units, 0.0)
                done = 0
                for u, n in unit_ranges(cc, j):
                    parts[u] = own[:, done : done + n]
                    done += n
        hidden = jnp.concatenate([parts[u] for u in sorted(parts)], axis=1)
    for f in range(8):

        def fill(ref, f=f):
            for n in range(2):
                ref[96 * n : 96 * n + 96, :] = full[96 * f : 96 * f + 96, 256 * n : 256 * n + 256]
            for t in range(3):
                lanes = slice(256 * t, 256 * t + 256)
                at = 192 + 80 * t
                if f == 0:
                    ref[at : at + 80, :] = zero_rows[:, lanes]
                elif f == 1:
                    ref[at : at + 48, :] = one_rows[:, lanes]
                    ref[at + 48 : at + 80, :] = dwout[0:32, lanes].astype(BF)
                else:
                    ref[at : at + 80, :] = dwout[80 * f - 128 : 80 * f - 48, lanes].astype(BF)
            if last:
                blank = lambda n: jnp.zeros((1, n), F32)
                rows = [hidden[:, 384 * f : 384 * f + 256],
                        jnp.concatenate([hidden[:, 384 * f + 256 : 384 * f + 384], ob[:, 96 * f : 96 * f + 96], blank(32)], axis=1),
                        jnp.concatenate([qs[:, 8 * f : 8 * f + 8], blank(120), ks[:, 8 * f : 8 * f + 8], blank(120)], axis=1)]
                ref[432:448, :] = jnp.concatenate([*rows, jnp.zeros((13, 256), F32)]).astype(BF)

        put(place, near_o, far_o, f, fill)
    for move in weights:
        move.wait()
    over(lambda i: [move.wait() for move in outgoing(i)])


def clamp(i, info, *_):
    return (jnp.minimum(i, info[NB] - 1), 0)


def whole(i, *_):
    return (0, 0)


def whole3(i, *_):
    return (0, 0, 0)


def mlp(info, place, nrm, cot, pieces, mb, dwo, came, vectors, chunk, after=()):
    sds = jax.ShapeDtypeStruct
    rows = 448 if chunk == 2 else 432
    outs = (sds((ROWS, U), BF), sds((ROWS, U), BF), sds((D, U), BF), sds((U, D), BF), sds((4, rows, 256), BF),
            sds((4, rows, 256), BF), sds((1, U), F32))
    hbm = pl.BlockSpec(memory_space=pl.ANY)
    v = pltpu.VMEM
    dma = pltpu.SemaphoreType.DMA
    scratch = [v((ROWS, D), BF)] * 2 + [v((ROWS, U), BF)] * 2 + [v((D, U), BF), v((U, D), BF), v((U, D), F32), v((U, D), F32),
               v((8, 432, 256), BF), dma((2, NRB)), dma((2, NRB)), dma((4,)), dma((2,))]
    given = (mb, dwo, came, *vectors)
    return call(functools.partial(mlp_body, chunk=chunk), outs, scratch, (info, place, nrm, cot, *pieces, *given),
                [SCALARS] * 2 + [hbm] * 6 + [ANYWHERE] * len(given), (hbm,) * 4 + (ANYWHERE,) * 3, vmem=60,
                cost=(10 * 10**9, 18 * 10**6), after=after, tick=True)


def sums_body(info, *refs, n, transposed):
    i = pl.program_id(0)
    lefts, rights, own, other, left, right, held, sems = refs[:n], refs[n : 2 * n], *refs[2 * n :]

    @pl.when(i == 0)
    def _():
        at = 0
        for b in rights:
            k = b.shape[1] if transposed else b.shape[0]
            if transposed:
                right[:, at : at + k] = b[...]
            else:
                right[at : at + k, :] = b[...]
            at += k

    @pl.when(i < info[NB])
    def _():
        at = 0
        for a in lefts:
            left[:, at : at + a.shape[1]] = a[...]
            at += a.shape[1]
        total = dot_nt(left[...], right[...]) if transposed else dot_nn(left[...], right[...])
        held[pl.ds(pl.multiple_of(i * RB, RB), RB), :] = total.astype(BF)

    @pl.when(i >= info[NB])
    def _():
        held[pl.ds(pl.multiple_of(i * RB, RB), RB), :] = jnp.zeros((RB, D), BF)

    move_own = pltpu.make_async_copy(held.at[pl.ds(0, CAN), :], own, sems.at[0])

    @pl.when(i == (CAN - 1) // RB)
    def _():
        move_own.start()

    @pl.when(i == pl.num_programs(0) - 1)
    def _():
        move_other = pltpu.make_async_copy(held.at[pl.ds(pl.multiple_of(info[BASE], 16), CAN), :], other, sems.at[1])
        move_other.start()
        move_own.wait()
        move_other.wait()


def sums(info, lefts, rights, transposed, after=()):
    n = len(lefts)
    bs = pl.BlockSpec
    sds = jax.ShapeDtypeStruct

    def rows_of(a, p):
        if p is None:
            return bs((RB, a.shape[1]), clamp)
        return bs((None, RB, a.shape[2]), lambda i, info: (p, jnp.minimum(i, info[NB] - 1), 0))

    def all_of(b, p):
        return bs(b.shape, whole) if p is None else bs((None, *b.shape[1:]), lambda i, info: (p, 0, 0))

    in_specs = [rows_of(*a) for a in lefts] + [all_of(*b) for b in rights]
    lefts, rights = [a for a, _ in lefts], [b for b, _ in rights]
    k = sum(a.shape[-1] for a in lefts)
    v = pltpu.VMEM
    scratch = [v((RB, k), BF), v((D, k) if transposed else (k, D), BF), v((ROWS, D), BF), pltpu.SemaphoreType.DMA((2,))]
    hbm = bs(memory_space=pl.ANY)
    return call(functools.partial(sums_body, n=n, transposed=transposed), (sds((CAN, D), BF),) * 2, scratch,
                (info, *lefts, *rights), in_specs, (hbm,) * 2, grid=(NRB,), prefetch=1,
                vmem=60, cost=(2 * 2304 * k * D, 2 * 2304 * (k + D)), after=after, tick=True)


def adds_body(*refs, counts, kinds):
    given = list(refs[: sum(counts)])
    outs = list(refs[sum(counts) :])
    for count, kind in zip(counts, kinds):
        terms = [given.pop(0) for _ in range(count)]
        if kind == "four":
            total = terms[0][...].astype(F32) + terms[1][...].astype(F32)
            for i in range(4):
                outs.pop(0)[...] = total[i : i + 1].astype(BF)
        else:
            total = terms[0][...].astype(F32)
            for t in terms[1:]:
                total = total + t[...].astype(F32)
            out = outs.pop(0)
            out[...] = total.astype(out.dtype)


def adds(items, after, vmem=VMEM_MIB):
    sds = jax.ShapeDtypeStruct
    outs = []
    for terms, kind in items:
        a = terms[0]
        shape = (1, *a.shape[1:]) if kind == "four" else a.shape
        outs += [sds(shape, F32 if kind == "float" else BF)] * (4 if kind == "four" else 1)
    args = [t for terms, _ in items for t in terms]
    body = functools.partial(adds_body, counts=[len(t) for t, _ in items], kinds=[k for _, k in items])
    *done, tick = call(body, tuple(outs), [], args, [ANYWHERE] * len(args), cost=(0, 3 * 10**6), after=after, tick=True, vmem=vmem)
    results = []
    for _, kind in items:
        results.append([done.pop(0) for _ in range(4)] if kind == "four" else done.pop(0))
    return *results, tick


def final_body(place, w_in, ln, *refs):
    own, other, parts = refs[:3], refs[3:6], refs[6:10]
    gin, gout, gln, gqs, gks, gmb, gob = refs[10:]
    mine, along_x, mate, across = (p[0].astype(F32) for p in parts)
    last_own, last_other = mine + along_x, mate + across
    c, f = place[CORE], place[FSDP]
    for cc in range(2):
        sources = [jnp.where(c == cc, a[0], b[0]) for a, b in zip(own, other)] + [jnp.where(c == cc, last_own, last_other)]
        for p in range(3):
            for n in range(3):
                at = D * n + 384 * cc + 128 * p
                gin[:, at : at + 128] = sources[0][288 * p + 96 * n : 288 * p + 96 * n + 96, :]
        for j in range(3):
            s = sources[1 + j]
            m = jnp.concatenate([s[0:96], s[96:192]], axis=1)
            done = 0
            for u, n in unit_ranges(cc, j):
                gin[:, 3 * D + u : 3 * D + u + n] = m[:, done : done + n]
                done += n
            for t in range(3):
                lanes = slice(256 * t, 256 * t + 256)
                part = s[192 + 80 * t : 272 + 80 * t]

                @pl.when(f != 1)
                def _():
                    gout[240 * cc + 80 * j : 240 * cc + 80 * j + 80, lanes] = part

                @pl.when(f == 1)
                def _():
                    a, b = 144 * cc + 48 * j, 288 + 96 * cc + 32 * j
                    gout[a : a + 48, lanes] = part[:48]
                    gout[b : b + 32, lanes] = part[48:]
    total = jnp.sum(w_in[...].astype(F32) * gin[...], axis=1, keepdims=True)
    gln[...] = jnp.transpose(jnp.broadcast_to(total, (96, 128)))[0:1, :] / ln[...]
    vec = last_own[432:440, :] + last_other[432:440, :]
    gmb[...] = jnp.concatenate([vec[0:1, :], vec[1:2, :128]], axis=1)
    gob[...] = vec[1:2, 128:224]
    gqs[...] = vec[2:3, 0:8]
    gks[...] = vec[2:3, 128:136]


def final(place, w_in, ln, own, other, parts, after=()):
    sds = jax.ShapeDtypeStruct
    outs = (sds((96, 7 * D), F32), sds((480, D), F32), sds((1, 96), F32), sds((1, 8), F32), sds((1, 8), F32),
            sds((1, 384), F32), sds((1, 96), F32))
    return call(final_body, outs, [], (place, w_in, ln, *own, *other, *parts), [SCALARS] + [ANYWHERE] * 12, cost=(0, 10**7), after=after)


def routes():
    places = [(x, c, z, y) for x in range(2) for c in range(2) for z in range(4) for y in range(2)]
    number = lambda x, c, z, y: (x * 2 + c) * 8 + z * 2 + y
    pairs = lambda move: [(number(*p), number(*move(*p))) for p in places]
    out = {
        "core": pairs(lambda x, c, z, y: (x, 1 - c, z, y)),
        "x": pairs(lambda x, c, z, y: (1 - x, c, z, y)),
        "x_core": pairs(lambda x, c, z, y: (1 - x, 1 - c, z, y)),
        "y": pairs(lambda x, c, z, y: (x, c, z, 1 - y)),
        "z1": pairs(lambda x, c, z, y: (x, c, z ^ 1, y)),
        "z2": pairs(lambda x, c, z, y: (x, c, z ^ 2, y)),
        "z3": pairs(lambda x, c, z, y: (x, c, z ^ 3, y)),
    }
    at = lambda n: (n % 8) // 2
    out["z2_up"] = [(a, b) for a, b in out["z2"] if at(a) == 0]
    out["z1_up"] = [(a, b) for a, b in out["z1"] if at(a) % 2 == 0]
    return out


def per_device_paired(
    tokens, lengths, assign, w_in, w_out, ln_scale, q_scale, k_scale, mlp_bias, out_bias, cotangent
):
    way = routes()
    go = lambda v, name: lax.ppermute(v, ("rep", "fsdp"), way[name])
    rep, f = lax.axis_index("rep"), lax.axis_index("fsdp")
    c, y, z = rep % 2, f % 2, f // 2
    cap = tokens.shape[0]
    device = rep * 8 + f
    place = jnp.stack([c, f, y, z, device, device + 8 - 16 * c, rep // 2]).astype(jnp.int32)

    late = lambda v, tick: v if tick is None else v + tick[0].astype(v.dtype)
    first = lambda piece, tick=None: jnp.stack([piece, late(go(piece, "z2"), tick)])
    second = lambda two, tick=None: jnp.concatenate([two, late(go(two, "z1"), tick)])
    third = lambda four: (four, go(four, "y"))
    vectors = (v.reshape(1, -1) for v in (ln_scale, q_scale, k_scale, mlp_bias, out_bias))
    a, wo, tick = pieces_of(place, w_in, w_out)
    a_b, wo_b = go(a, "z2"), go(wo, "z2_up")
    info, vectors = plan(place, lengths, assign, *vectors, after=(tick,))
    vectors = third(second(first(vectors)))
    wo = jnp.where(z == 0, wo, wo_b)
    near = jnp.concatenate([a[:288], a_b[:288], wo])
    b = jnp.concatenate([a[288:], a_b[288:]]).reshape(2, 576, 128)
    own, gob, tick = prepare(info, tokens, cotangent, (near, b, *vectors))
    far = late(go(near, "z1"), tick)
    m, own = split(place, w_in, w_out, own, (far,))
    wo = jnp.where(z % 2 == 0, wo, far[576:])
    near = jnp.concatenate([near[:576], far[:576], wo])
    far = go(near, "y")
    other = go(own, "core")
    b_b = go(b, "z1")
    m_b = go(m, "z2")
    cross = jnp.concatenate([wo, far[PARTS:]])
    nrm, cot, ln, ob, gain, mb, tick = combine(info, place, own, other, *vectors, after=(cross,))
    b = jnp.concatenate([b, late(b_b, tick)])
    wo_a, wo_b, tick = head_rows(place, near, far, go(cross, "x"), (b,))
    wo_b = go(wo_b, "core")
    m = jnp.stack([m, late(m_b, tick)])

    def heads(pairs, g, before, after):
        return attention(info, place, nrm, cot, *g, wo_a, wo_b, gain, pairs, before, after)

    att_0, dqkv_0, w_0, wo_0, dg, dwo, dw, tick = heads((0,), (near, far), (), (b, m))
    m_b = go(m, "z1")
    att_1, dqkv_1, w_1, wo_1, dg, dwo, send, *g_h, tick = heads((1, 2), (b, go(b, "y")), (dw, dwo, dg), (m_b,))
    pieces = (m, m_b, go(m, "y"), go(m_b, "y"))
    came = go(send, "core")
    att, dqkv, ws, wos = (((p, 0), (q, 0), (q, 1)) for p, q in ((att_0, att_1), (dqkv_0, dqkv_1), (w_0, w_1), (wo_0, wo_1)))

    def hidden(j, vectors, after):
        return mlp(info, place, nrm, cot, pieces, mb, dwo, came, vectors, j, after)

    step_y = lambda g: ((g[0], go(g[1], "y")), "four")
    step_z = lambda g: ((g[0], go(g[2], "z1"), go(g[1], "z2"), go(g[3], "z3")), "whole")
    step_x = lambda g: ((g, go(g, "x")), "float")

    *h0, tick = hidden(0, (), (tick,))
    g_h, tick = adds([step_y(g_h)], (tick,), 60)
    *h1, tick = hidden(1, (), (tick,))
    g_h, g_0, tick = adds([step_z(g_h), step_y(h0[4:6])], (tick,))
    *h2, tick = hidden(2, (gob, dg, h0[6], h1[6]), (tick,))
    act, gm, wins, wouts, _, _, _ = zip(h0, h1, h2)
    plain = lambda arrays: tuple((v, None) for v in arrays)

    g_h, g_0, g_1, tick = adds([step_x(g_h), step_z(g_0), step_y(h1[4:6])], (tick,))
    part, away, tick = sums(info, (*att, *plain(act)), (*wos, *plain(wouts)), False, (tick,))
    away = go(away, "core")
    g_0, g_1, g_2, tick = adds([step_x(g_0), step_z(g_1), step_y(h2[4:6])], (tick,))
    part_b, away_b, tick = sums(info, (*dqkv, *plain(gm)), (*ws, *plain(wins)), True, (tick,))
    away_b = go(away_b, "core")
    g_1, g_2, tick = adds([step_x(g_1), step_z(g_2)], (tick,))
    output, tick = last_rows(info, own, part, away, ob, cap, False, (tick,))
    grads = (g_h, g_0, g_1)
    others = [go(g, "core") for g in grads]
    parts = (g_2, *(go(g_2, name) for name in ("x", "core", "x_core")))
    grad_tokens, tick = last_rows(info, own, part_b, away_b, ln, cap, True, (tick,))
    g_win, g_wout, *small = final(place, w_in, ln_scale.astype(F32).reshape(1, 96), grads, others, parts, (tick,))
    return (output, grad_tokens, g_win, g_wout, *(g.reshape(-1) for g in small))


HEADS = 12
epsilon = 1e-06


def layer_norm(values, weight_gain):
    center = values - jnp.mean(values, axis=-1, keepdims=True)
    spread = jnp.mean(center * center, axis=-1, keepdims=True)
    return center * lax.rsqrt(spread + epsilon) * weight_gain


def layout(lengths, assign, device, row_count):
    own = assign == device
    own_sizes = jnp.where(own, lengths, 0)
    own_ends = jnp.cumsum(own_sizes)
    own_starts = own_ends - own_sizes
    position = lax.broadcasted_iota(jnp.int32, (row_count, lengths.shape[0]), 0)
    number = lax.broadcasted_iota(jnp.int32, (row_count, lengths.shape[0]), 1)
    inside = (position >= own_starts[None, :]) & (position < own_ends[None, :])
    filled = jnp.any(inside, axis=1)
    segment = jnp.sum(jnp.where(inside, number, 0), axis=1)
    return (jnp.where(filled, segment, -1), filled)


def contract_rows(left, right):
    return lax.dot_general(
        left, right, (((0,), (0,)), ((), ())), preferred_element_type=jnp.float32
    )


def contract_cols(left, right):
    return lax.dot_general(
        left, right, (((1,), (1,)), ((), ())), preferred_element_type=jnp.float32
    )


def per_device(
    tokens, lengths, assign, w_in, w_out, ln_scale, q_scale, k_scale, mlp_bias, out_bias, cotangent
):
    row_count = tokens.shape[0]
    head_dim = HD
    head_count = HEADS
    width = head_dim * head_count
    factor = head_dim ** (-0.5)
    device = lax.axis_index("rep") * lax.axis_size("fsdp") + lax.axis_index("fsdp")
    segment, filled = layout(lengths, assign, device, row_count)
    allowed = segment[:, None] == segment[None, :]
    params = (w_in, w_out, ln_scale, q_scale, k_scale, mlp_bias, out_bias)
    full = (
        lax.all_gather(params[0], "fsdp", axis=0, tiled=True),
        lax.all_gather(params[1], "fsdp", axis=0, tiled=True),
        lax.all_gather(params[2], "fsdp", axis=0, tiled=True),
        lax.all_gather(params[3], "fsdp", axis=0, tiled=True),
        lax.all_gather(params[4], "fsdp", axis=0, tiled=True),
        lax.all_gather(params[5], "fsdp", axis=0, tiled=True),
        lax.all_gather(params[6], "fsdp", axis=0, tiled=True),
    )
    win_full, wout_full = (full[0], full[1])
    small = [arr.astype(jnp.float32) for arr in full[2:]]
    ln_full, qs_full, ks_full, mb_full, ob_full = small
    inputs = tokens.astype(jnp.float32)
    normed_f, ln_pull = jax.vjp(layer_norm, inputs, ln_full)
    normed = normed_f.astype(jnp.bfloat16)
    joined = jnp.dot(normed, win_full, preferred_element_type=jnp.float32)
    q_pre = joined[:, :width].reshape(row_count, head_count, head_dim)
    k_pre = joined[:, width : 2 * width].reshape(row_count, head_count, head_dim)
    values = joined[:, 2 * width : 3 * width].astype(jnp.bfloat16)
    hidden_pre = joined[:, 3 * width :]
    q_norm, q_pull = jax.vjp(layer_norm, q_pre, qs_full)
    k_norm, k_pull = jax.vjp(layer_norm, k_pre, ks_full)
    queries = q_norm.reshape(row_count, width).astype(jnp.bfloat16)
    keys_all = k_norm.reshape(row_count, width).astype(jnp.bfloat16)

    def head_slice(array, head_index):
        return lax.dynamic_slice_in_dim(array, head_index * head_dim, head_dim, 1)

    def head_scores(head_index):
        raw = (
            contract_cols(head_slice(queries, head_index), head_slice(keys_all, head_index))
            * factor
        )
        return jnp.where(allowed, raw, -1e30)

    def head_forward(head_index):
        scores = head_scores(head_index)
        top = jnp.max(scores, axis=1, keepdims=True)
        expon = jnp.exp(scores - top)
        total = jnp.sum(expon, axis=1, keepdims=True)
        probs = (expon / total).astype(jnp.bfloat16)
        head_out = jnp.dot(
            probs, head_slice(values, head_index), preferred_element_type=jnp.float32
        )
        return (head_out, (top + jnp.log(total))[:, 0])

    head_outs, log_totals = lax.map(head_forward, jnp.arange(head_count))
    attended = jnp.transpose(head_outs, (1, 0, 2)).reshape(row_count, width)
    activated, gelu_pull = jax.vjp(lambda pre, bias: jax.nn.gelu(pre + bias), hidden_pre, mb_full)
    merged = jnp.concatenate([attended, activated], axis=1).astype(jnp.bfloat16)
    result = jnp.dot(merged, wout_full, preferred_element_type=jnp.float32) + ob_full
    output = jnp.where(filled[:, None], inputs + result, 0.0).astype(jnp.bfloat16)
    back = (
        lax.all_gather(params[0], "fsdp", axis=0, tiled=True),
        lax.all_gather(params[1], "fsdp", axis=0, tiled=True),
        lax.all_gather(params[2], "fsdp", axis=0, tiled=True),
        lax.all_gather(params[3], "fsdp", axis=0, tiled=True),
        lax.all_gather(params[4], "fsdp", axis=0, tiled=True),
        lax.all_gather(params[5], "fsdp", axis=0, tiled=True),
        lax.all_gather(params[6], "fsdp", axis=0, tiled=True),
    )
    win_back, wout_back = (back[0], back[1])
    grad_rows = jnp.where(filled[:, None], cotangent.astype(jnp.float32), 0.0)
    grad_low = grad_rows.astype(jnp.bfloat16)
    grad_ob = jnp.sum(grad_rows, axis=0)
    grad_wout = contract_rows(merged, grad_low)
    grad_merged = contract_cols(grad_low, wout_back)
    grad_attended = grad_merged[:, :width].astype(jnp.bfloat16)
    grad_m, grad_mb = gelu_pull(grad_merged[:, width:])

    def head_backward(head_index):
        scores = head_scores(head_index)
        probs_full = jnp.exp(scores - log_totals[head_index][:, None])
        probs = probs_full.astype(jnp.bfloat16)
        grad_head = head_slice(grad_attended, head_index)
        grad_probs = contract_cols(grad_head, head_slice(values, head_index))
        inner = jnp.sum(probs_full * grad_probs, axis=1, keepdims=True)
        grad_scores = (probs_full * (grad_probs - inner)).astype(jnp.bfloat16)
        grad_q = (
            jnp.dot(
                grad_scores, head_slice(keys_all, head_index), preferred_element_type=jnp.float32
            )
            * factor
        )
        grad_k = contract_rows(grad_scores, head_slice(queries, head_index)) * factor
        grad_v = contract_rows(probs, grad_head)
        return (grad_q, grad_k, grad_v)

    grad_qh, grad_kh, grad_vh = lax.map(head_backward, jnp.arange(head_count))
    grad_qn = jnp.transpose(grad_qh, (1, 0, 2))
    grad_kn = jnp.transpose(grad_kh, (1, 0, 2))
    grad_values = jnp.transpose(grad_vh, (1, 0, 2)).reshape(row_count, width)
    grad_q_pre, grad_qs = q_pull(grad_qn)
    grad_k_pre, grad_ks = k_pull(grad_kn)
    grad_joined = jnp.concatenate(
        [
            grad_q_pre.reshape(row_count, width),
            grad_k_pre.reshape(row_count, width),
            grad_values,
            grad_m,
        ],
        axis=1,
    ).astype(jnp.bfloat16)
    grad_win = contract_rows(normed, grad_joined)
    grad_normed = contract_cols(grad_joined, win_back)
    grad_x_norm, grad_ln = ln_pull(grad_normed)
    grad_tokens = (grad_rows + grad_x_norm).astype(jnp.bfloat16)
    grads = (grad_win, grad_wout, grad_ln, grad_qs, grad_ks, grad_mb, grad_ob)
    shares = (
        lax.psum_scatter(grads[0], "fsdp", scatter_dimension=0, tiled=True),
        lax.psum_scatter(grads[1], "fsdp", scatter_dimension=0, tiled=True),
        lax.psum_scatter(grads[2], "fsdp", scatter_dimension=0, tiled=True),
        lax.psum_scatter(grads[3], "fsdp", scatter_dimension=0, tiled=True),
        lax.psum_scatter(grads[4], "fsdp", scatter_dimension=0, tiled=True),
        lax.psum_scatter(grads[5], "fsdp", scatter_dimension=0, tiled=True),
        lax.psum_scatter(grads[6], "fsdp", scatter_dimension=0, tiled=True),
    )
    shares = lax.psum(
        (shares[0], shares[1], shares[2], shares[3], shares[4], shares[5], shares[6]), "rep"
    )
    return (
        output,
        grad_tokens,
        shares[0],
        shares[1],
        shares[2],
        shares[3],
        shares[4],
        shares[5],
        shares[6],
    )


def solution(mesh):
    in_specs = (
        P(("rep", "fsdp"), None),
        P(),
        P(),
        P("fsdp", None),
        P("fsdp", None),
        P("fsdp"),
        P("fsdp"),
        P("fsdp"),
        P("fsdp"),
        P("fsdp"),
        P(("rep", "fsdp"), None),
    )
    out_specs = (
        P(("rep", "fsdp"), None),
        P(("rep", "fsdp"), None),
        P("fsdp", None),
        P("fsdp", None),
        P("fsdp"),
        P("fsdp"),
        P("fsdp"),
        P("fsdp"),
        P("fsdp"),
    )
    paired = dict(mesh.shape) == {"rep": 4, "fsdp": 8}
    return jax.shard_map(
        per_device_paired if paired else per_device, mesh=mesh, in_specs=in_specs, out_specs=out_specs, check_vma=False
    )
```
